512 devices in a mesh: vec: 32 (over z_hi, y), space: 16 (over x, z_lo, core).
Axes of the slice: x: 4, y: 8, z: 8 (z_hi: 4, z_lo: 2; z = z_hi * 2 + z_lo), core: 2. Of those that a mesh axis runs over, the one named last changes fastest.
Arguments:
- perturbation: float32 [32, 6, 384, 512], P('vec', None, 'space'), may hold values from -40 to 40
- trajectory: bfloat16 [32, 3, 6, 384, 512], P('vec', None, None, 'space'), may hold values from -1.796875 to 1.796875
- step_order: int32 [32], replicated, may hold values from 0 to 31, each once
Outputs:
- ortho_vectors: float32 [32, 6, 384, 512], P('vec', None, 'space')
- upper_factor: float32 [32, 32], replicated
The draws below stay inside these ranges and needn't reach their ends.
Inputs may be any that keep to these rules, and one draw needn't show every extreme that they name: `step_order`: each number appears once.
All inputs are finite; a program needn't handle non-finite values.
Results may differ from the reference program's by a relative error of at most 0.0003.
Values may be sent and summed in bfloat16 or wider, within the bound.
No kernel may reach another device: no remote copies, remote signals or barrier semaphores. Data moves between devices by JAX's collectives and lax.ppermute only.
A program may use at most 64 MiB of HBM per device.

```python
import jax
import jax.numpy as jnp
from jax import lax

NY = 512
STEPS = 2
K = 32
NX = 384
TRAJ = 32


def draw_perturbation(key, part):
    noise = jnp.clip(jax.random.normal(jax.random.fold_in(key, 11), (K, 6, NX, NY), jnp.float32), -6.0, 6.0)
    return noise


def levels(own_key, shape, split, low, top_value):
    factor_of = 1.0
    for position, blocks in split:
        heights = jax.random.uniform(jax.random.fold_in(jax.random.fold_in(own_key, 6), position), (blocks,), jnp.float32, low / len(split), top_value / len(split))
        factor_of = factor_of * jnp.repeat(jnp.exp(heights), shape[position] // blocks).reshape((-1,) + (1,) * (len(shape) - 1 - position))
    return factor_of


def gaussian(stream_key, extent, width, bound, cuts=(), dtype=jnp.bfloat16):
    array = width * jax.random.normal(stream_key, extent, jnp.float32)
    if cuts:
        array = array * levels(stream_key, extent, cuts, -0.22, 0.18)
    return jnp.clip(array, -bound, bound).astype(dtype)


def setup_inputs(seed: int = 0) -> dict:
    streams_of = jax.random.split(jax.random.key(seed), 4)
    perturbation = draw_perturbation(jax.random.fold_in(streams_of[3], 71), 0)
    trajectory = gaussian(streams_of[1], (TRAJ, 3, 6, NX, NY), 0.3, 1.796875, ((0, 32), (3, 16)))
    step_order = jax.random.permutation(streams_of[2], TRAJ).astype(jnp.int32)
    return dict(perturbation=perturbation, trajectory=trajectory, step_order=step_order)


GRAVITY_TOP = 1.0
GRAVITY_LOW = 0.5
DEPTH_TOP = 1.0
DEPTH_LOW = 1.0
CORIOLIS = 0.3
TIME_STEP = 0.25

def diff_x(field):
    return 0.5 * (field[..., 2:, :] - field[..., :-2, :])

def diff_y(field):
    return 0.5 * (jnp.roll(field, -1, -1) - jnp.roll(field, 1, -1))

def trimmed(field, amount):
    return field[..., amount:field.shape[-2] - amount, :]

def tangent(base_state, tangent_state):
    dp_top = GRAVITY_TOP * (tangent_state[..., 0, :, :] + tangent_state[..., 3, :, :])
    dp_low = dp_top + GRAVITY_LOW * tangent_state[..., 3, :, :]
    results = []
    for layer_num, (mean_depth, pressure) in enumerate(((DEPTH_TOP, dp_top), (DEPTH_LOW, dp_low))):
        offset = 3 * layer_num
        base_depth = base_state[offset] + mean_depth
        base_xvel = base_state[offset + 1]
        base_yvel = base_state[offset + 2]
        pert_depth = tangent_state[..., offset, :, :]
        pert_xvel = tangent_state[..., offset + 1, :, :]
        pert_yvel = tangent_state[..., offset + 2, :, :]
        depth_rate = -diff_x(base_depth * pert_xvel + pert_depth * base_xvel) - trimmed(diff_y(base_depth * pert_yvel + pert_depth * base_yvel), 1)
        xvel_rate = -(trimmed(base_xvel, 1) * diff_x(pert_xvel) + trimmed(pert_xvel, 1) * diff_x(base_xvel)) - trimmed(base_yvel * diff_y(pert_xvel) + pert_yvel * diff_y(base_xvel), 1) + CORIOLIS * trimmed(pert_yvel, 1) - diff_x(pressure)
        yvel_rate = -(trimmed(base_xvel, 1) * diff_x(pert_yvel) + trimmed(pert_xvel, 1) * diff_x(base_yvel)) - trimmed(base_yvel * diff_y(pert_yvel) + pert_yvel * diff_y(base_yvel), 1) - CORIOLIS * trimmed(pert_xvel, 1) - trimmed(diff_y(pressure), 1)
        results += [depth_rate, xvel_rate, yvel_rate]
    return jnp.stack(results, axis=-3)

def combine(section_num, anchor, current, change):
    if section_num == 0:
        return current + TIME_STEP * change
    if section_num == 1:
        return 0.75 * anchor + 0.25 * (current + TIME_STEP * change)
    return anchor / 3.0 + 2.0 / 3.0 * (current + TIME_STEP * change)

def pad_rows(field):
    widths = [(0, 0)] * (field.ndim - 2) + [(1, 1), (0, 0)]
    return jnp.pad(field, widths, mode='wrap')

def reference(perturbation, trajectory, step_order):
    state = perturbation
    for step_num in range(STEPS):
        sections = trajectory[step_order[step_num]].astype(jnp.float32)
        padded_sections = pad_rows(sections)

        def advance(vector):
            current = vector
            for section_num in range(3):
                change = tangent(padded_sections[section_num], pad_rows(current))
                current = combine(section_num, vector, current, change)
            return current
        state = lax.map(advance, state)
    entries = 6 * state.shape[2] * state.shape[3]
    flat_cells = state.reshape(state.shape[0], -1)
    gram_matrix = jnp.dot(flat_cells.astype(jnp.float32), flat_cells.T.astype(jnp.float32), precision=lax.Precision.HIGHEST, preferred_element_type=jnp.float32) / entries
    lower_factor = jnp.linalg.cholesky(gram_matrix)
    ortho = jax.scipy.linalg.solve_triangular(lower_factor, flat_cells, lower=True)
    return (ortho.reshape(state.shape), jnp.transpose(lower_factor))
```

```python
import jax
import jax.numpy as jnp
from jax import lax
from jax.experimental import pallas as pl
from jax.experimental.pallas import tpu as pltpu
from jax.sharding import PartitionSpec as P

GRAVITY_TOP = 1.0
GRAVITY_LOW = 0.5
DEPTH = 1.0
CORIOLIS = 0.3
TIME_STEP = 0.25

ROWS = 24
HALO = 6
PAD = ROWS + 2 * HALO
PERT_TILES = 9
BASE_TILES = 14
TILES = PERT_TILES + BASE_TILES
STEP_ROWS = tuple(HALO - section for section in range(6))
BASE_HALO_ROWS = 6 * sum(STEP_ROWS)
STATE_HALO_ROWS = 6 * HALO * 8
HALO_ROWS = STATE_HALO_ROWS + BASE_HALO_ROWS + 2
COEF = 14
LIMIT = pltpu.CompilerParams(vmem_limit_bytes=40 * 1024 * 1024)


def roll_lanes(value, shift):
    shift %= value.shape[-1]
    return pltpu.roll(value, shift, 1) if shift else value


def roll_rows(value, shift):
    shift %= value.shape[0]
    return pltpu.roll(value, shift, 0) if shift else value


def lane_group(shape, size):
    return lax.broadcasted_iota(jnp.int32, shape, 1) // size


def quad_transpose(items, group):
    odd = (group % 2) == 1
    upper = group >= 2
    a, b, c, d = items
    a, b = jnp.where(odd, roll_lanes(b, 32), a), jnp.where(odd, b, roll_lanes(a, -32))
    c, d = jnp.where(odd, roll_lanes(d, 32), c), jnp.where(odd, d, roll_lanes(c, -32))
    a, c = jnp.where(upper, roll_lanes(c, 64), a), jnp.where(upper, c, roll_lanes(a, 64))
    b, d = jnp.where(upper, roll_lanes(d, 64), b), jnp.where(upper, d, roll_lanes(b, 64))
    return a, b, c, d


def pack_kernel(pert_ref, traj_ref, out_ref):
    group = lane_group((8, 128), 32)
    for parity in range(2):
        shift = 8 if parity == 0 else -8
        units = []
        for field in range(6):
            value = roll_lanes(pert_ref[field], shift)
            high = value.astype(jnp.bfloat16).astype(jnp.float32)
            low = value - high
            for tile in range(3):
                rows = slice(8 * tile, 8 * tile + 8)
                units += [high[rows], low[rows]]
        base = []
        for field in range(18):
            base.append(roll_lanes(traj_ref[field].astype(jnp.float32), shift))
        for tile in range(3):
            for field in range(18):
                units.append(base[field][8 * tile : 8 * tile + 8])
        while len(units) < 4 * TILES:
            units.append(jnp.zeros((8, 512), jnp.float32))
        for part in range(4):
            columns = slice(128 * part, 128 * part + 128)
            blocks = [[], [], [], []]
            for quad in range(TILES):
                four = [units[4 * quad + i][:, columns] for i in range(4)]
                for block, item in zip(blocks, quad_transpose(four, group)):
                    block.append(item)
            for position, block in enumerate(blocks):
                target = 2 * (4 * part + position) + parity
                out_ref[target] = jnp.concatenate(block, axis=0).astype(jnp.bfloat16)


def unpack_kernel(order_ref, in_ref, state_ref, base_ref, up_ref, down_ref, held_ref):
    rows = 8 * PERT_TILES
    group = lane_group((8, 128), 32)
    for vector in range(32):
        value = in_ref[vector, 0:80].astype(jnp.float32)[:rows]
        held_ref[rows * vector : rows * vector + rows] = value + roll_lanes(value, -32)
    for quad in range(PERT_TILES):
        for row in range(8):
            a, b, c, d = [
                held_ref[pl.ds(8 * rows * i + 8 * quad + row, 8, stride=rows), :] for i in range(4)
            ]
            first = jnp.where(
                group < 2,
                jnp.where(group == 0, a, roll_lanes(b, 32)),
                jnp.where(group == 2, roll_lanes(c, 64), roll_lanes(d, 96)),
            )
            second = jnp.where(
                group < 2,
                jnp.where(group == 0, roll_lanes(a, 64), roll_lanes(b, 96)),
                jnp.where(group == 2, c, roll_lanes(d, 32)),
            )
            for unit, item in ((2 * quad, first), (2 * quad + 1, second)):
                field, line = unit // 3, 8 * (unit % 3) + row
                state_ref[field, line] = item
                if line < HALO:
                    up_ref[pl.ds(8 * (HALO * field + line), 8)] = item
                if line >= ROWS - HALO:
                    down_ref[pl.ds(8 * (HALO * field + line - ROWS + HALO), 8)] = item
    source = lax.broadcasted_iota(jnp.int32, (128, 512), 0)
    target = lax.broadcasted_iota(jnp.int32, (128, 512), 1)
    spread = ((source % 32 == target % 32) & (source // 32 == target // 128)).astype(jnp.float32)
    spread = spread.astype(jnp.bfloat16)
    place = STATE_HALO_ROWS
    for step in range(2):
        block = in_ref[order_ref[step]].astype(jnp.float32)[8 * PERT_TILES :]
        wide = jnp.dot(block.astype(jnp.bfloat16), spread, preferred_element_type=jnp.float32)
        for unit in range(54):
            tile, field = unit // 18, unit % 18
            item = wide[8 * (unit // 4) : 8 * (unit // 4) + 8, 128 * (unit % 4) : 128 * (unit % 4) + 128]
            base_ref[18 * step + field, 8 * tile : 8 * tile + 8] = item
    for index in range(36):
        width = STEP_ROWS[index // 6]
        up_ref[place : place + width] = base_ref[index, 0:width]
        down_ref[place : place + width] = base_ref[index, ROWS - width : ROWS]
        place += width
    up_ref[place : place + 2] = jnp.zeros((2, 128), jnp.float32)
    down_ref[place : place + 2] = jnp.zeros((2, 128), jnp.float32)


def coefficients(fields, scale):
    results = []
    for layer in range(2):
        depth, xvel, yvel = fields[3 * layer : 3 * layer + 3]
        dx = lambda f: roll_rows(f, -1) - roll_rows(f, 1)
        dy = lambda f: roll_lanes(f, -1) - roll_lanes(f, 1)
        results += [
            scale * (depth + DEPTH),
            scale * xvel,
            scale * yvel,
            scale * dx(xvel),
            scale * dy(xvel) - TIME_STEP * CORIOLIS,
            scale * dx(yvel) + TIME_STEP * CORIOLIS,
            scale * dy(yvel),
        ]
    return results


def section_rows(cur_ref, anchor_ref, new_ref, coef_ref, first, section):
    scale = 0.5 * TIME_STEP
    kind = section % 3

    def coef(index, row):
        return coef_ref[first + index, row]

    def flux(layer, row):
        at = COEF // 2 * layer
        return (
            coef(at, row) * cur_ref[3 * layer + 1, row] + cur_ref[3 * layer, row] * coef(at + 1, row)
        )

    def pressure(row):
        low = cur_ref[3, row]
        top = (scale * GRAVITY_TOP) * (cur_ref[0, row] + low)
        return top, top + (scale * GRAVITY_LOW) * low

    def dy(value):
        return roll_lanes(value, -1) - roll_lanes(value, 1)

    def line(row):
        here, after, before = pressure(row), pressure(row + 1), pressure(row - 1)
        for layer in range(2):
            at = COEF // 2 * layer
            h, u, v = [cur_ref[3 * layer + i, row] for i in range(3)]
            depth, xvel, yvel, xvel_dx, xvel_dy, yvel_dx, yvel_dy = [coef(at + i, row) for i in range(7)]
            du = cur_ref[3 * layer + 1, row + 1] - cur_ref[3 * layer + 1, row - 1]
            dv = cur_ref[3 * layer + 2, row + 1] - cur_ref[3 * layer + 2, row - 1]
            h_new = h - (flux(layer, row + 1) - flux(layer, row - 1)) - dy(depth * v + h * yvel)
            u_new = u - (
                xvel * du + u * xvel_dx + yvel * dy(u) + v * xvel_dy + (after[layer] - before[layer])
            )
            v_new = v - (xvel * dv + u * yvel_dx + yvel * dy(v) + v * yvel_dy + dy(here[layer]))
            for i, value in enumerate((h_new, u_new, v_new)):
                if kind == 1:
                    value = 0.75 * anchor_ref[3 * layer + i, row] + 0.25 * value
                if kind == 2:
                    value = (1.0 / 3.0) * anchor_ref[3 * layer + i, row] + (2.0 / 3.0) * value
                new_ref[3 * layer + i, row] = value

    low, high = section + 1, PAD - 1 - section

    def pair(index, carry):
        line(low + 2 * index)
        line(low + 2 * index + 1)
        return carry

    lax.fori_loop(0, (high - low) // 2, pair, 0)


def step_kernel(
    state_ref, base_ref, top_ref, bottom_ref, cells_ref, gram_ref, start_ref, one_ref, two_ref, coef_ref
):
    for field in range(6):
        start_ref[field, HALO : HALO + ROWS] = state_ref[field]
        for line in range(HALO):
            at = 8 * (HALO * field + line)
            start_ref[field, line] = top_ref[at : at + 8]
            start_ref[field, HALO + ROWS + line] = bottom_ref[at : at + 8]
    place = STATE_HALO_ROWS
    for section in range(6):
        width = STEP_ROWS[section]
        fields = []
        for field in range(6):
            value = base_ref[6 * section + field]
            low = top_ref[place : place + width]
            high = bottom_ref[place : place + width]
            place += width
            fields.append(
                jnp.concatenate(
                    [value, high, jnp.zeros((16 - 2 * width, 128), jnp.float32), low], axis=0
                )
            )
        for index, value in enumerate(coefficients(fields, 0.5 * TIME_STEP)):
            for row in range(-width, ROWS + width):
                at = row % 40
                coef_ref[COEF * (section % 3) + index, HALO + row] = jnp.broadcast_to(
                    value[at : at + 1], (8, 128)
                )
        if section % 3 == 2:
            anchor = start_ref
            begin = section - 2
            section_rows(anchor, anchor, one_ref, coef_ref, 0, begin)
            section_rows(one_ref, anchor, two_ref, coef_ref, COEF, begin + 1)
            section_rows(two_ref, anchor, start_ref, coef_ref, 2 * COEF, begin + 2)
    block = lane_group((8, 128), 16)
    for unit in range(18):
        field, tile = unit // 3, unit % 3
        lines = [start_ref[field, HALO + 8 * tile + row] for row in range(8)]
        for quarter in range(4):
            total = None
            for row in range(8):
                moved = roll_lanes(lines[row], 16 * row - 32 * quarter - 8)
                total = moved if total is None else jnp.where(block == row, moved, total)
            cells_ref[8 * quarter : 8 * quarter + 8, 128 * unit : 128 * unit + 128] = total
    cells = cells_ref[...]
    gram = lax.dot_general(
        cells,
        cells,
        (((1,), (1,)), ((), ())),
        precision=lax.Precision.HIGHEST,
        preferred_element_type=jnp.float32,
    )
    compact = jnp.concatenate([gram[8 * i : 8 * i + 8] for i in range(4)], axis=1)
    for peer in range(gram_ref.shape[0]):
        gram_ref[peer] = compact


def sum_kernel(in_ref, out_ref):
    total = in_ref[0]
    for peer in range(1, in_ref.shape[0]):
        total = total + in_ref[peer]
    for peer in range(out_ref.shape[0]):
        out_ref[peer] = total


def solve_kernel(entries, parts_ref, cells_ref, ortho_ref, upper_ref):
    total = parts_ref[0]
    for peer in range(1, parts_ref.shape[0]):
        total = total + parts_ref[peer]
    total = total / entries
    lane = lax.broadcasted_iota(jnp.int32, (32, 128), 1)
    line = lax.broadcasted_iota(jnp.int32, (32, 128), 0)
    wide = jnp.concatenate([roll_lanes(total, -32 * i) for i in range(4)], axis=0)
    work = jnp.where(lane < 32, wide, jnp.where(lane == line + 32, 1.0, 0.0))
    roots = jnp.zeros((32, 128), jnp.float32)
    for k in range(32):
        row = work[k : k + 1]
        pivot = row[:, k : k + 1]
        factor = jnp.where(line[:, :1] > k, work[:, k : k + 1] / pivot, 0.0)
        roots = jnp.where(line == k, jnp.broadcast_to(pivot, (32, 128)), roots)
        work = work - factor * row
    work = work / jnp.sqrt(roots)
    upper_ref[...] = jnp.where(lane >= line, work, 0.0)[:, :32]
    inverse = roll_lanes(work, -32)[:, :32]
    ortho = jnp.dot(
        inverse, cells_ref[...], precision=lax.Precision.HIGHEST, preferred_element_type=jnp.float32
    )
    ortho_ref[...] = ortho.reshape(ortho_ref.shape)


def place_kernel(in_ref, out_ref):
    block = lane_group((8, 128), 16)
    line = lax.broadcasted_iota(jnp.int32, (8, 128), 0)
    distance = (block - line) % 8
    for unit in range(18):
        field, tile = unit // 3, unit % 3
        for part in range(4):
            value = in_ref[8 * part : 8 * part + 8, 0, 128 * unit : 128 * unit + 128]
            total = value
            for k in range(1, 8):
                moved = roll_rows(roll_lanes(value, 16 * k), -k)
                total = jnp.where(distance == k, moved, total)
            out_ref[field, 8 * tile : 8 * tile + 8, 128 * part : 128 * part + 128] = total


def call(kernel, out_shape, name, scratch=(), smem=0):
    specs = {}
    if smem:
        specs = dict(
            in_specs=[pl.BlockSpec(memory_space=pltpu.SMEM)] * smem
            + [pl.BlockSpec(memory_space=pltpu.VMEM)]
        )
    return pl.pallas_call(
        kernel, out_shape=out_shape, scratch_shapes=list(scratch), compiler_params=LIMIT, name=name, **specs
    )


def f32(*shape):
    return jax.ShapeDtypeStruct(shape, jnp.float32)


def body(perturbation, trajectory, step_order):
    vectors, tiles = lax.axis_size("vec"), lax.axis_size("space")
    sent = call(pack_kernel, jax.ShapeDtypeStruct((32, 8 * TILES, 128), jnp.bfloat16), "pack")(
        perturbation[0], trajectory[0].reshape(18, ROWS, 512)
    )
    held = lax.all_to_all(sent, "vec", split_axis=0, concat_axis=0, tiled=True)
    state, base, up, down = call(
        unpack_kernel,
        (f32(6, ROWS, 8, 128), f32(36, ROWS, 128), f32(HALO_ROWS, 128), f32(HALO_ROWS, 128)),
        "unpack",
        [pltpu.VMEM((32 * 8 * PERT_TILES, 128), jnp.float32)],
        smem=1,
    )(step_order, held)
    top = lax.ppermute(down, "space", [(i, (i + 1) % tiles) for i in range(tiles)])
    bottom = lax.ppermute(up, "space", [(i, (i - 1) % tiles) for i in range(tiles)])
    padded = pltpu.VMEM((6, PAD, 8, 128), jnp.float32)
    cells, gram = call(
        step_kernel,
        (f32(32, 2304), f32(tiles, 8, 128)),
        "steps",
        [padded, padded, padded, pltpu.VMEM((3 * COEF, PAD, 8, 128), jnp.float32)],
    )(state, base, top, bottom)
    gram = lax.all_to_all(gram, "space", split_axis=0, concat_axis=0, tiled=True)
    gram = call(sum_kernel, f32(vectors, 8, 128), "sums")(gram)
    gram = lax.all_to_all(gram, "vec", split_axis=0, concat_axis=0, tiled=True)
    entries = float(6 * ROWS * 512 * tiles)
    ortho, upper = call(
        lambda *refs: solve_kernel(entries, *refs), (f32(32, 1, 2304), f32(32, 32)), "solve"
    )(gram, cells)
    ortho = lax.all_to_all(ortho, "vec", split_axis=0, concat_axis=0, tiled=True)
    placed = call(place_kernel, f32(6, ROWS, 512), "place")(ortho)
    return placed[None], upper


def solution(mesh):
    in_specs = (P("vec", None, "space", None), P("vec", None, None, "space", None), P())
    out_specs = (P("vec", None, "space", None), P())
    return jax.shard_map(body, mesh=mesh, in_specs=in_specs, out_specs=out_specs, check_vma=False)
```

```python
import jax
import jax.numpy as jnp
from jax import lax
from jax.experimental import pallas as pl
from jax.experimental.pallas import tpu as pltpu
from jax.sharding import PartitionSpec as P

GRAVITY_TOP = 1.0
GRAVITY_LOW = 0.5
DEPTH = 1.0
CORIOLIS = 0.3
TIME_STEP = 0.25

ROWS = 24
HALO = 6
PAD = ROWS + 2 * HALO
PERT_PAIRS = 9
PAIRS = 36
QUADS = PAIRS // 4
BASE_QUAD = PERT_PAIRS // 4
TOP_CODE = 32000.0
BASE_SCALE = 16384.0
STEP_ROWS = tuple(HALO - section for section in range(6))
BASE_HALO_ROWS = 6 * sum(STEP_ROWS)
STATE_HALO_ROWS = 6 * HALO * 8
HALO_ROWS = STATE_HALO_ROWS + BASE_HALO_ROWS + 2
COEF = 14
LIMIT = pltpu.CompilerParams(vmem_limit_bytes=40 * 1024 * 1024)


def roll_lanes(value, shift):
    shift %= value.shape[-1]
    return pltpu.roll(value, shift, 1) if shift else value


def roll_rows(value, shift):
    shift %= value.shape[0]
    return pltpu.roll(value, shift, 0) if shift else value


def lane_group(shape, size):
    return lax.broadcasted_iota(jnp.int32, shape, 1) // size


def quad_transpose(items, group):
    odd = (group % 2) == 1
    upper = group >= 2
    a, b, c, d = items
    a, b = jnp.where(odd, roll_lanes(b, 32), a), jnp.where(odd, b, roll_lanes(a, -32))
    c, d = jnp.where(odd, roll_lanes(d, 32), c), jnp.where(odd, d, roll_lanes(c, -32))
    a, c = jnp.where(upper, roll_lanes(c, 64), a), jnp.where(upper, c, roll_lanes(a, 64))
    b, d = jnp.where(upper, roll_lanes(d, 64), b), jnp.where(upper, d, roll_lanes(b, 64))
    return a, b, c, d


def join(first, second):
    return (first & 0xFFFF) | (second << 16)


def halves(value):
    return (value << 16) >> 16, value >> 16


def to_code(value):
    return jnp.round(value).astype(jnp.int32)


def spacing(level):
    return jnp.exp2(level.astype(jnp.float32) * 0.125)


def pack_kernel(pert_hbm, traj_hbm, out_ref, pert_ref, traj_ref, pair_ref, sems):
    copies = [
        pltpu.make_async_copy(pert_hbm, pert_ref, sems.at[0]),
        pltpu.make_async_copy(traj_hbm, traj_ref, sems.at[1]),
    ]
    for copy in copies:
        copy.start()
    copies[0].wait()
    largest = jnp.abs(pert_ref[0, 0:8])
    for field in range(6):
        for tile in range(3):
            largest = jnp.maximum(largest, jnp.abs(pert_ref[field, 8 * tile : 8 * tile + 8]))
    largest = jnp.maximum(jnp.max(largest, axis=(0, 1), keepdims=True), 1e-30)
    level = jnp.ceil(8.0 * jnp.log2(largest)).astype(jnp.int32)
    inverse = jnp.broadcast_to(1.0 / spacing(level), (8, 512))
    level = jnp.broadcast_to(level, (8, 512))
    lane = lax.broadcasted_iota(jnp.int32, (8, 512), 1)
    line = lax.broadcasted_iota(jnp.int32, (8, 512), 0)

    def code(value):
        size = jnp.minimum(TOP_CODE * jnp.sqrt(jnp.abs(value) * inverse), 32767.0)
        return to_code(jnp.where(value < 0, -size, size))

    for pair in range(PERT_PAIRS):
        field, tile = pair // 3, pair % 3
        first = code(pert_ref[field, 8 * tile : 8 * tile + 8])
        second = code(pert_ref[field + 3, 8 * tile : 8 * tile + 8])
        pair_ref[8 * pair : 8 * pair + 8] = join(first, second)
    copies[1].wait()
    for section in range(3):
        for field in range(3):
            value = [
                to_code(traj_ref[6 * section + i].astype(jnp.float32) * BASE_SCALE)
                for i in (field, field + 3)
            ]
            both = join(*value)
            for tile in range(3):
                pair = PERT_PAIRS + 9 * tile + 3 * section + field
                pair_ref[8 * pair : 8 * pair + 8] = both[8 * tile : 8 * tile + 8]
    group = lane_group((8, 128), 32)
    for parity in range(2):
        shift = 8 if parity == 0 else -8
        for quad in range(QUADS):
            items = []
            for i in range(4):
                pair = 4 * quad + i
                item = roll_lanes(pair_ref[8 * pair : 8 * pair + 8], shift)
                if pair == 0:
                    item = jnp.where((lane % 32 == 0) & (line == 0), level, item)
                items.append(item)
            for part in range(4):
                columns = slice(128 * part, 128 * part + 128)
                four = quad_transpose([item[:, columns] for item in items], group)
                for position, item in enumerate(four):
                    target = 2 * (4 * part + position) + parity
                    out_ref[target, 8 * quad : 8 * quad + 8] = item


def unpack_kernel(order_ref, in_ref, state_ref, base_ref, up_ref, down_ref):
    group = lane_group((8, 128), 32)
    column = lax.broadcasted_iota(jnp.int32, (8, 128), 1) % 32
    scale = None
    for quad in range(BASE_QUAD + 1):
        for row in range(8):
            items = [
                in_ref[pl.ds(8 * QUADS * 8 * i + 8 * quad + row, 8, stride=8 * QUADS), :]
                for i in range(4)
            ]
            for position, both in enumerate(quad_transpose(items, group)):
                pair = 4 * quad + position
                if pair >= PERT_PAIRS:
                    continue
                first, second = halves(both)
                if scale is None:
                    level = jnp.where(column == 0, first, 0)
                    for shift in (1, 2, 4, 8, 16):
                        level = level + roll_lanes(level, shift)
                    scale = spacing(level) * (1.0 / (TOP_CODE * TOP_CODE))
                for layer, item in enumerate((first, second)):
                    item = item.astype(jnp.float32)
                    item = item * jnp.abs(item) * scale
                    field, line = pair // 3 + 3 * layer, 8 * (pair % 3) + row
                    state_ref[field, line] = item
                    if line < HALO:
                        up_ref[pl.ds(8 * (HALO * field + line), 8)] = item
                    if line >= ROWS - HALO:
                        down_ref[pl.ds(8 * (HALO * field + line - ROWS + HALO), 8)] = item
    source = lax.broadcasted_iota(jnp.int32, (128, 512), 0)
    target = lax.broadcasted_iota(jnp.int32, (128, 512), 1)
    spread = ((source % 32 == target % 32) & (source // 32 == target // 128)).astype(jnp.float32)
    spread = spread.astype(jnp.bfloat16)
    begin, end = 8 * BASE_QUAD, 8 * QUADS
    for step in range(2):
        block = in_ref[pl.ds(pl.multiple_of(order_ref[step] * end, 8) + begin, end - begin), :]
        for layer, part in enumerate(halves(block)):
            part = part.astype(jnp.float32).astype(jnp.bfloat16)
            wide = jnp.dot(part, spread, preferred_element_type=jnp.float32) * (1.0 / BASE_SCALE)
            for unit in range(27):
                tile, field = unit // 9, 6 * (unit % 9 // 3) + unit % 3 + 3 * layer
                at = PERT_PAIRS + unit - 4 * BASE_QUAD
                item = wide[8 * (at // 4) : 8 * (at // 4) + 8, 128 * (at % 4) : 128 * (at % 4) + 128]
                base_ref[18 * step + field, 8 * tile : 8 * tile + 8] = item
    place = STATE_HALO_ROWS
    for index in range(36):
        width = STEP_ROWS[index // 6]
        up_ref[place : place + width] = base_ref[index, 0:width]
        down_ref[place : place + width] = base_ref[index, ROWS - width : ROWS]
        place += width
    up_ref[place : place + 2] = jnp.zeros((2, 128), jnp.float32)
    down_ref[place : place + 2] = jnp.zeros((2, 128), jnp.float32)


def coefficients(fields, scale):
    results = []
    for layer in range(2):
        depth, xvel, yvel = fields[3 * layer : 3 * layer + 3]
        dx = lambda f: roll_rows(f, -1) - roll_rows(f, 1)
        dy = lambda f: roll_lanes(f, -1) - roll_lanes(f, 1)
        results += [
            scale * (depth + DEPTH),
            scale * xvel,
            scale * yvel,
            scale * dx(xvel),
            scale * dy(xvel) - TIME_STEP * CORIOLIS,
            scale * dx(yvel) + TIME_STEP * CORIOLIS,
            scale * dy(yvel),
        ]
    return results


def section_rows(cur_ref, anchor_ref, new_ref, coef_ref, first, section):
    scale = 0.5 * TIME_STEP
    kind = section % 3

    def coef(index, row):
        return coef_ref[first + index, row]

    def flux(layer, row):
        at = COEF // 2 * layer
        return (
            coef(at, row) * cur_ref[3 * layer + 1, row] + cur_ref[3 * layer, row] * coef(at + 1, row)
        )

    def pressure(row):
        low = cur_ref[3, row]
        top = (scale * GRAVITY_TOP) * (cur_ref[0, row] + low)
        return top, top + (scale * GRAVITY_LOW) * low

    def dy(value):
        return roll_lanes(value, -1) - roll_lanes(value, 1)

    def line(row):
        here, after, before = pressure(row), pressure(row + 1), pressure(row - 1)
        for layer in range(2):
            at = COEF // 2 * layer
            h, u, v = [cur_ref[3 * layer + i, row] for i in range(3)]
            depth, xvel, yvel, xvel_dx, xvel_dy, yvel_dx, yvel_dy = [coef(at + i, row) for i in range(7)]
            du = cur_ref[3 * layer + 1, row + 1] - cur_ref[3 * layer + 1, row - 1]
            dv = cur_ref[3 * layer + 2, row + 1] - cur_ref[3 * layer + 2, row - 1]
            h_new = h - (flux(layer, row + 1) - flux(layer, row - 1)) - dy(depth * v + h * yvel)
            u_new = u - (
                xvel * du + u * xvel_dx + yvel * dy(u) + v * xvel_dy + (after[layer] - before[layer])
            )
            v_new = v - (xvel * dv + u * yvel_dx + yvel * dy(v) + v * yvel_dy + dy(here[layer]))
            for i, value in enumerate((h_new, u_new, v_new)):
                if kind == 1:
                    value = 0.75 * anchor_ref[3 * layer + i, row] + 0.25 * value
                if kind == 2:
                    value = (1.0 / 3.0) * anchor_ref[3 * layer + i, row] + (2.0 / 3.0) * value
                new_ref[3 * layer + i, row] = value

    low, high = section + 1, PAD - 1 - section

    def pair(index, carry):
        line(low + 2 * index)
        line(low + 2 * index + 1)
        return carry

    lax.fori_loop(0, (high - low) // 2, pair, 0)


def step_kernel(
    state_ref, base_ref, top_ref, bottom_ref, cells_ref, gram_ref, start_ref, one_ref, two_ref, coef_ref
):
    for field in range(6):
        start_ref[field, HALO : HALO + ROWS] = state_ref[field]
        for line in range(HALO):
            at = 8 * (HALO * field + line)
            start_ref[field, line] = top_ref[at : at + 8]
            start_ref[field, HALO + ROWS + line] = bottom_ref[at : at + 8]
    place = STATE_HALO_ROWS
    for section in range(6):
        width = STEP_ROWS[section]
        fields = []
        for field in range(6):
            value = base_ref[6 * section + field]
            low = top_ref[place : place + width]
            high = bottom_ref[place : place + width]
            place += width
            fields.append(
                jnp.concatenate(
                    [value, high, jnp.zeros((16 - 2 * width, 128), jnp.float32), low], axis=0
                )
            )
        for index, value in enumerate(coefficients(fields, 0.5 * TIME_STEP)):
            for row in range(-width, ROWS + width):
                at = row % 40
                coef_ref[COEF * (section % 3) + index, HALO + row] = jnp.broadcast_to(
                    value[at : at + 1], (8, 128)
                )
        if section % 3 == 2:
            anchor = start_ref
            begin = section - 2
            section_rows(anchor, anchor, one_ref, coef_ref, 0, begin)
            section_rows(one_ref, anchor, two_ref, coef_ref, COEF, begin + 1)
            section_rows(two_ref, anchor, start_ref, coef_ref, 2 * COEF, begin + 2)
    block = lane_group((8, 128), 16)
    for unit in range(18):
        field, tile = unit // 3, unit % 3
        lines = [start_ref[field, HALO + 8 * tile + row] for row in range(8)]
        for quarter in range(4):
            total = None
            for row in range(8):
                moved = roll_lanes(lines[row], 16 * row - 32 * quarter - 8)
                total = moved if total is None else jnp.where(block == row, moved, total)
            cells_ref[8 * quarter : 8 * quarter + 8, 128 * unit : 128 * unit + 128] = total
    cells = cells_ref[...]
    gram = lax.dot_general(
        cells,
        cells,
        (((1,), (1,)), ((), ())),
        precision=lax.Precision.HIGHEST,
        preferred_element_type=jnp.float32,
    )
    compact = jnp.concatenate([gram[8 * i : 8 * i + 8] for i in range(4)], axis=1)
    for peer in range(gram_ref.shape[0]):
        gram_ref[peer] = compact


def sum_kernel(in_ref, out_ref):
    total = in_ref[0]
    for peer in range(1, in_ref.shape[0]):
        total = total + in_ref[peer]
    for peer in range(out_ref.shape[0]):
        out_ref[peer] = total


def solve_kernel(entries, parts_ref, cells_ref, ortho_ref, upper_ref):
    total = parts_ref[0]
    for peer in range(1, parts_ref.shape[0]):
        total = total + parts_ref[peer]
    total = total / entries
    lane = lax.broadcasted_iota(jnp.int32, (32, 128), 1)
    line = lax.broadcasted_iota(jnp.int32, (32, 128), 0)
    wide = jnp.concatenate([roll_lanes(total, -32 * i) for i in range(4)], axis=0)
    work = jnp.where(lane < 32, wide, jnp.where(lane == line + 32, 1.0, 0.0))
    roots = jnp.zeros((32, 128), jnp.float32)
    for k in range(32):
        row = work[k : k + 1]
        pivot = row[:, k : k + 1]
        factor = jnp.where(line[:, :1] > k, work[:, k : k + 1] / pivot, 0.0)
        roots = jnp.where(line == k, jnp.broadcast_to(pivot, (32, 128)), roots)
        work = work - factor * row
    work = work / jnp.sqrt(roots)
    upper_ref[...] = jnp.where(lane >= line, work, 0.0)[:, :32]
    inverse = roll_lanes(work, -32)[:, :32]
    ortho = jnp.dot(
        inverse, cells_ref[...], precision=lax.Precision.HIGHEST, preferred_element_type=jnp.float32
    )
    ortho_ref[...] = ortho.reshape(ortho_ref.shape)


def place_kernel(in_ref, out_ref):
    block = lane_group((8, 128), 16)
    line = lax.broadcasted_iota(jnp.int32, (8, 128), 0)
    distance = (block - line) % 8
    for unit in range(18):
        field, tile = unit // 3, unit % 3
        for part in range(4):
            value = in_ref[8 * part : 8 * part + 8, 0, 128 * unit : 128 * unit + 128]
            total = value
            for k in range(1, 8):
                moved = roll_rows(roll_lanes(value, 16 * k), -k)
                total = jnp.where(distance == k, moved, total)
            out_ref[field, 8 * tile : 8 * tile + 8, 128 * part : 128 * part + 128] = total


def call(kernel, out_shape, name, scratch=(), spaces=None):
    specs = {}
    if spaces:
        specs = dict(in_specs=[pl.BlockSpec(memory_space=space) for space in spaces])
    return pl.pallas_call(
        kernel, out_shape=out_shape, scratch_shapes=list(scratch), compiler_params=LIMIT, name=name, **specs
    )


def f32(*shape):
    return jax.ShapeDtypeStruct(shape, jnp.float32)


def body(perturbation, trajectory, step_order):
    vectors, tiles = lax.axis_size("vec"), lax.axis_size("space")
    sent = call(
        pack_kernel,
        jax.ShapeDtypeStruct((32, 8 * QUADS, 128), jnp.int32),
        "pack",
        [
            pltpu.VMEM((6, ROWS, 512), jnp.float32),
            pltpu.VMEM((18, ROWS, 512), jnp.bfloat16),
            pltpu.VMEM((8 * PAIRS, 512), jnp.int32),
            pltpu.SemaphoreType.DMA((2,)),
        ],
        spaces=(pl.ANY, pl.ANY),
    )(perturbation[0], trajectory[0].reshape(18, ROWS, 512))
    held = lax.all_to_all(sent, "vec", split_axis=0, concat_axis=0, tiled=True)
    state, base, up, down = call(
        unpack_kernel,
        (f32(6, ROWS, 8, 128), f32(36, ROWS, 128), f32(HALO_ROWS, 128), f32(HALO_ROWS, 128)),
        "unpack",
        spaces=(pltpu.SMEM, pltpu.VMEM),
    )(step_order, held.reshape(32 * 8 * QUADS, 128))
    top = lax.ppermute(down, "space", [(i, (i + 1) % tiles) for i in range(tiles)])
    bottom = lax.ppermute(up, "space", [(i, (i - 1) % tiles) for i in range(tiles)])
    padded = pltpu.VMEM((6, PAD, 8, 128), jnp.float32)
    cells, gram = call(
        step_kernel,
        (f32(32, 2304), f32(tiles, 8, 128)),
        "steps",
        [padded, padded, padded, pltpu.VMEM((3 * COEF, PAD, 8, 128), jnp.float32)],
    )(state, base, top, bottom)
    gram = lax.all_to_all(gram, "space", split_axis=0, concat_axis=0, tiled=True)
    gram = call(sum_kernel, f32(vectors, 8, 128), "sums")(gram)
    gram = lax.all_to_all(gram, "vec", split_axis=0, concat_axis=0, tiled=True)
    entries = float(6 * ROWS * 512 * tiles)
    ortho, upper = call(
        lambda *refs: solve_kernel(entries, *refs), (f32(32, 1, 2304), f32(32, 32)), "solve"
    )(gram, cells)
    ortho = lax.all_to_all(ortho, "vec", split_axis=0, concat_axis=0, tiled=True)
    placed = call(place_kernel, f32(6, ROWS, 512), "place")(ortho)
    return placed[None], upper


def solution(mesh):
    in_specs = (P("vec", None, "space", None), P("vec", None, None, "space", None), P())
    out_specs = (P("vec", None, "space", None), P())
    return jax.shard_map(body, mesh=mesh, in_specs=in_specs, out_specs=out_specs, check_vma=False)
```

```python
import jax
import jax.numpy as jnp
from jax import lax
from jax.experimental import pallas as pl
from jax.experimental.pallas import tpu as pltpu
from jax.sharding import PartitionSpec as P

GRAVITY_TOP = 1.0
GRAVITY_LOW = 0.5
DEPTH = 1.0
CORIOLIS = 0.3
TIME_STEP = 0.25

ROWS = 24
HALO = 6
PAD = ROWS + 2 * HALO
PERT_PAIRS = 9
PAIRS = 36
QUADS = PAIRS // 4
BASE_QUAD = PERT_PAIRS // 4
TOP_CODE = 32000.0
BASE_SCALE = 16384.0
STEP_ROWS = tuple(HALO - section for section in range(6))
BASE_HALO_ROWS = 6 * sum(STEP_ROWS)
STATE_HALO_ROWS = 6 * HALO * 8
HALO_ROWS = STATE_HALO_ROWS + BASE_HALO_ROWS + 2
COEF = 14


def roll_lanes(value, shift):
    shift %= value.shape[-1]
    return pltpu.roll(value, shift, 1) if shift else value


def roll_rows(value, shift):
    shift %= value.shape[0]
    return pltpu.roll(value, shift, 0) if shift else value


def lane_group(shape, size):
    return lax.broadcasted_iota(jnp.int32, shape, 1) // size


def quad_transposes(quads):
    group = lane_group((8, 128), 32)
    odd, upper = (group % 2) == 1, group >= 2
    moved = [(roll_lanes(b, 32), roll_lanes(a, -32), roll_lanes(d, 32), roll_lanes(c, -32)) for a, b, c, d in quads]
    quads = [
        (jnp.where(odd, p, a), jnp.where(odd, b, q), jnp.where(odd, r, c), jnp.where(odd, d, t))
        for (a, b, c, d), (p, q, r, t) in zip(quads, moved)
    ]
    moved = [tuple(roll_lanes(item, 64) for item in quad) for quad in quads]
    return [
        (jnp.where(upper, r, a), jnp.where(upper, t, b), jnp.where(upper, c, p), jnp.where(upper, d, q))
        for (a, b, c, d), (p, q, r, t) in zip(quads, moved)
    ]


def join(first, second):
    return (first & 0xFFFF) | (second << 16)


def halves(value):
    return (value << 16) >> 16, value >> 16


def to_code(value):
    return jnp.round(value).astype(jnp.int32)


def level_of(largest):
    return jnp.ceil(8.0 * jnp.log2(jnp.maximum(largest, 1e-30))).astype(jnp.int32)


def spacing(level):
    return jnp.exp2(level.astype(jnp.float32) * 0.125)


def root_code(value, inverse):
    size = jnp.minimum(TOP_CODE * jnp.sqrt(jnp.abs(value) * inverse), 32767.0)
    return to_code(jnp.where(value < 0, -size, size))


def from_root_code(code, scale):
    code = code.astype(jnp.float32)
    return code * jnp.abs(code) * scale


def code_scale(level):
    return spacing(level) * (1.0 / (TOP_CODE * TOP_CODE))


def pack_kernel(pert_hbm, traj_hbm, out_ref, pert_ref, traj_ref, pair_ref, sems):
    copies = [
        pltpu.make_async_copy(pert_hbm, pert_ref, sems.at[0]),
        pltpu.make_async_copy(traj_hbm, traj_ref, sems.at[1]),
    ]
    for copy in copies:
        copy.start()
    copies[0].wait()
    largest = jnp.abs(pert_ref[0, 0:8])
    for field in range(6):
        for tile in range(3):
            largest = jnp.maximum(largest, jnp.abs(pert_ref[field, 8 * tile : 8 * tile + 8]))
    level = level_of(jnp.max(largest, axis=(0, 1), keepdims=True))
    inverse = jnp.broadcast_to(1.0 / spacing(level), (8, 512))
    level = jnp.broadcast_to(level, (8, 512))
    lane = lax.broadcasted_iota(jnp.int32, (8, 512), 1)
    line = lax.broadcasted_iota(jnp.int32, (8, 512), 0)

    for pair in range(PERT_PAIRS):
        field, tile = pair // 3, pair % 3
        first = root_code(pert_ref[field, 8 * tile : 8 * tile + 8], inverse)
        second = root_code(pert_ref[field + 3, 8 * tile : 8 * tile + 8], inverse)
        pair_ref[8 * pair : 8 * pair + 8] = join(first, second)
    copies[1].wait()
    for section in range(3):
        for field in range(3):
            value = [
                to_code(traj_ref[6 * section + i].astype(jnp.float32) * BASE_SCALE)
                for i in (field, field + 3)
            ]
            both = join(*value)
            for tile in range(3):
                pair = PERT_PAIRS + 9 * tile + 3 * section + field
                pair_ref[8 * pair : 8 * pair + 8] = both[8 * tile : 8 * tile + 8]
    for begin in range(0, QUADS, 3):
        places, quads = [], []
        for quad in range(begin, begin + 3):
            raw = [pair_ref[8 * pair : 8 * pair + 8] for pair in range(4 * quad, 4 * quad + 4)]
            for parity in range(2):
                items = [roll_lanes(item, 8 if parity == 0 else -8) for item in raw]
                if quad == 0:
                    items[0] = jnp.where((lane % 32 == 0) & (line == 0), level, items[0])
                for part in range(4):
                    columns = slice(128 * part, 128 * part + 128)
                    places.append((8 * part + parity, 8 * quad))
                    quads.append([item[:, columns] for item in items])
        for (target, at), four in zip(places, quad_transposes(quads)):
            for position, item in enumerate(four):
                out_ref[target + 2 * position, at : at + 8] = item


def unpack_kernel(order_ref, in_ref, state_ref, base_ref, up_ref, down_ref):
    column = lax.broadcasted_iota(jnp.int32, (8, 128), 1) % 32
    scale = None
    for quad in range(BASE_QUAD + 1):
        rows = [
            [
                in_ref[pl.ds(8 * QUADS * 8 * i + 8 * quad + row, 8, stride=8 * QUADS), :]
                for i in range(4)
            ]
            for row in range(8)
        ]
        for row, four in enumerate(quad_transposes(rows)):
            for pair, both in enumerate(four, 4 * quad):
                if pair >= PERT_PAIRS:
                    continue
                first, second = halves(both)
                if scale is None:
                    level = jnp.where(column == 0, first, 0)
                    for shift in (1, 2, 4, 8, 16):
                        level = level + roll_lanes(level, shift)
                    scale = code_scale(level)
                for layer, item in enumerate((first, second)):
                    item = from_root_code(item, scale)
                    field, line = pair // 3 + 3 * layer, 8 * (pair % 3) + row
                    state_ref[field, line] = item
                    if line < HALO:
                        up_ref[pl.ds(8 * (HALO * field + line), 8)] = item
                    if line >= ROWS - HALO:
                        down_ref[pl.ds(8 * (HALO * field + line - ROWS + HALO), 8)] = item
    source = lax.broadcasted_iota(jnp.int32, (128, 512), 0)
    target = lax.broadcasted_iota(jnp.int32, (128, 512), 1)
    spread = ((source % 32 == target % 32) & (source // 32 == target // 128)).astype(jnp.float32)
    spread = spread.astype(jnp.bfloat16)
    begin, end = 8 * BASE_QUAD, 8 * QUADS
    for step in range(2):
        block = in_ref[pl.ds(pl.multiple_of(order_ref[step] * end, 8) + begin, end - begin), :]
        for layer, part in enumerate(halves(block)):
            part = part.astype(jnp.float32).astype(jnp.bfloat16)
            wide = jnp.dot(part, spread, preferred_element_type=jnp.float32) * (1.0 / BASE_SCALE)
            for unit in range(27):
                tile, field = unit // 9, 6 * (unit % 9 // 3) + unit % 3 + 3 * layer
                at = PERT_PAIRS + unit - 4 * BASE_QUAD
                item = wide[8 * (at // 4) : 8 * (at // 4) + 8, 128 * (at % 4) : 128 * (at % 4) + 128]
                base_ref[18 * step + field, 8 * tile : 8 * tile + 8] = item
    place = STATE_HALO_ROWS
    for index in range(36):
        width = STEP_ROWS[index // 6]
        up_ref[place : place + width] = base_ref[index, 0:width]
        down_ref[place : place + width] = base_ref[index, ROWS - width : ROWS]
        place += width
    up_ref[place : place + 2] = jnp.zeros((2, 128), jnp.float32)
    down_ref[place : place + 2] = jnp.zeros((2, 128), jnp.float32)


def coefficients(fields, scale):
    results = []
    dx = lambda f: roll_rows(f, -1) - roll_rows(f, 1)
    dy = lambda f: roll_lanes(f, -1) - roll_lanes(f, 1)
    for layer in range(2):
        depth, xvel, yvel = fields[3 * layer : 3 * layer + 3]
        results += [
            scale * (depth + DEPTH),
            scale * xvel,
            scale * yvel,
            scale * dx(xvel),
            scale * dy(xvel) - TIME_STEP * CORIOLIS,
            scale * dx(yvel) + TIME_STEP * CORIOLIS,
            scale * dy(yvel),
        ]
    return results


def section_rows(cur_ref, anchor_ref, new_ref, coef, section):
    scale = 0.5 * TIME_STEP
    kind = section % 3

    def dy(value):
        return roll_lanes(value, -1) - roll_lanes(value, 1)

    def block(row, count):
        span = range(-1, count + 1)
        h = [[cur_ref[3 * layer, row + i] for i in span] for layer in range(2)]
        top = [(scale * GRAVITY_TOP) * (h[0][i] + h[1][i]) for i in range(count + 2)]
        low = [top[i] + (scale * GRAVITY_LOW) * h[1][i] for i in range(count + 2)]
        for layer, pressure in enumerate((top, low)):
            at = COEF // 2 * layer
            u = [cur_ref[3 * layer + 1, row + i] for i in span]
            v = [cur_ref[3 * layer + 2, row + i] for i in span]
            depth = [coef(at, row + i) for i in span]
            xvel = [coef(at + 1, row + i) for i in span]
            flux = [depth[i] * u[i] + h[layer][i] * xvel[i] for i in range(count + 2)]
            for i in range(1, count + 1):
                line = row + i - 1
                h_i, u_i, v_i = h[layer][i], u[i], v[i]
                yvel, xvel_dx, xvel_dy, yvel_dx, yvel_dy = [coef(at + k, line) for k in range(2, 7)]
                h_new = h_i - (flux[i + 1] - flux[i - 1]) - dy(depth[i] * v_i + h_i * yvel)
                u_new = u_i - (
                    xvel[i] * (u[i + 1] - u[i - 1])
                    + u_i * xvel_dx
                    + yvel * dy(u_i)
                    + v_i * xvel_dy
                    + (pressure[i + 1] - pressure[i - 1])
                )
                v_new = v_i - (
                    xvel[i] * (v[i + 1] - v[i - 1])
                    + u_i * yvel_dx
                    + yvel * dy(v_i)
                    + v_i * yvel_dy
                    + dy(pressure[i])
                )
                for field, value in enumerate((h_new, u_new, v_new)):
                    field += 3 * layer
                    if kind == 1:
                        value = 0.75 * anchor_ref[field, line] + 0.25 * value
                    if kind == 2:
                        value = (1.0 / 3.0) * anchor_ref[field, line] + (2.0 / 3.0) * value
                    new_ref[field, line] = value

    block(section + 1, PAD - 2 - 2 * section)


def step_kernel(
    state_ref, base_ref, top_ref, bottom_ref, cells_ref, gram_ref, start_ref, one_ref, two_ref, coef_ref
):
    for field in range(6):
        start_ref[field, HALO : HALO + ROWS] = state_ref[field]
        for line in range(HALO):
            at = 8 * (HALO * field + line)
            start_ref[field, line] = top_ref[at : at + 8]
            start_ref[field, HALO + ROWS + line] = bottom_ref[at : at + 8]
    place = STATE_HALO_ROWS
    buffers = (start_ref, one_ref, two_ref, start_ref)
    for section in range(6):
        width = STEP_ROWS[section]
        fields = []
        for field in range(6):
            pieces = [
                top_ref[place : place + width],
                base_ref[6 * section + field],
                bottom_ref[place : place + width],
            ]
            if width < 8:
                pieces.append(jnp.zeros((16 - 2 * width, 128), jnp.float32))
            fields.append(jnp.concatenate(pieces, axis=0))
            place += width
        for index, value in enumerate(coefficients(fields, 0.5 * TIME_STEP)):
            coef_ref[index] = value

        def coef(index, row):
            return coef_ref[index, pl.ds(row - HALO + width, 8, stride=0), :]

        kind = section % 3
        section_rows(buffers[kind], start_ref, buffers[kind + 1], coef, section)
    block = lane_group((8, 128), 16)
    for unit in range(18):
        field, tile = unit // 3, unit % 3
        lines = [start_ref[field, HALO + 8 * tile + row] for row in range(8)]
        for quarter in range(4):
            total = None
            for row in range(8):
                moved = roll_lanes(lines[row], 16 * row - 32 * quarter - 8)
                total = moved if total is None else jnp.where(block == row, moved, total)
            cells_ref[8 * quarter : 8 * quarter + 8, 128 * unit : 128 * unit + 128] = total
    cells = cells_ref[...]
    gram = lax.dot_general(
        cells,
        cells,
        (((1,), (1,)), ((), ())),
        precision=lax.Precision.HIGHEST,
        preferred_element_type=jnp.float32,
    )
    compact = jnp.concatenate([gram[8 * i : 8 * i + 8] for i in range(4)], axis=1)
    for peer in range(gram_ref.shape[0]):
        gram_ref[peer] = compact


def sum_kernel(in_ref, out_ref):
    total = in_ref[0]
    for peer in range(1, in_ref.shape[0]):
        total = total + in_ref[peer]
    for peer in range(out_ref.shape[0]):
        out_ref[peer] = total


def solve_kernel(entries, parts_ref, cells_ref, ortho_ref, upper_ref):
    total = parts_ref[0]
    for peer in range(1, parts_ref.shape[0]):
        total = total + parts_ref[peer]
    total = total / entries
    lane = lax.broadcasted_iota(jnp.int32, (32, 128), 1)
    line = lax.broadcasted_iota(jnp.int32, (32, 128), 0)
    wide = jnp.concatenate([roll_lanes(total, -32 * i) for i in range(4)], axis=0)
    work = jnp.where(lane < 32, wide, jnp.where(lane == line + 32, 1.0, 0.0))
    roots = jnp.zeros((32, 128), jnp.float32)
    for k in range(32):
        row = work[k : k + 1]
        pivot = row[:, k : k + 1]
        factor = jnp.where(line[:, :1] > k, work[:, k : k + 1] / pivot, 0.0)
        roots = jnp.where(line == k, jnp.broadcast_to(pivot, (32, 128)), roots)
        work = work - factor * row
    work = work / jnp.sqrt(roots)
    upper_ref[...] = jnp.where(lane >= line, work, 0.0)[:, :32]
    inverse = roll_lanes(work, -32)[:, :32]
    ortho = jnp.dot(
        inverse, cells_ref[...], precision=lax.Precision.HIGHEST, preferred_element_type=jnp.float32
    )
    level = level_of(jnp.max(jnp.abs(ortho), axis=1, keepdims=True))
    code = root_code(ortho, 1.0 / spacing(level))
    half = ortho.shape[1] // 2
    both = join(code[:, :half], code[:, half:])
    ortho_ref[:, 0, :half] = both
    ortho_ref[:, 0, half:] = jnp.broadcast_to(level, (32, 128))


def place_kernel(in_ref, out_ref):
    block = lane_group((8, 128), 16)
    line = lax.broadcasted_iota(jnp.int32, (8, 128), 0)
    distance = (block - line) % 8
    for part in range(4):
        sources = slice(8 * part, 8 * part + 8)
        scale = code_scale(in_ref[sources, 0, 1152:1280])
        for pair in range(9):
            both = in_ref[sources, 0, 128 * pair : 128 * pair + 128]
            for unit, code in zip((pair, pair + 9), halves(both)):
                field, tile = unit // 3, unit % 3
                value = from_root_code(code, scale)
                total = value
                for k in range(1, 8):
                    moved = roll_rows(roll_lanes(value, 16 * k), -k)
                    total = jnp.where(distance == k, moved, total)
                out_ref[field, 8 * tile : 8 * tile + 8, 128 * part : 128 * part + 128] = total


def call(kernel, out_shape, name, scratch=(), spaces=None, vmem=40):
    specs = {}
    if spaces:
        specs = dict(in_specs=[pl.BlockSpec(memory_space=space) for space in spaces])
    return pl.pallas_call(
        kernel,
        out_shape=out_shape,
        scratch_shapes=list(scratch),
        compiler_params=pltpu.CompilerParams(vmem_limit_bytes=vmem * 1024 * 1024),
        name=name,
        **specs,
    )


def f32(*shape):
    return jax.ShapeDtypeStruct(shape, jnp.float32)


VEC = ("z_hi", "y")
SPACE = ("x", "z_lo", "core")
LINE = ("z_hi", "z_lo", "core")
PLANE = ("x", "y")


def body(perturbation, trajectory, step_order):
    tiles = lax.axis_size(SPACE)
    first, second = lax.axis_size(LINE), lax.axis_size(PLANE)
    sent = call(
        pack_kernel,
        jax.ShapeDtypeStruct((32, 8 * QUADS, 128), jnp.int32),
        "pack",
        [
            pltpu.VMEM((6, ROWS, 512), jnp.float32),
            pltpu.VMEM((18, ROWS, 512), jnp.bfloat16),
            pltpu.VMEM((8 * PAIRS, 512), jnp.int32),
            pltpu.SemaphoreType.DMA((2,)),
        ],
        spaces=(pltpu.HBM, pltpu.HBM),
        vmem=60,
    )(perturbation[0], trajectory[0].reshape(18, ROWS, 512))
    held = lax.all_to_all(sent, VEC, split_axis=0, concat_axis=0, tiled=True)
    state, base, up, down = call(
        unpack_kernel,
        (f32(6, ROWS, 8, 128), f32(36, ROWS, 128), f32(HALO_ROWS, 128), f32(HALO_ROWS, 128)),
        "unpack",
        spaces=(pltpu.SMEM, pltpu.VMEM),
    )(step_order, held.reshape(32 * 8 * QUADS, 128))
    top = lax.ppermute(down, SPACE, [(i, (i + 1) % tiles) for i in range(tiles)])
    bottom = lax.ppermute(up, SPACE, [(i, (i - 1) % tiles) for i in range(tiles)])
    padded = pltpu.VMEM((6, PAD, 8, 128), jnp.float32)
    cells, gram = call(
        step_kernel,
        (f32(32, 2304), f32(first, 8, 128)),
        "steps",
        [padded, padded, padded, pltpu.VMEM((COEF, ROWS + 16, 128), jnp.float32)],
    )(state, base, top, bottom)
    gram = lax.all_to_all(gram, LINE, split_axis=0, concat_axis=0, tiled=True)
    gram = call(sum_kernel, f32(second, 8, 128), "sums")(gram)
    gram = lax.all_to_all(gram, PLANE, split_axis=0, concat_axis=0, tiled=True)
    entries = float(6 * ROWS * 512 * tiles)
    ortho, upper = call(
        lambda *refs: solve_kernel(entries, *refs), (jax.ShapeDtypeStruct((32, 1, 1280), jnp.int32), f32(32, 32)), "solve"
    )(gram, cells)
    ortho = lax.all_to_all(ortho, VEC, split_axis=0, concat_axis=0, tiled=True)
    placed = call(place_kernel, f32(6, ROWS, 512), "place")(ortho)
    return placed[None], upper


def solution(mesh):
    fine = jax.sharding.Mesh(mesh.devices.reshape(4, 8, 4, 2, 2), VEC + SPACE)
    in_specs = (P(VEC, None, SPACE, None), P(VEC, None, None, SPACE, None), P())
    out_specs = (P(VEC, None, SPACE, None), P())
    return jax.shard_map(body, mesh=fine, in_specs=in_specs, out_specs=out_specs, check_vma=False)
```

```python
import jax
import jax.numpy as jnp
from jax import lax
from jax.experimental import pallas as pl
from jax.experimental.pallas import tpu as pltpu
from jax.sharding import PartitionSpec as P

GRAVITY_TOP = 1.0
GRAVITY_LOW = 0.5
DEPTH = 1.0
CORIOLIS = 0.3
TIME_STEP = 0.25

ROWS = 24
HALO = 6
WINDOW = 28
PAD = ROWS + 2 * HALO
PERT_PAIRS = 9
PAIRS = 36
WHOLE = 32
SPLIT_FROM = 4
QUADS = WHOLE // 4
BASE_QUAD = PERT_PAIRS // 4
TOP_CODE = 32000.0
BASE_SCALE = 16384.0
STEP_ROWS = tuple(HALO - section for section in range(6))
BASE_HALO_ROWS = 6 * sum(STEP_ROWS)
STATE_HALO_ROWS = 6 * HALO * 8
HALO_ROWS = STATE_HALO_ROWS + BASE_HALO_ROWS + 2
COEF = 14


def roll_lanes(value, shift):
    shift %= value.shape[-1]
    return pltpu.roll(value, shift, 1) if shift else value


def roll_rows(value, shift):
    shift %= value.shape[0]
    return pltpu.roll(value, shift, 0) if shift else value


def lane_group(shape, size):
    return lax.broadcasted_iota(jnp.int32, shape, 1) // size


def quad_transposes(quads):
    group = lane_group((8, 128), 32)
    odd, upper = (group % 2) == 1, group >= 2
    moved = [(roll_lanes(b, 32), roll_lanes(a, -32), roll_lanes(d, 32), roll_lanes(c, -32)) for a, b, c, d in quads]
    quads = [
        (jnp.where(odd, p, a), jnp.where(odd, b, q), jnp.where(odd, r, c), jnp.where(odd, d, t))
        for (a, b, c, d), (p, q, r, t) in zip(quads, moved)
    ]
    moved = [tuple(roll_lanes(item, 64) for item in quad) for quad in quads]
    return [
        (jnp.where(upper, r, a), jnp.where(upper, t, b), jnp.where(upper, c, p), jnp.where(upper, d, q))
        for (a, b, c, d), (p, q, r, t) in zip(quads, moved)
    ]


def join(first, second):
    return (first & 0xFFFF) | (second << 16)


def halves(value):
    return (value << 16) >> 16, value >> 16


def to_code(value):
    return jnp.round(value).astype(jnp.int32)


def level_of(largest):
    return jnp.ceil(8.0 * jnp.log2(jnp.maximum(largest, 1e-30))).astype(jnp.int32)


def spacing(level):
    return jnp.exp2(level.astype(jnp.float32) * 0.125)


def root_code(value, inverse):
    size = jnp.minimum(TOP_CODE * jnp.sqrt(jnp.abs(value) * inverse), 32767.0)
    return to_code(jnp.where(value < 0, -size, size))


def from_root_code(code, scale):
    code = code.astype(jnp.float32)
    return code * jnp.abs(code) * scale


def code_scale(level):
    return spacing(level) * (1.0 / (TOP_CODE * TOP_CODE))


def pack_kernel(pert_hbm, traj_hbm, out_ref, pert_ref, traj_ref, pair_ref, split_ref, sems):
    copies = [
        pltpu.make_async_copy(pert_hbm, pert_ref, sems.at[0]),
        pltpu.make_async_copy(traj_hbm, traj_ref, sems.at[1]),
    ]
    for copy in copies:
        copy.start()
    copies[0].wait()
    largest = jnp.abs(pert_ref[0, 0:8])
    for field in range(6):
        for tile in range(3):
            largest = jnp.maximum(largest, jnp.abs(pert_ref[field, 8 * tile : 8 * tile + 8]))
    level = level_of(jnp.max(largest, axis=(0, 1), keepdims=True))
    inverse = jnp.broadcast_to(1.0 / spacing(level), (8, 512))
    level = jnp.broadcast_to(level, (8, 128))

    for pair in range(PERT_PAIRS):
        field, tile = pair // 3, pair % 3
        first = root_code(pert_ref[field, 8 * tile : 8 * tile + 8], inverse)
        second = root_code(pert_ref[field + 3, 8 * tile : 8 * tile + 8], inverse)
        pair_ref[8 * pair : 8 * pair + 8] = join(first, second)
    copies[1].wait()
    for section in range(3):
        for field in range(3):
            value = [
                to_code(traj_ref[6 * section + i].astype(jnp.float32) * BASE_SCALE)
                for i in (field, field + 3)
            ]
            both = join(*value)
            for tile in range(3):
                pair = PERT_PAIRS + 9 * tile + 3 * section + field
                pair_ref[8 * pair : 8 * pair + 8] = both[8 * tile : 8 * tile + 8]
    spare = lax.broadcasted_iota(jnp.int32, (8, 128), 1) % 32 >= WINDOW
    for parity in range(2):
        split_ref[parity] = roll_lanes(pair_ref[8 * WHOLE :], 6 - 16 * parity)
    for begin in range(0, QUADS, 2):
        places, quads = [], []
        for quad in range(begin, begin + 2):
            raw = [pair_ref[8 * pair : 8 * pair + 8] for pair in range(4 * quad, 4 * quad + 4)]
            for parity in range(2):
                items = [roll_lanes(item, 6 - 16 * parity) for item in raw]
                for part in range(4):
                    columns = slice(128 * part, 128 * part + 128)
                    four = [item[:, columns] for item in items]
                    for i in range(4):
                        piece = 4 * quad + i - SPLIT_FROM
                        if piece >= 0:
                            moved = split_ref[parity, 8 * (piece // 7) : 8 * (piece // 7) + 8, columns]
                            moved = roll_lanes(moved, WINDOW - 4 * (piece % 7))
                            four[i] = jnp.where(spare, moved, four[i])
                        elif piece == -SPLIT_FROM:
                            four[i] = jnp.where(spare, level, four[i])
                    places.append((8 * part + parity, 8 * quad))
                    quads.append(four)
        for (target, at), four in zip(places, quad_transposes(quads)):
            for position, item in enumerate(four):
                out_ref[target + 2 * position, at : at + 8] = item


def odd_tile():
    return lax.axis_index("core") == 1


def unpack_kernel(order_ref, in_ref, state_ref, base_ref, far_ref, near_ref, up_ref, down_ref):
    column = lax.broadcasted_iota(jnp.int32, (8, 128), 1) % 32
    scale = None
    for quad in range(BASE_QUAD + 1):
        rows = [
            [
                in_ref[pl.ds(8 * QUADS * 8 * i + 8 * quad + row, 8, stride=8 * QUADS), :]
                for i in range(4)
            ]
            for row in range(8)
        ]
        for row, four in enumerate(quad_transposes(rows)):
            for pair, both in enumerate(four, 4 * quad):
                if pair >= PERT_PAIRS:
                    continue
                first, second = halves(both)
                if scale is None:
                    level = roll_lanes(jnp.where(column == WINDOW, first, 0), -WINDOW)
                    for shift in (1, 2, 4, 8, 16):
                        level = level + roll_lanes(level, shift)
                    scale = code_scale(level)
                for layer, item in enumerate((first, second)):
                    item = from_root_code(item, scale)
                    field, line = pair // 3 + 3 * layer, 8 * (pair % 3) + row
                    state_ref[field, line] = item
                    if line < HALO:
                        up_ref[pl.ds(8 * (HALO * field + line), 8)] = item
                    if line >= ROWS - HALO:
                        down_ref[pl.ds(8 * (HALO * field + line - ROWS + HALO), 8)] = item
    source = lax.broadcasted_iota(jnp.int32, (128, 512), 0)
    target = lax.broadcasted_iota(jnp.int32, (128, 512), 1)
    spread = ((source % 32 == target % 32) & (source // 32 == target // 128)).astype(jnp.float32)
    spread = spread.astype(jnp.bfloat16)
    lane = lax.broadcasted_iota(jnp.int32, (8, 128), 1)
    for step in range(2):
        block = in_ref[pl.ds(pl.multiple_of(order_ref[step] * (8 * QUADS), 8), 8 * QUADS), :]
        pieces = jnp.zeros((8, 128), jnp.int32)
        for piece in range(WHOLE - SPLIT_FROM):
            source = piece + SPLIT_FROM
            to = 32 * (piece // 7) + 4 * (piece % 7)
            moved = block[8 * (source // 4) : 8 * (source // 4) + 8]
            moved = roll_lanes(moved, to - 32 * (source % 4) - WINDOW)
            pieces = jnp.where((lane >= to) & (lane < to + 4), moved, pieces)
        block = jnp.concatenate([block[8 * BASE_QUAD :], pieces], axis=0)
        for layer, part in enumerate(halves(block)):
            part = part.astype(jnp.float32).astype(jnp.bfloat16)
            wide = jnp.dot(part, spread, preferred_element_type=jnp.float32) * (1.0 / BASE_SCALE)
            for unit in range(27):
                tile, field = unit // 9, 6 * (unit % 9 // 3) + unit % 3 + 3 * layer
                at = PERT_PAIRS + unit - 4 * BASE_QUAD
                item = wide[8 * (at // 4) : 8 * (at // 4) + 8, 128 * (at % 4) : 128 * (at % 4) + 128]
                base_ref[18 * step + field, 8 * tile : 8 * tile + 8] = item
    place = STATE_HALO_ROWS
    for index in range(36):
        width = STEP_ROWS[index // 6]
        up_ref[place : place + width] = base_ref[index, 0:width]
        down_ref[place : place + width] = base_ref[index, ROWS - width : ROWS]
        place += width
    up_ref[place : place + 2] = jnp.zeros((2, 128), jnp.float32)
    down_ref[place : place + 2] = jnp.zeros((2, 128), jnp.float32)
    odd = odd_tile()

    @pl.when(odd)
    def _():
        far_ref[...] = down_ref[...]
        near_ref[...] = up_ref[...]

    @pl.when(jnp.logical_not(odd))
    def _():
        far_ref[...] = up_ref[...]
        near_ref[...] = down_ref[...]


def coefficients(fields, scale):
    results = []
    dx = lambda f: roll_rows(f, -1) - roll_rows(f, 1)
    dy = lambda f: roll_lanes(f, -1) - roll_lanes(f, 1)
    for layer in range(2):
        depth, xvel, yvel = fields[3 * layer : 3 * layer + 3]
        results += [
            scale * (depth + DEPTH),
            scale * xvel,
            scale * yvel,
            scale * dx(xvel),
            scale * dy(xvel) - TIME_STEP * CORIOLIS,
            scale * dx(yvel) + TIME_STEP * CORIOLIS,
            scale * dy(yvel),
        ]
    return results


def section_rows(cur_ref, anchor_ref, new_ref, coef, section):
    scale = 0.5 * TIME_STEP
    kind = section % 3

    def dy(value):
        return roll_lanes(value, -1) - roll_lanes(value, 1)

    def block(row, count):
        span = range(-1, count + 1)
        h = [[cur_ref[3 * layer, row + i] for i in span] for layer in range(2)]
        top = [(scale * GRAVITY_TOP) * (h[0][i] + h[1][i]) for i in range(count + 2)]
        low = [top[i] + (scale * GRAVITY_LOW) * h[1][i] for i in range(count + 2)]
        for layer, pressure in enumerate((top, low)):
            at = COEF // 2 * layer
            u = [cur_ref[3 * layer + 1, row + i] for i in span]
            v = [cur_ref[3 * layer + 2, row + i] for i in span]
            depth = [coef(at, row + i) for i in span]
            xvel = [coef(at + 1, row + i) for i in span]
            flux = [depth[i] * u[i] + h[layer][i] * xvel[i] for i in range(count + 2)]
            for i in range(1, count + 1):
                line = row + i - 1
                h_i, u_i, v_i = h[layer][i], u[i], v[i]
                yvel, xvel_dx, xvel_dy, yvel_dx, yvel_dy = [coef(at + k, line) for k in range(2, 7)]
                h_new = h_i - (flux[i + 1] - flux[i - 1]) - dy(depth[i] * v_i + h_i * yvel)
                u_new = u_i - (
                    xvel[i] * (u[i + 1] - u[i - 1])
                    + u_i * xvel_dx
                    + yvel * dy(u_i)
                    + v_i * xvel_dy
                    + (pressure[i + 1] - pressure[i - 1])
                )
                v_new = v_i - (
                    xvel[i] * (v[i + 1] - v[i - 1])
                    + u_i * yvel_dx
                    + yvel * dy(v_i)
                    + v_i * yvel_dy
                    + dy(pressure[i])
                )
                for field, value in enumerate((h_new, u_new, v_new)):
                    field += 3 * layer
                    if kind == 1:
                        value = 0.75 * anchor_ref[field, line] + 0.25 * value
                    if kind == 2:
                        value = (1.0 / 3.0) * anchor_ref[field, line] + (2.0 / 3.0) * value
                    new_ref[field, line] = value

    block(section + 1, PAD - 2 - 2 * section)


def step_kernel(
    state_ref, base_ref, far_ref, near_ref, cells_ref, gram_ref, start_ref, one_ref, two_ref, coef_ref, sides_ref
):
    odd = odd_tile()
    top_ref, bottom_ref = sides_ref.at[0], sides_ref.at[1]

    @pl.when(odd)
    def _():
        top_ref[...] = near_ref[...]
        bottom_ref[...] = far_ref[...]

    @pl.when(jnp.logical_not(odd))
    def _():
        top_ref[...] = far_ref[...]
        bottom_ref[...] = near_ref[...]

    for field in range(6):
        start_ref[field, HALO : HALO + ROWS] = state_ref[field]
        for line in range(HALO):
            at = 8 * (HALO * field + line)
            start_ref[field, line] = top_ref[at : at + 8]
            start_ref[field, HALO + ROWS + line] = bottom_ref[at : at + 8]
    place = STATE_HALO_ROWS
    buffers = (start_ref, one_ref, two_ref, start_ref)
    for section in range(6):
        width = STEP_ROWS[section]
        fields = []
        for field in range(6):
            pieces = [
                top_ref[place : place + width],
                base_ref[6 * section + field],
                bottom_ref[place : place + width],
            ]
            if width < 8:
                pieces.append(jnp.zeros((16 - 2 * width, 128), jnp.float32))
            fields.append(jnp.concatenate(pieces, axis=0))
            place += width
        for index, value in enumerate(coefficients(fields, 0.5 * TIME_STEP)):
            coef_ref[index] = value

        def coef(index, row):
            return coef_ref[index, pl.ds(row - HALO + width, 8, stride=0), :]

        kind = section % 3
        section_rows(buffers[kind], start_ref, buffers[kind + 1], coef, section)
    block = lane_group((8, 128), 16)
    for unit in range(18):
        field, tile = unit // 3, unit % 3
        lines = [start_ref[field, HALO + 8 * tile + row] for row in range(8)]
        for quarter in range(4):
            total = None
            for row in range(8):
                moved = roll_lanes(lines[row], 16 * row - 32 * quarter - HALO)
                total = moved if total is None else jnp.where(block == row, moved, total)
            cells_ref[8 * quarter : 8 * quarter + 8, 128 * unit : 128 * unit + 128] = total
    cells = cells_ref[...]
    gram = lax.dot_general(
        cells,
        cells,
        (((1,), (1,)), ((), ())),
        precision=lax.Precision.HIGHEST,
        preferred_element_type=jnp.float32,
    )
    compact = jnp.concatenate([gram[8 * i : 8 * i + 8] for i in range(4)], axis=1)
    for peer in range(gram_ref.shape[0]):
        gram_ref[peer] = compact


def sum_kernel(in_ref, out_ref):
    total = in_ref[0]
    for peer in range(1, in_ref.shape[0]):
        total = total + in_ref[peer]
    for peer in range(out_ref.shape[0]):
        out_ref[peer] = total


def solve_kernel(entries, parts_ref, cells_ref, ortho_ref, upper_ref):
    total = parts_ref[0]
    for peer in range(1, parts_ref.shape[0]):
        total = total + parts_ref[peer]
    total = total / entries
    lane = lax.broadcasted_iota(jnp.int32, (32, 128), 1)
    line = lax.broadcasted_iota(jnp.int32, (32, 128), 0)
    wide = jnp.concatenate([roll_lanes(total, -32 * i) for i in range(4)], axis=0)
    work = jnp.where(lane < 32, wide, jnp.where(lane == line + 32, 1.0, 0.0))
    roots = jnp.zeros((32, 128), jnp.float32)
    for begin in range(0, 32, 8):
        columns = [jnp.broadcast_to(work[:, k : k + 1], (32, 128)) for k in range(begin, begin + 8)]
        rows = [work[k : k + 1] for k in range(begin, begin + 8)]
        factors = []
        for j in range(8):
            k = begin + j
            pivot = columns[j][k : k + 1]
            roots = jnp.where(line == k, pivot, roots)
            factor = jnp.where(line > k, columns[j] * (1.0 / pivot), 0.0)
            factors.append(factor)
            for i in range(j + 1, 8):
                columns[i] = columns[i] - factor * columns[i][k : k + 1]
                rows[i] = rows[i] - factor[begin + i : begin + i + 1] * rows[j]
        for factor, row in zip(factors, rows):
            work = work - factor * row
    work = work / jnp.sqrt(roots)
    upper_ref[...] = jnp.where(lane >= line, work, 0.0)[:, :32]
    inverse = roll_lanes(work, -32)[:, :32]
    ortho = jnp.dot(
        inverse, cells_ref[...], precision=lax.Precision.HIGHEST, preferred_element_type=jnp.float32
    )
    level = level_of(jnp.max(jnp.abs(ortho), axis=1, keepdims=True))
    code = root_code(ortho, 1.0 / spacing(level))
    half = ortho.shape[1] // 2
    both = join(code[:, :half], code[:, half:])
    ortho_ref[:, 0, :half] = both
    ortho_ref[:, 0, half:] = jnp.broadcast_to(level, (32, 128))


def place_kernel(in_ref, out_ref):
    block = lane_group((8, 128), 16)
    line = lax.broadcasted_iota(jnp.int32, (8, 128), 0)
    distance = (block - line) % 8
    for part in range(4):
        sources = slice(8 * part, 8 * part + 8)
        scale = code_scale(in_ref[sources, 0, 1152:1280])
        for pair in range(9):
            both = in_ref[sources, 0, 128 * pair : 128 * pair + 128]
            for unit, code in zip((pair, pair + 9), halves(both)):
                field, tile = unit // 3, unit % 3
                value = from_root_code(code, scale)
                total = value
                for k in range(1, 8):
                    moved = roll_rows(roll_lanes(value, 16 * k), -k)
                    total = jnp.where(distance == k, moved, total)
                out_ref[field, 8 * tile : 8 * tile + 8, 128 * part : 128 * part + 128] = total


def call(kernel, out_shape, name, scratch=(), spaces=None, vmem=40):
    specs = {}
    if spaces:
        specs = dict(in_specs=[pl.BlockSpec(memory_space=space) for space in spaces])
    return pl.pallas_call(
        kernel,
        out_shape=out_shape,
        scratch_shapes=list(scratch),
        compiler_params=pltpu.CompilerParams(vmem_limit_bytes=vmem * 1024 * 1024),
        name=name,
        **specs,
    )


def f32(*shape):
    return jax.ShapeDtypeStruct(shape, jnp.float32)


VEC = ("z_hi", "y")
SPACE = ("x", "z_lo", "core")
LINE = ("z_hi", "z_lo", "core")
PLANE = ("x", "y")


def body(perturbation, trajectory, step_order):
    tiles = lax.axis_size(SPACE)
    first, second = lax.axis_size(LINE), lax.axis_size(PLANE)
    sent = call(
        pack_kernel,
        jax.ShapeDtypeStruct((32, 8 * QUADS, 128), jnp.int32),
        "pack",
        [
            pltpu.VMEM((6, ROWS, 512), jnp.float32),
            pltpu.VMEM((18, ROWS, 512), jnp.bfloat16),
            pltpu.VMEM((8 * PAIRS, 512), jnp.int32),
            pltpu.VMEM((2, 8 * (PAIRS - WHOLE), 512), jnp.int32),
            pltpu.SemaphoreType.DMA((2,)),
        ],
        spaces=(pltpu.HBM, pltpu.HBM),
        vmem=60,
    )(perturbation[0], trajectory[0].reshape(18, ROWS, 512))
    held = lax.all_to_all(sent, VEC, split_axis=0, concat_axis=0, tiled=True)
    state, base, far, near = call(
        unpack_kernel,
        (f32(6, ROWS, 8, 128), f32(36, ROWS, 128), f32(HALO_ROWS, 128), f32(HALO_ROWS, 128)),
        "unpack",
        [pltpu.VMEM((HALO_ROWS, 128), jnp.float32)] * 2,
        spaces=(pltpu.SMEM, pltpu.VMEM),
    )(step_order, held.reshape(32 * 8 * QUADS, 128))
    far = lax.ppermute(far, SPACE, [(i, (i + 1 if i % 2 else i - 1) % tiles) for i in range(tiles)])
    near = lax.ppermute(near, SPACE, [(i, i ^ 1) for i in range(tiles)])
    padded = pltpu.VMEM((6, PAD, 8, 128), jnp.float32)
    cells, gram = call(
        step_kernel,
        (f32(32, 2304), f32(first, 8, 128)),
        "steps",
        [
            padded,
            padded,
            padded,
            pltpu.VMEM((COEF, ROWS + 16, 128), jnp.float32),
            pltpu.VMEM((2, HALO_ROWS, 128), jnp.float32),
        ],
    )(state, base, far, near)
    gram = lax.all_to_all(gram, LINE, split_axis=0, concat_axis=0, tiled=True)
    gram = call(sum_kernel, f32(second, 8, 128), "sums")(gram)
    gram = lax.all_to_all(gram, PLANE, split_axis=0, concat_axis=0, tiled=True)
    entries = float(6 * ROWS * 512 * tiles)
    ortho, upper = call(
        lambda *refs: solve_kernel(entries, *refs), (jax.ShapeDtypeStruct((32, 1, 1280), jnp.int32), f32(32, 32)), "solve"
    )(gram, cells)
    ortho = lax.all_to_all(ortho, VEC, split_axis=0, concat_axis=0, tiled=True)
    placed = call(place_kernel, f32(6, ROWS, 512), "place")(ortho)
    return placed[None], upper


def solution(mesh):
    fine = jax.sharding.Mesh(mesh.devices.reshape(4, 8, 4, 2, 2), VEC + SPACE)
    in_specs = (P(VEC, None, SPACE, None), P(VEC, None, None, SPACE, None), P())
    out_specs = (P(VEC, None, SPACE, None), P())
    return jax.shard_map(body, mesh=fine, in_specs=in_specs, out_specs=out_specs, check_vma=False)
```

```python
import jax
import jax.numpy as jnp
from jax import lax
from jax.experimental import pallas as pl
from jax.experimental.pallas import tpu as pltpu
from jax.sharding import PartitionSpec as P

GRAVITY_TOP = 1.0
GRAVITY_LOW = 0.5
DEPTH = 1.0
CORIOLIS = 0.3
TIME_STEP = 0.25

ROWS = 24
HALO = 6
WINDOW = 28
PAD = ROWS + 2 * HALO
PERT_PAIRS = 9
PAIRS = 36
WHOLE = 32
SPLIT_FROM = 4
QUADS = WHOLE // 4
BASE_QUAD = PERT_PAIRS // 4
TOP_CODE = 32000.0
BASE_SCALE = 16384.0
STEP_ROWS = tuple(HALO - section for section in range(6))
BASE_HALO_ROWS = 6 * sum(STEP_ROWS)
STATE_HALO_ROWS = 6 * HALO * 8
HALO_ROWS = STATE_HALO_ROWS + BASE_HALO_ROWS + 2
COEF = 14


def roll_lanes(value, shift):
    shift %= value.shape[-1]
    return pltpu.roll(value, shift, 1) if shift else value


def roll_rows(value, shift):
    shift %= value.shape[0]
    return pltpu.roll(value, shift, 0) if shift else value


def lane_group(shape, size):
    return lax.broadcasted_iota(jnp.int32, shape, 1) // size


def quad_transposes(quads):
    group = lane_group((8, 128), 32)
    odd, upper = (group % 2) == 1, group >= 2
    moved = [(roll_lanes(b, 32), roll_lanes(a, -32), roll_lanes(d, 32), roll_lanes(c, -32)) for a, b, c, d in quads]
    quads = [
        (jnp.where(odd, p, a), jnp.where(odd, b, q), jnp.where(odd, r, c), jnp.where(odd, d, t))
        for (a, b, c, d), (p, q, r, t) in zip(quads, moved)
    ]
    moved = [tuple(roll_lanes(item, 64) for item in quad) for quad in quads]
    return [
        (jnp.where(upper, r, a), jnp.where(upper, t, b), jnp.where(upper, c, p), jnp.where(upper, d, q))
        for (a, b, c, d), (p, q, r, t) in zip(quads, moved)
    ]


def join(first, second):
    return (first & 0xFFFF) | (second << 16)


def halves(value):
    return (value << 16) >> 16, value >> 16


def to_code(value):
    return jnp.round(value).astype(jnp.int32)


def level_of(largest):
    return jnp.ceil(8.0 * jnp.log2(jnp.maximum(largest, 1e-30))).astype(jnp.int32)


def spacing(level):
    return jnp.exp2(level.astype(jnp.float32) * 0.125)


def root_code(value, inverse):
    size = jnp.minimum(TOP_CODE * jnp.sqrt(jnp.abs(value) * inverse), 32767.0)
    return to_code(jnp.where(value < 0, -size, size))


def from_root_code(code, scale):
    code = code.astype(jnp.float32)
    return code * jnp.abs(code) * scale


def code_scale(level):
    return spacing(level) * (1.0 / (TOP_CODE * TOP_CODE))


def pack_kernel(pert_hbm, traj_hbm, out_ref, pert_ref, traj_ref, pair_ref, split_ref, sems):
    copies = [
        pltpu.make_async_copy(pert_hbm, pert_ref, sems.at[0]),
        pltpu.make_async_copy(traj_hbm, traj_ref, sems.at[1]),
    ]
    for copy in copies:
        copy.start()
    copies[0].wait()
    largest = jnp.abs(pert_ref[0, 0:8])
    for field in range(6):
        for tile in range(3):
            largest = jnp.maximum(largest, jnp.abs(pert_ref[field, 8 * tile : 8 * tile + 8]))
    level = level_of(jnp.max(largest, axis=(0, 1), keepdims=True))
    inverse = jnp.broadcast_to(1.0 / spacing(level), (8, 512))
    level = jnp.broadcast_to(level, (8, 128))

    for pair in range(PERT_PAIRS):
        field, tile = pair // 3, pair % 3
        first = root_code(pert_ref[field, 8 * tile : 8 * tile + 8], inverse)
        second = root_code(pert_ref[field + 3, 8 * tile : 8 * tile + 8], inverse)
        pair_ref[8 * pair : 8 * pair + 8] = join(first, second)
    copies[1].wait()
    for section in range(3):
        for field in range(3):
            value = [
                to_code(traj_ref[6 * section + i].astype(jnp.float32) * BASE_SCALE)
                for i in (field, field + 3)
            ]
            both = join(*value)
            for tile in range(3):
                pair = PERT_PAIRS + 9 * tile + 3 * section + field
                pair_ref[8 * pair : 8 * pair + 8] = both[8 * tile : 8 * tile + 8]
    spare = lax.broadcasted_iota(jnp.int32, (8, 128), 1) % 32 >= WINDOW
    for parity in range(2):
        split_ref[parity] = roll_lanes(pair_ref[8 * WHOLE :], 6 - 16 * parity)
    for begin in range(0, QUADS, 2):
        places, quads = [], []
        for quad in range(begin, begin + 2):
            raw = [pair_ref[8 * pair : 8 * pair + 8] for pair in range(4 * quad, 4 * quad + 4)]
            for parity in range(2):
                items = [roll_lanes(item, 6 - 16 * parity) for item in raw]
                for part in range(4):
                    columns = slice(128 * part, 128 * part + 128)
                    four = [item[:, columns] for item in items]
                    for i in range(4):
                        piece = 4 * quad + i - SPLIT_FROM
                        if piece >= 0:
                            moved = split_ref[parity, 8 * (piece // 7) : 8 * (piece // 7) + 8, columns]
                            moved = roll_lanes(moved, WINDOW - 4 * (piece % 7))
                            four[i] = jnp.where(spare, moved, four[i])
                        elif piece == -SPLIT_FROM:
                            four[i] = jnp.where(spare, level, four[i])
                    places.append((8 * part + parity, 8 * quad))
                    quads.append(four)
        for (target, at), four in zip(places, quad_transposes(quads)):
            for position, item in enumerate(four):
                out_ref[target + 2 * position, at : at + 8] = item


def odd_tile():
    return lax.axis_index("core") == 1


def unpack_kernel(order_ref, in_ref, state_ref, base_ref, far_ref, near_ref, up_ref, down_ref):
    column = lax.broadcasted_iota(jnp.int32, (8, 128), 1) % 32
    scale = None
    for quad in range(BASE_QUAD + 1):
        rows = [
            [
                in_ref[pl.ds(8 * QUADS * 8 * i + 8 * quad + row, 8, stride=8 * QUADS), :]
                for i in range(4)
            ]
            for row in range(8)
        ]
        for row, four in enumerate(quad_transposes(rows)):
            for pair, both in enumerate(four, 4 * quad):
                if pair >= PERT_PAIRS:
                    continue
                first, second = halves(both)
                if scale is None:
                    level = roll_lanes(jnp.where(column == WINDOW, first, 0), -WINDOW)
                    for shift in (1, 2, 4, 8, 16):
                        level = level + roll_lanes(level, shift)
                    scale = code_scale(level)
                for layer, item in enumerate((first, second)):
                    item = from_root_code(item, scale)
                    field, line = pair // 3 + 3 * layer, 8 * (pair % 3) + row
                    state_ref[field, line] = item
                    if line < HALO:
                        up_ref[pl.ds(8 * (HALO * field + line), 8)] = item
                    if line >= ROWS - HALO:
                        down_ref[pl.ds(8 * (HALO * field + line - ROWS + HALO), 8)] = item
    source = lax.broadcasted_iota(jnp.int32, (128, 512), 0)
    target = lax.broadcasted_iota(jnp.int32, (128, 512), 1)
    spread = ((source % 32 == target % 32) & (source // 32 == target // 128)).astype(jnp.float32)
    spread = spread.astype(jnp.bfloat16)
    lane = lax.broadcasted_iota(jnp.int32, (8, 128), 1)
    for step in range(2):
        block = in_ref[pl.ds(pl.multiple_of(order_ref[step] * (8 * QUADS), 8), 8 * QUADS), :]
        pieces = jnp.zeros((8, 128), jnp.int32)
        for piece in range(WHOLE - SPLIT_FROM):
            source = piece + SPLIT_FROM
            to = 32 * (piece // 7) + 4 * (piece % 7)
            moved = block[8 * (source // 4) : 8 * (source // 4) + 8]
            moved = roll_lanes(moved, to - 32 * (source % 4) - WINDOW)
            pieces = jnp.where((lane >= to) & (lane < to + 4), moved, pieces)
        block = jnp.concatenate([block[8 * BASE_QUAD :], pieces], axis=0)
        for layer, part in enumerate(halves(block)):
            part = part.astype(jnp.float32).astype(jnp.bfloat16)
            wide = jnp.dot(part, spread, preferred_element_type=jnp.float32) * (1.0 / BASE_SCALE)
            for unit in range(27):
                tile, field = unit // 9, 6 * (unit % 9 // 3) + unit % 3 + 3 * layer
                at = PERT_PAIRS + unit - 4 * BASE_QUAD
                item = wide[8 * (at // 4) : 8 * (at // 4) + 8, 128 * (at % 4) : 128 * (at % 4) + 128]
                base_ref[18 * step + field, 8 * tile : 8 * tile + 8] = item
    place = STATE_HALO_ROWS
    for index in range(36):
        width = STEP_ROWS[index // 6]
        up_ref[place : place + width] = base_ref[index, 0:width]
        down_ref[place : place + width] = base_ref[index, ROWS - width : ROWS]
        place += width
    up_ref[place : place + 2] = jnp.zeros((2, 128), jnp.float32)
    down_ref[place : place + 2] = jnp.zeros((2, 128), jnp.float32)
    odd = odd_tile()

    @pl.when(odd)
    def _():
        far_ref[...] = down_ref[...]
        near_ref[...] = up_ref[...]

    @pl.when(jnp.logical_not(odd))
    def _():
        far_ref[...] = up_ref[...]
        near_ref[...] = down_ref[...]


def coefficients(fields, scale):
    results = []
    dx = lambda f: roll_rows(f, -1) - roll_rows(f, 1)
    dy = lambda f: roll_lanes(f, -1) - roll_lanes(f, 1)
    for layer in range(2):
        depth, xvel, yvel = fields[3 * layer : 3 * layer + 3]
        results += [
            scale * (depth + DEPTH),
            scale * xvel,
            scale * yvel,
            scale * dx(xvel),
            scale * dy(xvel) - TIME_STEP * CORIOLIS,
            scale * dx(yvel) + TIME_STEP * CORIOLIS,
            scale * dy(yvel),
        ]
    return results


def section_rows(cur, anchor, put, coef, kind, row, count):
    scale = 0.5 * TIME_STEP

    def dy(value):
        return roll_lanes(value, -1) - roll_lanes(value, 1)

    span = range(row - 1, row + count + 1)
    h = [[cur(3 * layer, i) for i in span] for layer in range(2)]
    top = [(scale * GRAVITY_TOP) * (h[0][i] + h[1][i]) for i in range(count + 2)]
    low = [top[i] + (scale * GRAVITY_LOW) * h[1][i] for i in range(count + 2)]
    for layer, pressure in enumerate((top, low)):
        at = COEF // 2 * layer
        u = [cur(3 * layer + 1, i) for i in span]
        v = [cur(3 * layer + 2, i) for i in span]
        depth = [coef(at, i) for i in span]
        xvel = [coef(at + 1, i) for i in span]
        flux = [depth[i] * u[i] + h[layer][i] * xvel[i] for i in range(count + 2)]
        for i in range(1, count + 1):
            line = row + i - 1
            h_i, u_i, v_i = h[layer][i], u[i], v[i]
            yvel, xvel_dx, xvel_dy, yvel_dx, yvel_dy = [coef(at + k, line) for k in range(2, 7)]
            h_new = h_i - (flux[i + 1] - flux[i - 1]) - dy(depth[i] * v_i + h_i * yvel)
            u_new = u_i - (
                xvel[i] * (u[i + 1] - u[i - 1])
                + u_i * xvel_dx
                + yvel * dy(u_i)
                + v_i * xvel_dy
                + (pressure[i + 1] - pressure[i - 1])
            )
            v_new = v_i - (
                xvel[i] * (v[i + 1] - v[i - 1])
                + u_i * yvel_dx
                + yvel * dy(v_i)
                + v_i * yvel_dy
                + dy(pressure[i])
            )
            for field, value in enumerate((h_new, u_new, v_new)):
                field += 3 * layer
                if kind == 1:
                    value = 0.75 * anchor(field, line) + 0.25 * value
                if kind == 2:
                    value = (1.0 / 3.0) * anchor(field, line) + (2.0 / 3.0) * value
                put(field, line, value)


def own_cells(lines):
    block = lane_group((8, 128), 16)
    results = []
    for quarter in range(4):
        total = None
        for row in range(8):
            moved = roll_lanes(lines[row], 16 * row - 32 * quarter - HALO)
            total = moved if total is None else jnp.where(block == row, moved, total)
        results.append(total)
    return results


def inside(section, row):
    return section < row < ROWS - 1 - section


def inner_kernel(state_ref, base_ref, kept_ref, middle_ref, coef_ref):
    for section in range(6):
        fields = [base_ref[6 * section + field] for field in range(6)]
        for index, value in enumerate(coefficients(fields, 0.5 * TIME_STEP)):
            coef_ref[section % 2, index] = value
        source = state_ref if section == 0 else kept_ref.at[section - 1]
        anchor = state_ref if section < 3 else kept_ref.at[2]

        def put(field, row, value):
            kept_ref[section, field, row] = value

        section_rows(
            lambda field, row: source[field, row],
            lambda field, row: anchor[field, row],
            put,
            lambda index, row: coef_ref[section % 2, index, pl.ds(row, 8, stride=0), :],
            section % 3,
            section + 1,
            ROWS - 2 - 2 * section,
        )
    for field in range(6):
        cells = own_cells([kept_ref[5, field, 8 + row] for row in range(8)])
        for quarter, item in enumerate(cells):
            middle_ref[8 * quarter : 8 * quarter + 8, 128 * field : 128 * field + 128] = item


def outer_kernel(
    state_ref, base_ref, far_ref, near_ref, kept_ref, middle_ref, cells_ref, gram_ref, edge_ref, coef_ref, sides_ref
):
    odd = odd_tile()
    top_ref, bottom_ref = sides_ref.at[0], sides_ref.at[1]

    @pl.when(odd)
    def _():
        top_ref[...] = near_ref[...]
        bottom_ref[...] = far_ref[...]

    @pl.when(jnp.logical_not(odd))
    def _():
        top_ref[...] = far_ref[...]
        bottom_ref[...] = near_ref[...]

    def slot(row):
        return row + HALO if row < ROWS // 2 else row - HALO

    def after(section):
        def read(field, row):
            if section < 0:
                if row < 0:
                    return top_ref[pl.ds(8 * (HALO * field + row + HALO), 8)]
                if row >= ROWS:
                    return bottom_ref[pl.ds(8 * (HALO * field + row - ROWS), 8)]
                return state_ref[field, row]
            if inside(section, row):
                return kept_ref[section, field, row]
            return edge_ref[section, field, slot(row)]

        return read

    place = STATE_HALO_ROWS
    for section in range(6):
        width = STEP_ROWS[section]
        fields = []
        for field in range(6):
            pieces = [
                top_ref[place : place + width],
                base_ref[6 * section + field],
                bottom_ref[place : place + width],
                jnp.zeros((16 - 2 * width, 128), jnp.float32),
            ]
            fields.append(jnp.concatenate(pieces, axis=0))
            place += width
        for index, value in enumerate(coefficients(fields, 0.5 * TIME_STEP)):
            coef_ref[section % 2, index] = value

        def put(field, row, value):
            edge_ref[section, field, slot(row)] = value

        for begin in (section + 1 - HALO, ROWS - 1 - section):
            section_rows(
                after(section - 1),
                after(-1 if section < 3 else 2),
                put,
                lambda index, row: coef_ref[section % 2, index, pl.ds(row + width, 8, stride=0), :],
                section % 3,
                begin,
                HALO,
            )
    last = after(5)
    for unit in range(18):
        field, tile = unit // 3, unit % 3
        columns = slice(128 * unit, 128 * unit + 128)
        if tile == 1:
            cells_ref[:, columns] = middle_ref[:, 128 * field : 128 * field + 128]
            continue
        cells = own_cells([last(field, 8 * tile + row) for row in range(8)])
        for quarter, item in enumerate(cells):
            cells_ref[8 * quarter : 8 * quarter + 8, columns] = item
    cells = cells_ref[...]
    gram = lax.dot_general(
        cells,
        cells,
        (((1,), (1,)), ((), ())),
        precision=lax.Precision.HIGHEST,
        preferred_element_type=jnp.float32,
    )
    compact = jnp.concatenate([gram[8 * i : 8 * i + 8] for i in range(4)], axis=1)
    for peer in range(gram_ref.shape[0]):
        gram_ref[peer] = compact


def sum_kernel(in_ref, out_ref):
    total = in_ref[0]
    for peer in range(1, in_ref.shape[0]):
        total = total + in_ref[peer]
    for peer in range(out_ref.shape[0]):
        out_ref[peer] = total


def solve_kernel(entries, parts_ref, cells_ref, ortho_ref, upper_ref):
    total = parts_ref[0]
    for peer in range(1, parts_ref.shape[0]):
        total = total + parts_ref[peer]
    total = total / entries
    lane = lax.broadcasted_iota(jnp.int32, (32, 128), 1)
    line = lax.broadcasted_iota(jnp.int32, (32, 128), 0)
    wide = jnp.concatenate([roll_lanes(total, -32 * i) for i in range(4)], axis=0)
    work = jnp.where(lane < 32, wide, jnp.where(lane == line + 32, 1.0, 0.0))
    roots = jnp.zeros((32, 128), jnp.float32)
    for begin in range(0, 32, 8):
        columns = [jnp.broadcast_to(work[:, k : k + 1], (32, 128)) for k in range(begin, begin + 8)]
        rows = [work[k : k + 1] for k in range(begin, begin + 8)]
        factors = []
        for j in range(8):
            k = begin + j
            pivot = columns[j][k : k + 1]
            roots = jnp.where(line == k, pivot, roots)
            factor = jnp.where(line > k, columns[j] * (1.0 / pivot), 0.0)
            factors.append(factor)
            for i in range(j + 1, 8):
                columns[i] = columns[i] - factor * columns[i][k : k + 1]
                rows[i] = rows[i] - factor[begin + i : begin + i + 1] * rows[j]
        for factor, row in zip(factors, rows):
            work = work - factor * row
    work = work / jnp.sqrt(roots)
    upper_ref[...] = jnp.where(lane >= line, work, 0.0)[:, :32]
    inverse = roll_lanes(work, -32)[:, :32]
    ortho = jnp.dot(
        inverse, cells_ref[...], precision=lax.Precision.HIGHEST, preferred_element_type=jnp.float32
    )
    level = level_of(jnp.max(jnp.abs(ortho), axis=1, keepdims=True))
    code = root_code(ortho, 1.0 / spacing(level))
    half = ortho.shape[1] // 2
    both = join(code[:, :half], code[:, half:])
    ortho_ref[:, 0, :half] = both
    ortho_ref[:, 0, half:] = jnp.broadcast_to(level, (32, 128))


def place_kernel(in_ref, out_ref):
    block = lane_group((8, 128), 16)
    line = lax.broadcasted_iota(jnp.int32, (8, 128), 0)
    distance = (block - line) % 8
    for part in range(4):
        sources = slice(8 * part, 8 * part + 8)
        scale = code_scale(in_ref[sources, 0, 1152:1280])
        for pair in range(9):
            both = in_ref[sources, 0, 128 * pair : 128 * pair + 128]
            for unit, code in zip((pair, pair + 9), halves(both)):
                field, tile = unit // 3, unit % 3
                value = from_root_code(code, scale)
                total = value
                for k in range(1, 8):
                    moved = roll_rows(roll_lanes(value, 16 * k), -k)
                    total = jnp.where(distance == k, moved, total)
                out_ref[field, 8 * tile : 8 * tile + 8, 128 * part : 128 * part + 128] = total


def call(kernel, out_shape, name, scratch=(), spaces=None, vmem=40, cost=None):
    specs = {}
    if spaces:
        specs = dict(in_specs=[pl.BlockSpec(memory_space=space) for space in spaces])
    return pl.pallas_call(
        kernel,
        out_shape=out_shape,
        scratch_shapes=list(scratch),
        compiler_params=pltpu.CompilerParams(vmem_limit_bytes=vmem * 1024 * 1024),
        name=name,
        cost_estimate=cost,
        **specs,
    )


def f32(*shape):
    return jax.ShapeDtypeStruct(shape, jnp.float32)


VEC = ("z_hi", "y")
SPACE = ("x", "z_lo", "core")
LINE = ("z_hi", "z_lo", "core")
PLANE = ("x", "y")


def body(perturbation, trajectory, step_order):
    tiles = lax.axis_size(SPACE)
    first, second = lax.axis_size(LINE), lax.axis_size(PLANE)
    sent = call(
        pack_kernel,
        jax.ShapeDtypeStruct((32, 8 * QUADS, 128), jnp.int32),
        "pack",
        [
            pltpu.VMEM((6, ROWS, 512), jnp.float32),
            pltpu.VMEM((18, ROWS, 512), jnp.bfloat16),
            pltpu.VMEM((8 * PAIRS, 512), jnp.int32),
            pltpu.VMEM((2, 8 * (PAIRS - WHOLE), 512), jnp.int32),
            pltpu.SemaphoreType.DMA((2,)),
        ],
        spaces=(pltpu.HBM, pltpu.HBM),
        vmem=60,
    )(perturbation[0], trajectory[0].reshape(18, ROWS, 512))
    held = lax.all_to_all(sent, VEC, split_axis=0, concat_axis=0, tiled=True)
    state, base, far, near = call(
        unpack_kernel,
        (f32(6, ROWS, 8, 128), f32(36, ROWS, 128), f32(HALO_ROWS, 128), f32(HALO_ROWS, 128)),
        "unpack",
        [pltpu.VMEM((HALO_ROWS, 128), jnp.float32)] * 2,
        spaces=(pltpu.SMEM, pltpu.VMEM),
    )(step_order, held.reshape(32 * 8 * QUADS, 128))
    far = lax.ppermute(far, SPACE, [(i, (i + 1 if i % 2 else i - 1) % tiles) for i in range(tiles)])
    near = lax.ppermute(near, SPACE, [(i, i ^ 1) for i in range(tiles)])
    coefs = pltpu.VMEM((2, COEF, ROWS + 16, 128), jnp.float32)
    kept, middle = call(
        inner_kernel,
        (f32(6, 6, ROWS, 8, 128), f32(32, 768)),
        "inner",
        [pltpu.VMEM((2, COEF, ROWS, 128), jnp.float32)],
        cost=pl.CostEstimate(flops=20_000_000, bytes_accessed=8_000_000, transcendentals=0),
    )(state, base)
    cells, gram = call(
        outer_kernel,
        (f32(32, 2304), f32(first, 8, 128)),
        "outer",
        [
            pltpu.VMEM((6, 6, ROWS, 8, 128), jnp.float32),
            coefs,
            pltpu.VMEM((2, HALO_ROWS, 128), jnp.float32),
        ],
    )(state, base, far, near, kept, middle)
    gram = lax.all_to_all(gram, LINE, split_axis=0, concat_axis=0, tiled=True)
    gram = call(sum_kernel, f32(second, 8, 128), "sums")(gram)
    gram = lax.all_to_all(gram, PLANE, split_axis=0, concat_axis=0, tiled=True)
    entries = float(6 * ROWS * 512 * tiles)
    ortho, upper = call(
        lambda *refs: solve_kernel(entries, *refs), (jax.ShapeDtypeStruct((32, 1, 1280), jnp.int32), f32(32, 32)), "solve"
    )(gram, cells)
    ortho = lax.all_to_all(ortho, VEC, split_axis=0, concat_axis=0, tiled=True)
    placed = call(place_kernel, f32(6, ROWS, 512), "place")(ortho)
    return placed[None], upper


def solution(mesh):
    fine = jax.sharding.Mesh(mesh.devices.reshape(4, 8, 4, 2, 2), VEC + SPACE)
    in_specs = (P(VEC, None, SPACE, None), P(VEC, None, None, SPACE, None), P())
    out_specs = (P(VEC, None, SPACE, None), P())
    return jax.shard_map(body, mesh=fine, in_specs=in_specs, out_specs=out_specs, check_vma=False)
```

```python
import jax
import jax.numpy as jnp
from jax import lax
from jax.experimental import pallas as pl
from jax.experimental.pallas import tpu as pltpu
from jax.sharding import PartitionSpec as P

GRAVITY_TOP = 1.0
GRAVITY_LOW = 0.5
DEPTH = 1.0
CORIOLIS = 0.3
TIME_STEP = 0.25

ROWS = 24
HALO = 6
WINDOW = 28
PAD = ROWS + 2 * HALO
PERT_PAIRS = 9
PAIRS = 36
WHOLE = 32
SPLIT_FROM = 4
QUADS = WHOLE // 4
BASE_QUAD = PERT_PAIRS // 4
TOP_CODE = 32000.0
BASE_SCALE = 16384.0
STEP_ROWS = tuple(HALO - section for section in range(6))
STATE_HALO_ROWS = 3 * HALO * 8
HALO_ROWS = STATE_HALO_ROWS + 3 * sum(STEP_ROWS) + 1
COEF = 14


def roll_lanes(value, shift):
    shift %= value.shape[-1]
    return pltpu.roll(value, shift, 1) if shift else value


def roll_rows(value, shift):
    shift %= value.shape[0]
    return pltpu.roll(value, shift, 0) if shift else value


def lane_group(shape, size):
    return lax.broadcasted_iota(jnp.int32, shape, 1) // size


def quad_transposes(quads):
    group = lane_group((8, 128), 32)
    odd, upper = (group % 2) == 1, group >= 2
    moved = [(roll_lanes(b, 32), roll_lanes(a, -32), roll_lanes(d, 32), roll_lanes(c, -32)) for a, b, c, d in quads]
    quads = [
        (jnp.where(odd, p, a), jnp.where(odd, b, q), jnp.where(odd, r, c), jnp.where(odd, d, t))
        for (a, b, c, d), (p, q, r, t) in zip(quads, moved)
    ]
    moved = [tuple(roll_lanes(item, 64) for item in quad) for quad in quads]
    return [
        (jnp.where(upper, r, a), jnp.where(upper, t, b), jnp.where(upper, c, p), jnp.where(upper, d, q))
        for (a, b, c, d), (p, q, r, t) in zip(quads, moved)
    ]


def join(first, second):
    return (first & 0xFFFF) | (second << 16)


def halves(value):
    return (value << 16) >> 16, value >> 16


def to_code(value):
    return jnp.round(value).astype(jnp.int32)


def level_of(largest):
    return jnp.ceil(8.0 * jnp.log2(jnp.maximum(largest, 1e-30))).astype(jnp.int32)


def spacing(level):
    return jnp.exp2(level.astype(jnp.float32) * 0.125)


def root_code(value, inverse):
    size = jnp.minimum(TOP_CODE * jnp.sqrt(jnp.abs(value) * inverse), 32767.0)
    return to_code(jnp.where(value < 0, -size, size))


def from_root_code(code, scale):
    code = code.astype(jnp.float32)
    return code * jnp.abs(code) * scale


def code_scale(level):
    return spacing(level) * (1.0 / (TOP_CODE * TOP_CODE))


def spread_level(level):
    for shift in (1, 2, 4, 8, 16):
        level = level + roll_lanes(level, shift)
    return level


def pack_kernel(pert_hbm, traj_hbm, out_hbm, out_ref, pert_ref, traj_ref, pair_ref, split_ref, sems):
    copies = [
        pltpu.make_async_copy(pert_hbm, pert_ref, sems.at[0]),
        pltpu.make_async_copy(traj_hbm, traj_ref, sems.at[1]),
    ]
    for copy in copies:
        copy.start()
    copies[0].wait()
    largest = jnp.abs(pert_ref[0, 0:8])
    for field in range(6):
        for tile in range(3):
            largest = jnp.maximum(largest, jnp.abs(pert_ref[field, 8 * tile : 8 * tile + 8]))
    level = level_of(jnp.max(largest, axis=(0, 1), keepdims=True))
    inverse = jnp.broadcast_to(1.0 / spacing(level), (8, 512))
    level = jnp.broadcast_to(level, (8, 128))

    for pair in range(PERT_PAIRS):
        field, tile = pair // 3, pair % 3
        first = root_code(pert_ref[field, 8 * tile : 8 * tile + 8], inverse)
        second = root_code(pert_ref[field + 3, 8 * tile : 8 * tile + 8], inverse)
        pair_ref[8 * pair : 8 * pair + 8] = join(first, second)
    copies[1].wait()
    for section in range(3):
        for field in range(3):
            value = [
                to_code(traj_ref[6 * section + i].astype(jnp.float32) * BASE_SCALE)
                for i in (field, field + 3)
            ]
            both = join(*value)
            for tile in range(3):
                pair = PERT_PAIRS + 9 * tile + 3 * section + field
                pair_ref[8 * pair : 8 * pair + 8] = both[8 * tile : 8 * tile + 8]
    spare = lax.broadcasted_iota(jnp.int32, (8, 128), 1) % 32 >= WINDOW
    for parity in range(2):
        split_ref[parity] = roll_lanes(pair_ref[8 * WHOLE :], 6 - 16 * parity)
    for begin in range(0, QUADS, 2):
        places, quads = [], []
        for quad in range(begin, begin + 2):
            raw = [pair_ref[8 * pair : 8 * pair + 8] for pair in range(4 * quad, 4 * quad + 4)]
            for parity in range(2):
                items = [roll_lanes(item, 6 - 16 * parity) for item in raw]
                for part in range(4):
                    columns = slice(128 * part, 128 * part + 128)
                    four = [item[:, columns] for item in items]
                    for i in range(4):
                        piece = 4 * quad + i - SPLIT_FROM
                        if piece >= 0:
                            moved = split_ref[parity, 8 * (piece // 7) : 8 * (piece // 7) + 8, columns]
                            moved = roll_lanes(moved, WINDOW - 4 * (piece % 7))
                            four[i] = jnp.where(spare, moved, four[i])
                        elif piece == -SPLIT_FROM:
                            four[i] = jnp.where(spare, level, four[i])
                    places.append((8 * part + parity, 8 * quad))
                    quads.append(four)
        for (target, at), four in zip(places, quad_transposes(quads)):
            for position, item in enumerate(four):
                out_ref[target + 2 * position, at : at + 8] = item
        rows = pl.ds(8 * begin, 16)
        copy = pltpu.make_async_copy(
            out_ref.at[:, rows], out_hbm.at[:, rows], sems.at[2 + begin // 2]
        )
        copy.start()
        copies.append(copy)
    for copy in copies[2:]:
        copy.wait()


def odd_tile():
    return lax.axis_index("core") == 1


def unpack_kernel(order_ref, in_ref, state_ref, base_ref, far_ref, near_ref, up_ref, down_ref):
    column = lax.broadcasted_iota(jnp.int32, (8, 128), 1) % 32
    scale = None
    for quad in range(BASE_QUAD + 1):
        rows = [
            [
                in_ref[pl.ds(8 * QUADS * 8 * i + 8 * quad + row, 8, stride=8 * QUADS), :]
                for i in range(4)
            ]
            for row in range(8)
        ]
        for row, four in enumerate(quad_transposes(rows)):
            for pair, both in enumerate(four, 4 * quad):
                if pair >= PERT_PAIRS:
                    continue
                first, second = halves(both)
                if scale is None:
                    level = roll_lanes(jnp.where(column == WINDOW, first, 0), -WINDOW)
                    level = spread_level(level)
                    scale = code_scale(level)
                field, line = pair // 3, 8 * (pair % 3) + row
                if line < HALO or line >= ROWS - HALO:
                    coded = jnp.where(column >= WINDOW, level, both)
                    side_ref, at = (up_ref, line) if line < HALO else (down_ref, line - ROWS + HALO)
                    side_ref[pl.ds(8 * (HALO * field + at), 8)] = coded
                for layer, item in enumerate((first, second)):
                    item = from_root_code(item, scale)
                    state_ref[field + 3 * layer, line] = item
    source = lax.broadcasted_iota(jnp.int32, (128, 512), 0)
    target = lax.broadcasted_iota(jnp.int32, (128, 512), 1)
    spread = ((source % 32 == target % 32) & (source // 32 == target // 128)).astype(jnp.float32)
    spread = spread.astype(jnp.bfloat16)
    lane = lax.broadcasted_iota(jnp.int32, (8, 128), 1)
    for step in range(2):
        block = in_ref[pl.ds(pl.multiple_of(order_ref[step] * (8 * QUADS), 8), 8 * QUADS), :]
        pieces = jnp.zeros((8, 128), jnp.int32)
        for piece in range(WHOLE - SPLIT_FROM):
            source = piece + SPLIT_FROM
            to = 32 * (piece // 7) + 4 * (piece % 7)
            moved = block[8 * (source // 4) : 8 * (source // 4) + 8]
            moved = roll_lanes(moved, to - 32 * (source % 4) - WINDOW)
            pieces = jnp.where((lane >= to) & (lane < to + 4), moved, pieces)
        block = jnp.concatenate([block[8 * BASE_QUAD :], pieces], axis=0)
        for layer, part in enumerate(halves(block)):
            part = part.astype(jnp.float32).astype(jnp.bfloat16)
            wide = jnp.dot(part, spread, preferred_element_type=jnp.float32) * (1.0 / BASE_SCALE)
            for unit in range(27):
                tile, field = unit // 9, 6 * (unit % 9 // 3) + unit % 3 + 3 * layer
                at = PERT_PAIRS + unit - 4 * BASE_QUAD
                item = wide[8 * (at // 4) : 8 * (at // 4) + 8, 128 * (at % 4) : 128 * (at % 4) + 128]
                base_ref[18 * step + field, 8 * tile : 8 * tile + 8] = item
    place = STATE_HALO_ROWS
    for section in range(6):
        width = STEP_ROWS[section]
        for field in range(3):
            for side_ref, rows in ((up_ref, slice(0, 8)), (down_ref, slice(ROWS - 8, ROWS))):
                codes = [
                    to_code(base_ref[6 * section + field + 3 * layer, rows] * BASE_SCALE)
                    for layer in range(2)
                ]
                both = join(*codes)
                both = both[0:width] if side_ref is up_ref else both[8 - width : 8]
                side_ref[place : place + width] = both
            place += width
    for side_ref in (up_ref, down_ref):
        side_ref[place : place + 1] = jnp.zeros((1, 128), jnp.int32)
    odd = odd_tile()

    @pl.when(odd)
    def _():
        far_ref[...] = down_ref[...]
        near_ref[...] = up_ref[...]

    @pl.when(jnp.logical_not(odd))
    def _():
        far_ref[...] = up_ref[...]
        near_ref[...] = down_ref[...]


def coefficients(fields, scale):
    results = []
    dx = lambda f: roll_rows(f, -1) - roll_rows(f, 1)
    dy = lambda f: roll_lanes(f, -1) - roll_lanes(f, 1)
    for layer in range(2):
        depth, xvel, yvel = fields[3 * layer : 3 * layer + 3]
        results += [
            scale * (depth + DEPTH),
            scale * xvel,
            scale * yvel,
            scale * dx(xvel),
            scale * dy(xvel) - TIME_STEP * CORIOLIS,
            scale * dx(yvel) + TIME_STEP * CORIOLIS,
            scale * dy(yvel),
        ]
    return results


def section_rows(cur, anchor, put, coef, kind, row, count):
    scale = 0.5 * TIME_STEP

    def dy(value):
        return roll_lanes(value, -1) - roll_lanes(value, 1)

    span = range(row - 1, row + count + 1)
    h = [[cur(3 * layer, i) for i in span] for layer in range(2)]
    top = [(scale * GRAVITY_TOP) * (h[0][i] + h[1][i]) for i in range(count + 2)]
    low = [top[i] + (scale * GRAVITY_LOW) * h[1][i] for i in range(count + 2)]
    for layer, pressure in enumerate((top, low)):
        at = COEF // 2 * layer
        u = [cur(3 * layer + 1, i) for i in span]
        v = [cur(3 * layer + 2, i) for i in span]
        depth = [coef(at, i) for i in span]
        xvel = [coef(at + 1, i) for i in span]
        flux = [depth[i] * u[i] + h[layer][i] * xvel[i] for i in range(count + 2)]
        for i in range(1, count + 1):
            line = row + i - 1
            h_i, u_i, v_i = h[layer][i], u[i], v[i]
            yvel, xvel_dx, xvel_dy, yvel_dx, yvel_dy = [coef(at + k, line) for k in range(2, 7)]
            h_new = h_i - (flux[i + 1] - flux[i - 1]) - dy(depth[i] * v_i + h_i * yvel)
            u_new = u_i - (
                xvel[i] * (u[i + 1] - u[i - 1])
                + u_i * xvel_dx
                + yvel * dy(u_i)
                + v_i * xvel_dy
                + (pressure[i + 1] - pressure[i - 1])
            )
            v_new = v_i - (
                xvel[i] * (v[i + 1] - v[i - 1])
                + u_i * yvel_dx
                + yvel * dy(v_i)
                + v_i * yvel_dy
                + dy(pressure[i])
            )
            for field, value in enumerate((h_new, u_new, v_new)):
                field += 3 * layer
                if kind == 1:
                    value = 0.75 * anchor(field, line) + 0.25 * value
                if kind == 2:
                    value = (1.0 / 3.0) * anchor(field, line) + (2.0 / 3.0) * value
                put(field, line, value)


def own_cells(lines):
    block = lane_group((8, 128), 16)
    results = []
    for quarter in range(4):
        total = None
        for row in range(8):
            moved = roll_lanes(lines[row], 16 * row - 32 * quarter - HALO)
            total = moved if total is None else jnp.where(block == row, moved, total)
        results.append(total)
    return results


def inside(section, row):
    return section < row < ROWS - 1 - section


def inner_kernel(state_ref, base_ref, kept_ref, middle_ref, coef_ref):
    for section in range(6):
        fields = [base_ref[6 * section + field] for field in range(6)]
        for index, value in enumerate(coefficients(fields, 0.5 * TIME_STEP)):
            coef_ref[section % 2, index] = value
        source = state_ref if section == 0 else kept_ref.at[section - 1]
        anchor = state_ref if section < 3 else kept_ref.at[2]

        def put(field, row, value):
            kept_ref[section, field, row] = value

        section_rows(
            lambda field, row: source[field, row],
            lambda field, row: anchor[field, row],
            put,
            lambda index, row: coef_ref[section % 2, index, pl.ds(row, 8, stride=0), :],
            section % 3,
            section + 1,
            ROWS - 2 - 2 * section,
        )
    for field in range(6):
        cells = own_cells([kept_ref[5, field, 8 + row] for row in range(8)])
        for quarter, item in enumerate(cells):
            middle_ref[8 * quarter : 8 * quarter + 8, 128 * field : 128 * field + 128] = item


def outer_kernel(
    state_ref, base_ref, far_ref, near_ref, kept_ref, middle_ref, cells_ref, gram_ref, edge_ref, coef_ref, sides_ref, halo_ref
):
    odd = odd_tile()

    @pl.when(odd)
    def _():
        sides_ref[0] = near_ref[...]
        sides_ref[1] = far_ref[...]

    @pl.when(jnp.logical_not(odd))
    def _():
        sides_ref[0] = far_ref[...]
        sides_ref[1] = near_ref[...]

    column = lax.broadcasted_iota(jnp.int32, (8, 128), 1) % 32
    for side in range(2):
        level = roll_lanes(jnp.where(column == WINDOW, sides_ref[side, 0:8], 0), -WINDOW)
        scale = code_scale(spread_level(level))
        for field in range(3):
            for line in range(HALO):
                both = sides_ref[side, pl.ds(8 * (HALO * field + line), 8)]
                for layer, code in enumerate(halves(both)):
                    halo_ref[field + 3 * layer, HALO * side + line] = from_root_code(code, scale)

    def slot(row):
        return row + HALO if row < ROWS // 2 else row - HALO

    def after(section):
        def read(field, row):
            if section < 0:
                if row < 0:
                    return halo_ref[field, row + HALO]
                if row >= ROWS:
                    return halo_ref[field, row - ROWS + HALO]
                return state_ref[field, row]
            if inside(section, row):
                return kept_ref[section, field, row]
            return edge_ref[section, field, slot(row)]

        return read

    place = STATE_HALO_ROWS
    for section in range(6):
        width = STEP_ROWS[section]
        fields = []
        for field in range(6):
            at = place + width * (field % 3)
            low, high = [
                halves(sides_ref[side, at : at + width])[field // 3].astype(jnp.float32) * (1.0 / BASE_SCALE)
                for side in range(2)
            ]
            gap = jnp.zeros((16 - 2 * width, 128), jnp.float32)
            fields.append(jnp.concatenate([low, base_ref[6 * section + field], high, gap], axis=0))
        place += 3 * width
        for index, value in enumerate(coefficients(fields, 0.5 * TIME_STEP)):
            coef_ref[section % 2, index] = value

        def put(field, row, value):
            edge_ref[section, field, slot(row)] = value

        for begin in (section + 1 - HALO, ROWS - 1 - section):
            section_rows(
                after(section - 1),
                after(-1 if section < 3 else 2),
                put,
                lambda index, row: coef_ref[section % 2, index, pl.ds(row + width, 8, stride=0), :],
                section % 3,
                begin,
                HALO,
            )
    last = after(5)
    for unit in range(18):
        field, tile = unit // 3, unit % 3
        columns = slice(128 * unit, 128 * unit + 128)
        if tile == 1:
            cells_ref[:, columns] = middle_ref[:, 128 * field : 128 * field + 128]
            continue
        cells = own_cells([last(field, 8 * tile + row) for row in range(8)])
        for quarter, item in enumerate(cells):
            cells_ref[8 * quarter : 8 * quarter + 8, columns] = item
    cells = cells_ref[...]
    gram = lax.dot_general(
        cells,
        cells,
        (((1,), (1,)), ((), ())),
        precision=lax.Precision.HIGHEST,
        preferred_element_type=jnp.float32,
    )
    compact = jnp.concatenate([gram[8 * i : 8 * i + 8] for i in range(4)], axis=1)
    for peer in range(gram_ref.shape[0]):
        gram_ref[peer] = compact


def sum_kernel(in_ref, out_ref):
    total = in_ref[0]
    for peer in range(1, in_ref.shape[0]):
        total = total + in_ref[peer]
    for peer in range(out_ref.shape[0]):
        out_ref[peer] = total


def solve_kernel(entries, parts_ref, cells_ref, ortho_ref, upper_ref):
    total = parts_ref[0]
    for peer in range(1, parts_ref.shape[0]):
        total = total + parts_ref[peer]
    total = total / entries
    lane = lax.broadcasted_iota(jnp.int32, (32, 128), 1)
    line = lax.broadcasted_iota(jnp.int32, (32, 128), 0)
    wide = jnp.concatenate([roll_lanes(total, -32 * i) for i in range(4)], axis=0)
    work = jnp.where(lane < 32, wide, jnp.where(lane == line + 32, 1.0, 0.0))
    roots = jnp.zeros((32, 128), jnp.float32)
    for begin in range(0, 32, 8):
        columns = [jnp.broadcast_to(work[:, k : k + 1], (32, 128)) for k in range(begin, begin + 8)]
        rows = [work[k : k + 1] for k in range(begin, begin + 8)]
        factors = []
        for j in range(8):
            k = begin + j
            pivot = columns[j][k : k + 1]
            roots = jnp.where(line == k, pivot, roots)
            factor = jnp.where(line > k, columns[j] * (1.0 / pivot), 0.0)
            factors.append(factor)
            for i in range(j + 1, 8):
                columns[i] = columns[i] - factor * columns[i][k : k + 1]
                rows[i] = rows[i] - factor[begin + i : begin + i + 1] * rows[j]
        for factor, row in zip(factors, rows):
            work = work - factor * row
    work = work / jnp.sqrt(roots)
    upper_ref[...] = jnp.where(lane >= line, work, 0.0)[:, :32]
    inverse = roll_lanes(work, -32)[:, :32]
    ortho = jnp.dot(
        inverse, cells_ref[...], precision=lax.Precision.HIGHEST, preferred_element_type=jnp.float32
    )
    level = level_of(jnp.max(jnp.abs(ortho), axis=1, keepdims=True))
    code = root_code(ortho, 1.0 / spacing(level))
    half = ortho.shape[1] // 2
    both = join(code[:, :half], code[:, half:])
    ortho_ref[:, 0, :half] = both
    ortho_ref[:, 0, half:] = jnp.broadcast_to(level, (32, 128))


def place_kernel(in_ref, out_hbm, out_ref, sems):
    block = lane_group((8, 128), 16)
    line = lax.broadcasted_iota(jnp.int32, (8, 128), 0)
    distance = (block - line) % 8
    scales = [code_scale(in_ref[8 * part : 8 * part + 8, 0, 1152:1280]) for part in range(4)]
    copies = []
    for first in range(3):
        for tile in range(3):
            pair = 3 * first + tile
            for part in range(4):
                both = in_ref[8 * part : 8 * part + 8, 0, 128 * pair : 128 * pair + 128]
                for field, code in zip((first, first + 3), halves(both)):
                    value = from_root_code(code, scales[part])
                    total = value
                    for k in range(1, 8):
                        moved = roll_rows(roll_lanes(value, 16 * k), -k)
                        total = jnp.where(distance == k, moved, total)
                    out_ref[field, 8 * tile : 8 * tile + 8, 128 * part : 128 * part + 128] = total
        for field in (first, first + 3):
            copy = pltpu.make_async_copy(out_ref.at[field], out_hbm.at[field], sems.at[field])
            copy.start()
            copies.append(copy)
    for copy in copies:
        copy.wait()


def call(kernel, out_shape, name, scratch=(), spaces=None, vmem=40, cost=None, out_space=None):
    specs = {}
    if spaces:
        specs = dict(in_specs=[pl.BlockSpec(memory_space=space) for space in spaces])
    if out_space is not None:
        specs["out_specs"] = pl.BlockSpec(memory_space=out_space)
    return pl.pallas_call(
        kernel,
        out_shape=out_shape,
        scratch_shapes=list(scratch),
        compiler_params=pltpu.CompilerParams(vmem_limit_bytes=vmem * 1024 * 1024),
        name=name,
        cost_estimate=cost,
        **specs,
    )


def f32(*shape):
    return jax.ShapeDtypeStruct(shape, jnp.float32)


VEC = ("z_hi", "y")
SPACE = ("x", "z_lo", "core")
LINE = ("z_hi", "z_lo", "core")
PLANE = ("x", "y")


def body(perturbation, trajectory, step_order):
    tiles = lax.axis_size(SPACE)
    first, second = lax.axis_size(LINE), lax.axis_size(PLANE)
    sent = call(
        pack_kernel,
        jax.ShapeDtypeStruct((32, 8 * QUADS, 128), jnp.int32),
        "pack",
        [
            pltpu.VMEM((32, 8 * QUADS, 128), jnp.int32),
            pltpu.VMEM((6, ROWS, 512), jnp.float32),
            pltpu.VMEM((18, ROWS, 512), jnp.bfloat16),
            pltpu.VMEM((8 * PAIRS, 512), jnp.int32),
            pltpu.VMEM((2, 8 * (PAIRS - WHOLE), 512), jnp.int32),
            pltpu.SemaphoreType.DMA((2 + QUADS // 2,)),
        ],
        spaces=(pltpu.HBM, pltpu.HBM),
        out_space=pltpu.HBM,
        vmem=60,
    )(perturbation[0], trajectory[0].reshape(18, ROWS, 512))
    held = lax.all_to_all(sent, VEC, split_axis=0, concat_axis=0, tiled=True)
    side = jax.ShapeDtypeStruct((HALO_ROWS, 128), jnp.int32)
    state, base, far, near = call(
        unpack_kernel,
        (f32(6, ROWS, 8, 128), f32(36, ROWS, 128), side, side),
        "unpack",
        [pltpu.VMEM((HALO_ROWS, 128), jnp.int32)] * 2,
        spaces=(pltpu.SMEM, pltpu.VMEM),
    )(step_order, held.reshape(32 * 8 * QUADS, 128))
    far = lax.ppermute(far, SPACE, [(i, (i + 1 if i % 2 else i - 1) % tiles) for i in range(tiles)])
    near = lax.ppermute(near, SPACE, [(i, i ^ 1) for i in range(tiles)])
    coefs = pltpu.VMEM((2, COEF, ROWS + 16, 128), jnp.float32)
    kept, middle = call(
        inner_kernel,
        (f32(6, 6, ROWS, 8, 128), f32(32, 768)),
        "inner",
        [pltpu.VMEM((2, COEF, ROWS, 128), jnp.float32)],
        cost=pl.CostEstimate(flops=20_000_000, bytes_accessed=8_000_000, transcendentals=0),
    )(state, base)
    cells, gram = call(
        outer_kernel,
        (f32(32, 2304), f32(first, 8, 128)),
        "outer",
        [
            pltpu.VMEM((6, 6, ROWS, 8, 128), jnp.float32),
            coefs,
            pltpu.VMEM((2, HALO_ROWS, 128), jnp.int32),
            pltpu.VMEM((6, 2 * HALO, 8, 128), jnp.float32),
        ],
    )(state, base, far, near, kept, middle)
    gram = lax.all_to_all(gram, LINE, split_axis=0, concat_axis=0, tiled=True)
    gram = call(sum_kernel, f32(second, 8, 128), "sums")(gram)
    gram = lax.all_to_all(gram, PLANE, split_axis=0, concat_axis=0, tiled=True)
    entries = float(6 * ROWS * 512 * tiles)
    ortho, upper = call(
        lambda *refs: solve_kernel(entries, *refs), (jax.ShapeDtypeStruct((32, 1, 1280), jnp.int32), f32(32, 32)), "solve"
    )(gram, cells)
    ortho = lax.all_to_all(ortho, VEC, split_axis=0, concat_axis=0, tiled=True)
    placed = call(
        place_kernel,
        f32(6, ROWS, 512),
        "place",
        [pltpu.VMEM((6, ROWS, 512), jnp.float32), pltpu.SemaphoreType.DMA((6,))],
        spaces=(pltpu.VMEM,),
        out_space=pltpu.HBM,
    )(ortho)
    return placed[None], upper


def solution(mesh):
    fine = jax.sharding.Mesh(mesh.devices.reshape(4, 8, 4, 2, 2), VEC + SPACE)
    in_specs = (P(VEC, None, SPACE, None), P(VEC, None, None, SPACE, None), P())
    out_specs = (P(VEC, None, SPACE, None), P())
    return jax.shard_map(body, mesh=fine, in_specs=in_specs, out_specs=out_specs, check_vma=False)
```

```python
import jax
import jax.numpy as jnp
from jax import lax
from jax.experimental import pallas as pl
from jax.experimental.pallas import tpu as pltpu
from jax.sharding import PartitionSpec as P

GRAVITY_TOP = 1.0
GRAVITY_LOW = 0.5
DEPTH = 1.0
CORIOLIS = 0.3
TIME_STEP = 0.25

ROWS = 24
HALO = 6
WINDOW = 28
PAD = ROWS + 2 * HALO
PERT_PAIRS = 9
PAIRS = 36
WHOLE = 32
SPLIT_FROM = 4
QUADS = WHOLE // 4
BASE_QUAD = PERT_PAIRS // 4
TOP_CODE = 32000.0
BASE_SCALE = 16384.0
STEP_ROWS = tuple(HALO - section for section in range(6))
STATE_HALO_ROWS = 3 * HALO * 8
HALO_ROWS = STATE_HALO_ROWS + 3 * sum(STEP_ROWS) + 1
COEF = 14
PANEL = 16


def roll_lanes(value, shift):
    shift %= value.shape[-1]
    return pltpu.roll(value, shift, 1) if shift else value


def roll_rows(value, shift):
    shift %= value.shape[0]
    return pltpu.roll(value, shift, 0) if shift else value


def lane_group(shape, size):
    return lax.broadcasted_iota(jnp.int32, shape, 1) // size


def quad_transposes(quads):
    group = lane_group((8, 128), 32)
    odd, upper = (group % 2) == 1, group >= 2
    moved = [(roll_lanes(b, 32), roll_lanes(a, -32), roll_lanes(d, 32), roll_lanes(c, -32)) for a, b, c, d in quads]
    quads = [
        (jnp.where(odd, p, a), jnp.where(odd, b, q), jnp.where(odd, r, c), jnp.where(odd, d, t))
        for (a, b, c, d), (p, q, r, t) in zip(quads, moved)
    ]
    moved = [tuple(roll_lanes(item, 64) for item in quad) for quad in quads]
    return [
        (jnp.where(upper, r, a), jnp.where(upper, t, b), jnp.where(upper, c, p), jnp.where(upper, d, q))
        for (a, b, c, d), (p, q, r, t) in zip(quads, moved)
    ]


def join(first, second):
    return (first & 0xFFFF) | (second << 16)


def halves(value):
    return (value << 16) >> 16, value >> 16


def to_code(value):
    return jnp.round(value).astype(jnp.int32)


def level_of(largest):
    return jnp.ceil(8.0 * jnp.log2(jnp.maximum(largest, 1e-30))).astype(jnp.int32)


def spacing(level):
    return jnp.exp2(level.astype(jnp.float32) * 0.125)


def root_code(value, inverse):
    size = jnp.minimum(TOP_CODE * jnp.sqrt(jnp.abs(value) * inverse), 32767.0)
    return to_code(jnp.where(value < 0, -size, size))


def from_root_code(code, scale):
    code = code.astype(jnp.float32)
    return code * jnp.abs(code) * scale


def code_scale(level):
    return spacing(level) * (1.0 / (TOP_CODE * TOP_CODE))


def spread_level(level):
    for shift in (1, 2, 4, 8, 16):
        level = level + roll_lanes(level, shift)
    return level


def pack_kernel(pert_hbm, traj_hbm, out_hbm, out_ref, pert_ref, traj_ref, pair_ref, split_ref, sems):
    copies = [
        pltpu.make_async_copy(pert_hbm, pert_ref, sems.at[0]),
        pltpu.make_async_copy(traj_hbm, traj_ref, sems.at[1]),
    ]
    for copy in copies:
        copy.start()
    copies[0].wait()
    largest = jnp.abs(pert_ref[0, 0:8])
    for field in range(6):
        for tile in range(3):
            largest = jnp.maximum(largest, jnp.abs(pert_ref[field, 8 * tile : 8 * tile + 8]))
    level = level_of(jnp.max(largest, axis=(0, 1), keepdims=True))
    inverse = jnp.broadcast_to(1.0 / spacing(level), (8, 512))
    level = jnp.broadcast_to(level, (8, 128))

    for pair in range(PERT_PAIRS):
        field, tile = pair // 3, pair % 3
        first = root_code(pert_ref[field, 8 * tile : 8 * tile + 8], inverse)
        second = root_code(pert_ref[field + 3, 8 * tile : 8 * tile + 8], inverse)
        pair_ref[8 * pair : 8 * pair + 8] = join(first, second)
    copies[1].wait()
    for section in range(3):
        for field in range(3):
            value = [
                to_code(traj_ref[6 * section + i].astype(jnp.float32) * BASE_SCALE)
                for i in (field, field + 3)
            ]
            both = join(*value)
            for tile in range(3):
                pair = PERT_PAIRS + 9 * tile + 3 * section + field
                pair_ref[8 * pair : 8 * pair + 8] = both[8 * tile : 8 * tile + 8]
    spare = lax.broadcasted_iota(jnp.int32, (8, 128), 1) % 32 >= WINDOW
    for parity in range(2):
        split_ref[parity] = roll_lanes(pair_ref[8 * WHOLE :], 6 - 16 * parity)
    for begin in range(0, QUADS, 2):
        places, quads = [], []
        for quad in range(begin, begin + 2):
            raw = [pair_ref[8 * pair : 8 * pair + 8] for pair in range(4 * quad, 4 * quad + 4)]
            for parity in range(2):
                items = [roll_lanes(item, 6 - 16 * parity) for item in raw]
                for part in range(4):
                    columns = slice(128 * part, 128 * part + 128)
                    four = [item[:, columns] for item in items]
                    for i in range(4):
                        piece = 4 * quad + i - SPLIT_FROM
                        if piece >= 0:
                            moved = split_ref[parity, 8 * (piece // 7) : 8 * (piece // 7) + 8, columns]
                            moved = roll_lanes(moved, WINDOW - 4 * (piece % 7))
                            four[i] = jnp.where(spare, moved, four[i])
                        elif piece == -SPLIT_FROM:
                            four[i] = jnp.where(spare, level, four[i])
                    places.append((8 * part + parity, 8 * quad))
                    quads.append(four)
        for (target, at), four in zip(places, quad_transposes(quads)):
            for position, item in enumerate(four):
                out_ref[target + 2 * position, at : at + 8] = item
        rows = pl.ds(8 * begin, 16)
        copy = pltpu.make_async_copy(
            out_ref.at[:, rows], out_hbm.at[:, rows], sems.at[2 + begin // 2]
        )
        copy.start()
        copies.append(copy)
    for copy in copies[2:]:
        copy.wait()


def odd_tile():
    return lax.axis_index("core") == 1


def unpack_kernel(order_ref, in_ref, state_ref, base_ref, far_ref, near_ref, up_ref, down_ref):
    column = lax.broadcasted_iota(jnp.int32, (8, 128), 1) % 32
    scale = None
    for quad in range(BASE_QUAD + 1):
        rows = [
            [
                in_ref[pl.ds(8 * QUADS * 8 * i + 8 * quad + row, 8, stride=8 * QUADS), :]
                for i in range(4)
            ]
            for row in range(8)
        ]
        for row, four in enumerate(quad_transposes(rows)):
            for pair, both in enumerate(four, 4 * quad):
                if pair >= PERT_PAIRS:
                    continue
                first, second = halves(both)
                if scale is None:
                    level = roll_lanes(jnp.where(column == WINDOW, first, 0), -WINDOW)
                    level = spread_level(level)
                    scale = code_scale(level)
                field, line = pair // 3, 8 * (pair % 3) + row
                if line < HALO or line >= ROWS - HALO:
                    coded = jnp.where(column >= WINDOW, level, both)
                    side_ref, at = (up_ref, line) if line < HALO else (down_ref, line - ROWS + HALO)
                    side_ref[pl.ds(8 * (HALO * field + at), 8)] = coded
                for layer, item in enumerate((first, second)):
                    item = from_root_code(item, scale)
                    state_ref[field + 3 * layer, line] = item
    source = lax.broadcasted_iota(jnp.int32, (128, 512), 0)
    target = lax.broadcasted_iota(jnp.int32, (128, 512), 1)
    spread = ((source % 32 == target % 32) & (source // 32 == target // 128)).astype(jnp.float32)
    spread = spread.astype(jnp.bfloat16)
    lane = lax.broadcasted_iota(jnp.int32, (8, 128), 1)
    for step in range(2):
        block = in_ref[pl.ds(pl.multiple_of(order_ref[step] * (8 * QUADS), 8), 8 * QUADS), :]
        pieces = jnp.zeros((8, 128), jnp.int32)
        for piece in range(WHOLE - SPLIT_FROM):
            source = piece + SPLIT_FROM
            to = 32 * (piece // 7) + 4 * (piece % 7)
            moved = block[8 * (source // 4) : 8 * (source // 4) + 8]
            moved = roll_lanes(moved, to - 32 * (source % 4) - WINDOW)
            pieces = jnp.where((lane >= to) & (lane < to + 4), moved, pieces)
        block = jnp.concatenate([block[8 * BASE_QUAD :], pieces], axis=0)
        for layer, part in enumerate(halves(block)):
            part = part.astype(jnp.float32).astype(jnp.bfloat16)
            wide = jnp.dot(part, spread, preferred_element_type=jnp.float32) * (1.0 / BASE_SCALE)
            for unit in range(27):
                tile, field = unit // 9, 6 * (unit % 9 // 3) + unit % 3 + 3 * layer
                at = PERT_PAIRS + unit - 4 * BASE_QUAD
                item = wide[8 * (at // 4) : 8 * (at // 4) + 8, 128 * (at % 4) : 128 * (at % 4) + 128]
                base_ref[18 * step + field, 8 * tile : 8 * tile + 8] = item
    place = STATE_HALO_ROWS
    for section in range(6):
        width = STEP_ROWS[section]
        for field in range(3):
            for side_ref, rows in ((up_ref, slice(0, 8)), (down_ref, slice(ROWS - 8, ROWS))):
                codes = [
                    to_code(base_ref[6 * section + field + 3 * layer, rows] * BASE_SCALE)
                    for layer in range(2)
                ]
                both = join(*codes)
                both = both[0:width] if side_ref is up_ref else both[8 - width : 8]
                side_ref[place : place + width] = both
            place += width
    for side_ref in (up_ref, down_ref):
        side_ref[place : place + 1] = jnp.zeros((1, 128), jnp.int32)
    odd = odd_tile()

    @pl.when(odd)
    def _():
        far_ref[...] = down_ref[...]
        near_ref[...] = up_ref[...]

    @pl.when(jnp.logical_not(odd))
    def _():
        far_ref[...] = up_ref[...]
        near_ref[...] = down_ref[...]


def coefficients(fields, scale):
    results = []
    dx = lambda f: roll_rows(f, -1) - roll_rows(f, 1)
    dy = lambda f: roll_lanes(f, -1) - roll_lanes(f, 1)
    for layer in range(2):
        depth, xvel, yvel = fields[3 * layer : 3 * layer + 3]
        results += [
            scale * (depth + DEPTH),
            scale * xvel,
            scale * yvel,
            scale * dx(xvel),
            scale * dy(xvel) - TIME_STEP * CORIOLIS,
            scale * dx(yvel) + TIME_STEP * CORIOLIS,
            scale * dy(yvel),
        ]
    return results


def section_rows(cur, anchor, put, coef, kind, row, count):
    scale = 0.5 * TIME_STEP

    def dy(value):
        return roll_lanes(value, -1) - roll_lanes(value, 1)

    span = range(row - 1, row + count + 1)
    h = [[cur(3 * layer, i) for i in span] for layer in range(2)]
    top = [(scale * GRAVITY_TOP) * (h[0][i] + h[1][i]) for i in range(count + 2)]
    low = [top[i] + (scale * GRAVITY_LOW) * h[1][i] for i in range(count + 2)]
    for layer, pressure in enumerate((top, low)):
        at = COEF // 2 * layer
        u = [cur(3 * layer + 1, i) for i in span]
        v = [cur(3 * layer + 2, i) for i in span]
        depth = [coef(at, i) for i in span]
        xvel = [coef(at + 1, i) for i in span]
        flux = [depth[i] * u[i] + h[layer][i] * xvel[i] for i in range(count + 2)]
        for i in range(1, count + 1):
            line = row + i - 1
            h_i, u_i, v_i = h[layer][i], u[i], v[i]
            yvel, xvel_dx, xvel_dy, yvel_dx, yvel_dy = [coef(at + k, line) for k in range(2, 7)]
            h_new = h_i - (flux[i + 1] - flux[i - 1]) - dy(depth[i] * v_i + h_i * yvel)
            u_new = u_i - (
                xvel[i] * (u[i + 1] - u[i - 1])
                + u_i * xvel_dx
                + yvel * dy(u_i)
                + v_i * xvel_dy
                + (pressure[i + 1] - pressure[i - 1])
            )
            v_new = v_i - (
                xvel[i] * (v[i + 1] - v[i - 1])
                + u_i * yvel_dx
                + yvel * dy(v_i)
                + v_i * yvel_dy
                + dy(pressure[i])
            )
            for field, value in enumerate((h_new, u_new, v_new)):
                field += 3 * layer
                if kind == 1:
                    value = 0.75 * anchor(field, line) + 0.25 * value
                if kind == 2:
                    value = (1.0 / 3.0) * anchor(field, line) + (2.0 / 3.0) * value
                put(field, line, value)


def own_cells(tiles):
    first = lane_group((8, 128), 16) % 2 == 0
    merged = [
        [
            jnp.where(first, roll_lanes(lines[-2 * i % 8], -HALO), roll_lanes(lines[(-2 * i - 1) % 8], 16 - HALO))
            for i in range(4)
        ]
        for lines in tiles
    ]
    return quad_transposes(merged)


def inside(section, row):
    return section < row < ROWS - 1 - section


def inner_kernel(state_ref, base_ref, kept_ref, middle_ref, coef_ref):
    for section in range(6):
        fields = [base_ref[6 * section + field] for field in range(6)]
        for index, value in enumerate(coefficients(fields, 0.5 * TIME_STEP)):
            coef_ref[section % 2, index] = value
        source = state_ref if section == 0 else kept_ref.at[section - 1]
        anchor = state_ref if section < 3 else kept_ref.at[2]

        def put(field, row, value):
            kept_ref[section, field, row] = value

        section_rows(
            lambda field, row: source[field, row],
            lambda field, row: anchor[field, row],
            put,
            lambda index, row: coef_ref[section % 2, index, pl.ds(row, 8, stride=0), :],
            section % 3,
            section + 1,
            ROWS - 2 - 2 * section,
        )
    tiles = [[kept_ref[5, field, 8 + row] for row in range(8)] for field in range(6)]
    for field, cells in enumerate(own_cells(tiles)):
        for quarter, item in enumerate(cells):
            middle_ref[8 * quarter : 8 * quarter + 8, 128 * field : 128 * field + 128] = item


def outer_kernel(
    state_ref, base_ref, far_ref, near_ref, kept_ref, middle_ref, cells_ref, gram_ref, edge_ref, coef_ref, sides_ref, halo_ref
):
    odd = odd_tile()

    @pl.when(odd)
    def _():
        sides_ref[0] = near_ref[...]
        sides_ref[1] = far_ref[...]

    @pl.when(jnp.logical_not(odd))
    def _():
        sides_ref[0] = far_ref[...]
        sides_ref[1] = near_ref[...]

    column = lax.broadcasted_iota(jnp.int32, (8, 128), 1) % 32
    for side in range(2):
        level = roll_lanes(jnp.where(column == WINDOW, sides_ref[side, 0:8], 0), -WINDOW)
        scale = code_scale(spread_level(level))
        for field in range(3):
            for line in range(HALO):
                both = sides_ref[side, pl.ds(8 * (HALO * field + line), 8)]
                for layer, code in enumerate(halves(both)):
                    halo_ref[field + 3 * layer, HALO * side + line] = from_root_code(code, scale)

    def slot(row):
        return row + HALO if row < ROWS // 2 else row - HALO

    def after(section):
        def read(field, row):
            if section < 0:
                if row < 0:
                    return halo_ref[field, row + HALO]
                if row >= ROWS:
                    return halo_ref[field, row - ROWS + HALO]
                return state_ref[field, row]
            if inside(section, row):
                return kept_ref[section, field, row]
            return edge_ref[section, field, slot(row)]

        return read

    place = STATE_HALO_ROWS
    for section in range(6):
        width = STEP_ROWS[section]
        fields = []
        for field in range(6):
            at = place + width * (field % 3)
            low, high = [
                halves(sides_ref[side, at : at + width])[field // 3].astype(jnp.float32) * (1.0 / BASE_SCALE)
                for side in range(2)
            ]
            gap = jnp.zeros((16 - 2 * width, 128), jnp.float32)
            fields.append(jnp.concatenate([low, base_ref[6 * section + field], high, gap], axis=0))
        place += 3 * width
        for index, value in enumerate(coefficients(fields, 0.5 * TIME_STEP)):
            coef_ref[section % 2, index] = value

        def put(field, row, value):
            edge_ref[section, field, slot(row)] = value

        for begin in (section + 1 - HALO, ROWS - 1 - section):
            section_rows(
                after(section - 1),
                after(-1 if section < 3 else 2),
                put,
                lambda index, row: coef_ref[section % 2, index, pl.ds(row + width, 8, stride=0), :],
                section % 3,
                begin,
                HALO,
            )
    last = after(5)
    for field in range(6):
        outer = [[last(field, 8 * tile + row) for row in range(8)] for tile in (0, 2)]
        for tile, cells in zip((0, 2), own_cells(outer)):
            for quarter, item in enumerate(cells):
                unit = 3 * field + tile
                cells_ref[8 * quarter : 8 * quarter + 8, 128 * unit : 128 * unit + 128] = item
        unit = 3 * field + 1
        cells_ref[:, 128 * unit : 128 * unit + 128] = middle_ref[:, 128 * field : 128 * field + 128]
    cells = cells_ref[...]
    gram = lax.dot_general(
        cells,
        cells,
        (((1,), (1,)), ((), ())),
        precision=lax.Precision.HIGHEST,
        preferred_element_type=jnp.float32,
    )
    compact = jnp.concatenate([gram[8 * i : 8 * i + 8] for i in range(4)], axis=1)
    for peer in range(gram_ref.shape[0]):
        gram_ref[peer] = compact


def sum_kernel(in_ref, out_ref):
    total = in_ref[0]
    for peer in range(1, in_ref.shape[0]):
        total = total + in_ref[peer]
    for peer in range(out_ref.shape[0]):
        out_ref[peer] = total


def solve_kernel(entries, parts_ref, cells_ref, ortho_ref, upper_ref):
    total = parts_ref[0]
    for peer in range(1, parts_ref.shape[0]):
        total = total + parts_ref[peer]
    total = total / entries
    lane = lax.broadcasted_iota(jnp.int32, (32, 128), 1)
    line = lax.broadcasted_iota(jnp.int32, (32, 128), 0)
    wide = jnp.concatenate([roll_lanes(total, -32 * i) for i in range(4)], axis=0)
    work = jnp.where(lane < 32, wide, jnp.where(lane == line + 32, 1.0, 0.0))
    roots = jnp.zeros((32, 128), jnp.float32)
    for begin in range(0, 32, PANEL):
        columns = [jnp.broadcast_to(work[:, k : k + 1], (32, 128)) for k in range(begin, begin + PANEL)]
        rows = [work[k : k + 1] for k in range(begin, begin + PANEL)]
        factors = []
        for j in range(PANEL):
            k = begin + j
            pivot = columns[j][k : k + 1]
            roots = jnp.where(line == k, pivot, roots)
            factor = jnp.where(line > k, columns[j] * (1.0 / pivot), 0.0)
            factors.append(factor)
            for i in range(j + 1, PANEL):
                columns[i] = columns[i] - factor * columns[i][k : k + 1]
                rows[i] = rows[i] - factor[begin + i : begin + i + 1] * rows[j]
        for factor, row in zip(factors, rows):
            work = work - factor * row
    work = work / jnp.sqrt(roots)
    upper_ref[...] = jnp.where(lane >= line, work, 0.0)[:, :32]
    inverse = roll_lanes(work, -32)[:, :32]
    ortho = jnp.dot(
        inverse, cells_ref[...], precision=lax.Precision.HIGHEST, preferred_element_type=jnp.float32
    )
    level = level_of(jnp.max(jnp.abs(ortho), axis=1, keepdims=True))
    code = root_code(ortho, 1.0 / spacing(level))
    half = ortho.shape[1] // 2
    both = join(code[:, :half], code[:, half:])
    ortho_ref[:, 0, :half] = both
    ortho_ref[:, 0, half:] = jnp.broadcast_to(level, (32, 128))


def block_transposes(values):
    block = lane_group((8, 128), 16)
    line = lax.broadcasted_iota(jnp.int32, (8, 128), 0)

    def shear(values, index, roll, step):
        for bit in (1, 2, 4):
            mask = (index & bit) != 0
            values = [jnp.where(mask, roll(value, step * bit), value) for value in values]
        return values

    values = shear(values, line, roll_lanes, 16)
    values = shear(values, block, roll_rows, -1)
    return shear(values, line, roll_lanes, 16)


def place_kernel(in_ref, out_hbm, out_ref, sems):
    def chunk(part, index):
        return in_ref[8 * part : 8 * part + 8, 0, 128 * index : 128 * index + 128]

    scales = [code_scale(level) for level in block_transposes([chunk(part, 9) for part in range(4)])]
    copies = []
    for first in range(3):
        places = [(tile, part) for tile in range(3) for part in range(4)]
        items = block_transposes([chunk(part, 3 * first + tile) for tile, part in places])
        for (tile, part), both in zip(places, items):
            for field, code in zip((first, first + 3), halves(both)):
                out_ref[field, 8 * tile : 8 * tile + 8, 128 * part : 128 * part + 128] = from_root_code(
                    code, scales[part]
                )
        for field in (first, first + 3):
            copy = pltpu.make_async_copy(out_ref.at[field], out_hbm.at[field], sems.at[field])
            copy.start()
            copies.append(copy)
    for copy in copies:
        copy.wait()


def call(kernel, out_shape, name, scratch=(), spaces=None, vmem=40, cost=None, out_space=None):
    specs = {}
    if spaces:
        specs = dict(in_specs=[pl.BlockSpec(memory_space=space) for space in spaces])
    if out_space is not None:
        specs["out_specs"] = pl.BlockSpec(memory_space=out_space)
    return pl.pallas_call(
        kernel,
        out_shape=out_shape,
        scratch_shapes=list(scratch),
        compiler_params=pltpu.CompilerParams(vmem_limit_bytes=vmem * 1024 * 1024),
        name=name,
        cost_estimate=cost,
        **specs,
    )


def f32(*shape):
    return jax.ShapeDtypeStruct(shape, jnp.float32)


VEC = ("z_hi", "y")
SPACE = ("x", "z_lo", "core")
LINE = ("z_hi", "z_lo", "core")
PLANE = ("x", "y")


def body(perturbation, trajectory, step_order):
    tiles = lax.axis_size(SPACE)
    first, second = lax.axis_size(LINE), lax.axis_size(PLANE)
    sent = call(
        pack_kernel,
        jax.ShapeDtypeStruct((32, 8 * QUADS, 128), jnp.int32),
        "pack",
        [
            pltpu.VMEM((32, 8 * QUADS, 128), jnp.int32),
            pltpu.VMEM((6, ROWS, 512), jnp.float32),
            pltpu.VMEM((18, ROWS, 512), jnp.bfloat16),
            pltpu.VMEM((8 * PAIRS, 512), jnp.int32),
            pltpu.VMEM((2, 8 * (PAIRS - WHOLE), 512), jnp.int32),
            pltpu.SemaphoreType.DMA((2 + QUADS // 2,)),
        ],
        spaces=(pltpu.HBM, pltpu.HBM),
        out_space=pltpu.HBM,
        vmem=60,
    )(perturbation[0], trajectory[0].reshape(18, ROWS, 512))
    held = lax.all_to_all(sent, VEC, split_axis=0, concat_axis=0, tiled=True)
    side = jax.ShapeDtypeStruct((HALO_ROWS, 128), jnp.int32)
    state, base, far, near = call(
        unpack_kernel,
        (f32(6, ROWS, 8, 128), f32(36, ROWS, 128), side, side),
        "unpack",
        [pltpu.VMEM((HALO_ROWS, 128), jnp.int32)] * 2,
        spaces=(pltpu.SMEM, pltpu.VMEM),
    )(step_order, held.reshape(32 * 8 * QUADS, 128))
    far = lax.ppermute(far, SPACE, [(i, (i + 1 if i % 2 else i - 1) % tiles) for i in range(tiles)])
    near = lax.ppermute(near, SPACE, [(i, i ^ 1) for i in range(tiles)])
    coefs = pltpu.VMEM((2, COEF, ROWS + 16, 128), jnp.float32)
    kept, middle = call(
        inner_kernel,
        (f32(6, 6, ROWS, 8, 128), f32(32, 768)),
        "inner",
        [pltpu.VMEM((2, COEF, ROWS, 128), jnp.float32)],
        cost=pl.CostEstimate(flops=20_000_000, bytes_accessed=8_000_000, transcendentals=0),
    )(state, base)
    cells, gram = call(
        outer_kernel,
        (f32(32, 2304), f32(first, 8, 128)),
        "outer",
        [
            pltpu.VMEM((6, 6, ROWS, 8, 128), jnp.float32),
            coefs,
            pltpu.VMEM((2, HALO_ROWS, 128), jnp.int32),
            pltpu.VMEM((6, 2 * HALO, 8, 128), jnp.float32),
        ],
    )(state, base, far, near, kept, middle)
    gram = lax.all_to_all(gram, LINE, split_axis=0, concat_axis=0, tiled=True)
    gram = call(sum_kernel, f32(second, 8, 128), "sums")(gram)
    gram = lax.all_to_all(gram, PLANE, split_axis=0, concat_axis=0, tiled=True)
    entries = float(6 * ROWS * 512 * tiles)
    ortho, upper = call(
        lambda *refs: solve_kernel(entries, *refs), (jax.ShapeDtypeStruct((32, 1, 1280), jnp.int32), f32(32, 32)), "solve"
    )(gram, cells)
    ortho = lax.all_to_all(ortho, VEC, split_axis=0, concat_axis=0, tiled=True)
    placed = call(
        place_kernel,
        f32(6, ROWS, 512),
        "place",
        [pltpu.VMEM((6, ROWS, 512), jnp.float32), pltpu.SemaphoreType.DMA((6,))],
        spaces=(pltpu.VMEM,),
        out_space=pltpu.HBM,
    )(ortho)
    return placed[None], upper


def solution(mesh):
    fine = jax.sharding.Mesh(mesh.devices.reshape(4, 8, 4, 2, 2), VEC + SPACE)
    in_specs = (P(VEC, None, SPACE, None), P(VEC, None, None, SPACE, None), P())
    out_specs = (P(VEC, None, SPACE, None), P())
    return jax.shard_map(body, mesh=fine, in_specs=in_specs, out_specs=out_specs, check_vma=False)
```

```python
import jax
import jax.numpy as jnp
from jax import lax
from jax.experimental import pallas as pl
from jax.experimental.pallas import tpu as pltpu
from jax.sharding import PartitionSpec as P

GRAVITY_TOP = 1.0
GRAVITY_LOW = 0.5
DEPTH = 1.0
CORIOLIS = 0.3
TIME_STEP = 0.25

ROWS = 24
HALO = 6
WINDOW = 28
PAD = ROWS + 2 * HALO
PERT_PAIRS = 9
PAIRS = 36
WHOLE = 32
SPLIT_FROM = 4
QUADS = WHOLE // 4
BASE_QUAD = PERT_PAIRS // 4
TOP_CODE = 32000.0
BASE_SCALE = 16384.0
STEP_ROWS = tuple(HALO - section for section in range(6))
STATE_HALO_ROWS = 3 * HALO * 8
HALO_ROWS = STATE_HALO_ROWS + 3 * sum(STEP_ROWS) + 1
COEF = 14
PANEL = 16


def roll_lanes(value, shift):
    shift %= value.shape[-1]
    return pltpu.roll(value, shift, 1) if shift else value


def roll_rows(value, shift):
    shift %= value.shape[0]
    return pltpu.roll(value, shift, 0) if shift else value


def lane_group(shape, size):
    return lax.broadcasted_iota(jnp.int32, shape, 1) // size


def quad_transposes(quads):
    group = lane_group((8, 128), 32)
    odd, upper = (group % 2) == 1, group >= 2
    moved = [(roll_lanes(b, 32), roll_lanes(a, -32), roll_lanes(d, 32), roll_lanes(c, -32)) for a, b, c, d in quads]
    quads = [
        (jnp.where(odd, p, a), jnp.where(odd, b, q), jnp.where(odd, r, c), jnp.where(odd, d, t))
        for (a, b, c, d), (p, q, r, t) in zip(quads, moved)
    ]
    moved = [tuple(roll_lanes(item, 64) for item in quad) for quad in quads]
    return [
        (jnp.where(upper, r, a), jnp.where(upper, t, b), jnp.where(upper, c, p), jnp.where(upper, d, q))
        for (a, b, c, d), (p, q, r, t) in zip(quads, moved)
    ]


def join(first, second):
    return (first & 0xFFFF) | (second << 16)


def halves(value):
    return (value << 16) >> 16, value >> 16


def to_code(value):
    return jnp.round(value).astype(jnp.int32)


def level_of(largest):
    return jnp.ceil(8.0 * jnp.log2(jnp.maximum(largest, 1e-30))).astype(jnp.int32)


def spacing(level):
    return jnp.exp2(level.astype(jnp.float32) * 0.125)


def root_code(value, inverse):
    size = jnp.minimum(TOP_CODE * jnp.sqrt(jnp.abs(value) * inverse), 32767.0)
    return to_code(jnp.where(value < 0, -size, size))


def from_root_code(code, scale):
    code = code.astype(jnp.float32)
    return code * jnp.abs(code) * scale


def code_scale(level):
    return spacing(level) * (1.0 / (TOP_CODE * TOP_CODE))


def spread_level(level):
    for shift in (1, 2, 4, 8, 16):
        level = level + roll_lanes(level, shift)
    return level


def pack_kernel(pert_hbm, traj_hbm, out_hbm, out_ref, pert_ref, traj_ref, pair_ref, split_ref, sems):
    copies = [
        pltpu.make_async_copy(pert_hbm, pert_ref, sems.at[0]),
        pltpu.make_async_copy(traj_hbm, traj_ref, sems.at[1]),
    ]
    for copy in copies:
        copy.start()
    copies[0].wait()
    largest = jnp.abs(pert_ref[0, 0:8])
    for field in range(6):
        for tile in range(3):
            largest = jnp.maximum(largest, jnp.abs(pert_ref[field, 8 * tile : 8 * tile + 8]))
    level = level_of(jnp.max(largest, axis=(0, 1), keepdims=True))
    inverse = jnp.broadcast_to(1.0 / spacing(level), (8, 512))
    level = jnp.broadcast_to(level, (8, 128))

    for pair in range(PERT_PAIRS):
        field, tile = pair // 3, pair % 3
        first = root_code(pert_ref[field, 8 * tile : 8 * tile + 8], inverse)
        second = root_code(pert_ref[field + 3, 8 * tile : 8 * tile + 8], inverse)
        pair_ref[8 * pair : 8 * pair + 8] = join(first, second)
    copies[1].wait()
    for section in range(3):
        for field in range(3):
            value = [
                to_code(traj_ref[6 * section + i].astype(jnp.float32) * BASE_SCALE)
                for i in (field, field + 3)
            ]
            both = join(*value)
            for tile in range(3):
                pair = PERT_PAIRS + 9 * tile + 3 * section + field
                pair_ref[8 * pair : 8 * pair + 8] = both[8 * tile : 8 * tile + 8]
    spare = lax.broadcasted_iota(jnp.int32, (8, 128), 1) % 32 >= WINDOW
    for parity in range(2):
        split_ref[parity] = roll_lanes(pair_ref[8 * WHOLE :], 6 - 16 * parity)
    for begin in range(0, QUADS, 2):
        places, quads = [], []
        for quad in range(begin, begin + 2):
            raw = [pair_ref[8 * pair : 8 * pair + 8] for pair in range(4 * quad, 4 * quad + 4)]
            for parity in range(2):
                items = [roll_lanes(item, 6 - 16 * parity) for item in raw]
                for part in range(4):
                    columns = slice(128 * part, 128 * part + 128)
                    four = [item[:, columns] for item in items]
                    for i in range(4):
                        piece = 4 * quad + i - SPLIT_FROM
                        if piece >= 0:
                            moved = split_ref[parity, 8 * (piece // 7) : 8 * (piece // 7) + 8, columns]
                            moved = roll_lanes(moved, WINDOW - 4 * (piece % 7))
                            four[i] = jnp.where(spare, moved, four[i])
                        elif piece == -SPLIT_FROM:
                            four[i] = jnp.where(spare, level, four[i])
                    places.append((8 * part + parity, 8 * quad))
                    quads.append(four)
        for (target, at), four in zip(places, quad_transposes(quads)):
            for position, item in enumerate(four):
                out_ref[target + 2 * position, at : at + 8] = item
        rows = pl.ds(8 * begin, 16)
        copy = pltpu.make_async_copy(
            out_ref.at[:, rows], out_hbm.at[:, rows], sems.at[2 + begin // 2]
        )
        copy.start()
        copies.append(copy)
    for copy in copies[2:]:
        copy.wait()


def odd_tile():
    return lax.axis_index("core") == 1


def unpack_kernel(order_ref, in_ref, state_ref, base_ref, far_ref, near_ref, up_ref, down_ref):
    column = lax.broadcasted_iota(jnp.int32, (8, 128), 1) % 32
    scale = None
    for quad in range(BASE_QUAD + 1):
        rows = [
            [
                in_ref[pl.ds(8 * QUADS * 8 * i + 8 * quad + row, 8, stride=8 * QUADS), :]
                for i in range(4)
            ]
            for row in range(8)
        ]
        for row, four in enumerate(quad_transposes(rows)):
            for pair, both in enumerate(four, 4 * quad):
                if pair >= PERT_PAIRS:
                    continue
                first, second = halves(both)
                if scale is None:
                    level = roll_lanes(jnp.where(column == WINDOW, first, 0), -WINDOW)
                    level = spread_level(level)
                    scale = code_scale(level)
                field, line = pair // 3, 8 * (pair % 3) + row
                if line < HALO or line >= ROWS - HALO:
                    coded = jnp.where(column >= WINDOW, level, both)
                    side_ref, at = (up_ref, line) if line < HALO else (down_ref, line - ROWS + HALO)
                    side_ref[pl.ds(8 * (HALO * field + at), 8)] = coded
                for layer, item in enumerate((first, second)):
                    item = from_root_code(item, scale)
                    state_ref[field + 3 * layer, line] = item
    source = lax.broadcasted_iota(jnp.int32, (128, 512), 0)
    target = lax.broadcasted_iota(jnp.int32, (128, 512), 1)
    spread = ((source % 32 == target % 32) & (source // 32 == target // 128)).astype(jnp.float32)
    spread = spread.astype(jnp.bfloat16)
    lane = lax.broadcasted_iota(jnp.int32, (8, 128), 1)
    for step in range(2):
        block = in_ref[pl.ds(pl.multiple_of(order_ref[step] * (8 * QUADS), 8), 8 * QUADS), :]
        pieces = jnp.zeros((8, 128), jnp.int32)
        for piece in range(WHOLE - SPLIT_FROM):
            source = piece + SPLIT_FROM
            to = 32 * (piece // 7) + 4 * (piece % 7)
            moved = block[8 * (source // 4) : 8 * (source // 4) + 8]
            moved = roll_lanes(moved, to - 32 * (source % 4) - WINDOW)
            pieces = jnp.where((lane >= to) & (lane < to + 4), moved, pieces)
        block = jnp.concatenate([block[8 * BASE_QUAD :], pieces], axis=0)
        for layer, part in enumerate(halves(block)):
            part = part.astype(jnp.float32).astype(jnp.bfloat16)
            wide = jnp.dot(part, spread, preferred_element_type=jnp.float32) * (1.0 / BASE_SCALE)
            for unit in range(27):
                tile, field = unit // 9, 6 * (unit % 9 // 3) + unit % 3 + 3 * layer
                at = PERT_PAIRS + unit - 4 * BASE_QUAD
                item = wide[8 * (at // 4) : 8 * (at // 4) + 8, 128 * (at % 4) : 128 * (at % 4) + 128]
                base_ref[18 * step + field, 8 * tile : 8 * tile + 8] = item
    place = STATE_HALO_ROWS
    for section in range(6):
        width = STEP_ROWS[section]
        for field in range(3):
            for side_ref, rows in ((up_ref, slice(0, 8)), (down_ref, slice(ROWS - 8, ROWS))):
                codes = [
                    to_code(base_ref[6 * section + field + 3 * layer, rows] * BASE_SCALE)
                    for layer in range(2)
                ]
                both = join(*codes)
                both = both[0:width] if side_ref is up_ref else both[8 - width : 8]
                side_ref[place : place + width] = both
            place += width
    for side_ref in (up_ref, down_ref):
        side_ref[place : place + 1] = jnp.zeros((1, 128), jnp.int32)
    odd = odd_tile()

    @pl.when(odd)
    def _():
        far_ref[...] = down_ref[...]
        near_ref[...] = up_ref[...]

    @pl.when(jnp.logical_not(odd))
    def _():
        far_ref[...] = up_ref[...]
        near_ref[...] = down_ref[...]


def coefficients(fields, scale):
    results = []
    dx = lambda f: roll_rows(f, -1) - roll_rows(f, 1)
    dy = lambda f: roll_lanes(f, -1) - roll_lanes(f, 1)
    for layer in range(2):
        depth, xvel, yvel = fields[3 * layer : 3 * layer + 3]
        results += [
            scale * (depth + DEPTH),
            scale * xvel,
            scale * yvel,
            scale * dx(xvel),
            scale * dy(xvel) - TIME_STEP * CORIOLIS,
            scale * dx(yvel) + TIME_STEP * CORIOLIS,
            scale * dy(yvel),
        ]
    return results


def section_rows(cur, anchor, put, coef, kind, row, count):
    scale = 0.5 * TIME_STEP

    def dy(value):
        return roll_lanes(value, -1) - roll_lanes(value, 1)

    span = range(row - 1, row + count + 1)
    h = [[cur(3 * layer, i) for i in span] for layer in range(2)]
    top = [(scale * GRAVITY_TOP) * (h[0][i] + h[1][i]) for i in range(count + 2)]
    low = [top[i] + (scale * GRAVITY_LOW) * h[1][i] for i in range(count + 2)]
    for layer, pressure in enumerate((top, low)):
        at = COEF // 2 * layer
        u = [cur(3 * layer + 1, i) for i in span]
        v = [cur(3 * layer + 2, i) for i in span]
        depth = [coef(at, i) for i in span]
        xvel = [coef(at + 1, i) for i in span]
        flux = [depth[i] * u[i] + h[layer][i] * xvel[i] for i in range(count + 2)]
        for i in range(1, count + 1):
            line = row + i - 1
            h_i, u_i, v_i = h[layer][i], u[i], v[i]
            yvel, xvel_dx, xvel_dy, yvel_dx, yvel_dy = [coef(at + k, line) for k in range(2, 7)]
            h_new = h_i - (flux[i + 1] - flux[i - 1]) - dy(depth[i] * v_i + h_i * yvel)
            u_new = u_i - (
                xvel[i] * (u[i + 1] - u[i - 1])
                + u_i * xvel_dx
                + yvel * dy(u_i)
                + v_i * xvel_dy
                + (pressure[i + 1] - pressure[i - 1])
            )
            v_new = v_i - (
                xvel[i] * (v[i + 1] - v[i - 1])
                + u_i * yvel_dx
                + yvel * dy(v_i)
                + v_i * yvel_dy
                + dy(pressure[i])
            )
            for field, value in enumerate((h_new, u_new, v_new)):
                field += 3 * layer
                if kind == 1:
                    value = 0.75 * anchor(field, line) + 0.25 * value
                if kind == 2:
                    value = (1.0 / 3.0) * anchor(field, line) + (2.0 / 3.0) * value
                put(field, line, value)


def own_cells(tiles):
    first = lane_group((8, 128), 16) % 2 == 0
    merged = [
        [
            jnp.where(first, roll_lanes(lines[-2 * i % 8], -HALO), roll_lanes(lines[(-2 * i - 1) % 8], 16 - HALO))
            for i in range(4)
        ]
        for lines in tiles
    ]
    return quad_transposes(merged)


def inside(section, row):
    return section < row < ROWS - 1 - section


def split(value):
    high = value.astype(jnp.bfloat16)
    return high, (value - high.astype(jnp.float32)).astype(jnp.bfloat16)


def inner_kernel(state_ref, base_ref, kept_ref, middle_ref, coef_ref):
    for section in range(6):
        fields = [base_ref[6 * section + field] for field in range(6)]
        for index, value in enumerate(coefficients(fields, 0.5 * TIME_STEP)):
            coef_ref[section % 2, index] = value
        source = state_ref if section == 0 else kept_ref.at[section - 1]
        anchor = state_ref if section < 3 else kept_ref.at[2]

        def put(field, row, value):
            kept_ref[section, field, row] = value

        section_rows(
            lambda field, row: source[field, row],
            lambda field, row: anchor[field, row],
            put,
            lambda index, row: coef_ref[section % 2, index, pl.ds(row, 8, stride=0), :],
            section % 3,
            section + 1,
            ROWS - 2 - 2 * section,
        )
    tiles = [[kept_ref[5, field, 8 + row] for row in range(8)] for field in range(6)]
    for field, cells in enumerate(own_cells(tiles)):
        for quarter, item in enumerate(cells):
            middle_ref[8 * quarter : 8 * quarter + 8, 128 * field : 128 * field + 128] = item


def outer_kernel(
    state_ref, base_ref, far_ref, near_ref, kept_ref, middle_ref, cells_ref, gram_ref, whole_ref, edge_ref, coef_ref, sides_ref, halo_ref
):
    odd = odd_tile()

    @pl.when(odd)
    def _():
        sides_ref[0] = near_ref[...]
        sides_ref[1] = far_ref[...]

    @pl.when(jnp.logical_not(odd))
    def _():
        sides_ref[0] = far_ref[...]
        sides_ref[1] = near_ref[...]

    column = lax.broadcasted_iota(jnp.int32, (8, 128), 1) % 32
    for side in range(2):
        level = roll_lanes(jnp.where(column == WINDOW, sides_ref[side, 0:8], 0), -WINDOW)
        scale = code_scale(spread_level(level))
        for field in range(3):
            for line in range(HALO):
                both = sides_ref[side, pl.ds(8 * (HALO * field + line), 8)]
                for layer, code in enumerate(halves(both)):
                    halo_ref[field + 3 * layer, HALO * side + line] = from_root_code(code, scale)

    def slot(row):
        return row + HALO if row < ROWS // 2 else row - HALO

    def after(section):
        def read(field, row):
            if section < 0:
                if row < 0:
                    return halo_ref[field, row + HALO]
                if row >= ROWS:
                    return halo_ref[field, row - ROWS + HALO]
                return state_ref[field, row]
            if inside(section, row):
                return kept_ref[section, field, row]
            return edge_ref[section, field, slot(row)]

        return read

    place = STATE_HALO_ROWS
    for section in range(6):
        width = STEP_ROWS[section]
        fields = []
        for field in range(6):
            at = place + width * (field % 3)
            low, high = [
                halves(sides_ref[side, at : at + width])[field // 3].astype(jnp.float32) * (1.0 / BASE_SCALE)
                for side in range(2)
            ]
            gap = jnp.zeros((16 - 2 * width, 128), jnp.float32)
            fields.append(jnp.concatenate([low, base_ref[6 * section + field], high, gap], axis=0))
        place += 3 * width
        for index, value in enumerate(coefficients(fields, 0.5 * TIME_STEP)):
            coef_ref[section % 2, index] = value

        def put(field, row, value):
            edge_ref[section, field, slot(row)] = value

        for begin in (section + 1 - HALO, ROWS - 1 - section):
            section_rows(
                after(section - 1),
                after(-1 if section < 3 else 2),
                put,
                lambda index, row: coef_ref[section % 2, index, pl.ds(row + width, 8, stride=0), :],
                section % 3,
                begin,
                HALO,
            )
    last = after(5)
    for field in range(6):
        outer = [[last(field, 8 * tile + row) for row in range(8)] for tile in (0, 2)]
        for tile, cells in zip((0, 2), own_cells(outer)):
            for quarter, item in enumerate(cells):
                unit = 3 * field + tile
                whole_ref[8 * quarter : 8 * quarter + 8, 128 * unit : 128 * unit + 128] = item
        unit = 3 * field + 1
        whole_ref[:, 128 * unit : 128 * unit + 128] = middle_ref[:, 128 * field : 128 * field + 128]
    cells = jnp.concatenate(split(whole_ref[...]), axis=0)
    cells_ref[...] = cells
    gram = lax.dot_general(cells, cells, (((1,), (1,)), ((), ())), preferred_element_type=jnp.float32)
    gram = gram[:32] + gram[32:]
    gram = gram[:, :32] + gram[:, 32:]
    compact = jnp.concatenate([gram[8 * i : 8 * i + 8] for i in range(4)], axis=1)
    for peer in range(gram_ref.shape[0]):
        gram_ref[peer] = compact


def sum_kernel(in_ref, out_ref):
    total = in_ref[0]
    for peer in range(1, in_ref.shape[0]):
        total = total + in_ref[peer]
    for peer in range(out_ref.shape[0]):
        out_ref[peer] = total


def solve_kernel(entries, parts_ref, cells_ref, ortho_ref, upper_ref):
    total = parts_ref[0]
    for peer in range(1, parts_ref.shape[0]):
        total = total + parts_ref[peer]
    total = total / entries
    lane = lax.broadcasted_iota(jnp.int32, (32, 128), 1)
    line = lax.broadcasted_iota(jnp.int32, (32, 128), 0)
    wide = jnp.concatenate([roll_lanes(total, -32 * i) for i in range(4)], axis=0)
    work = jnp.where(lane < 32, wide, jnp.where(lane == line + 32, 1.0, 0.0))
    roots = jnp.zeros((32, 128), jnp.float32)
    for begin in range(0, 32, PANEL):
        columns = [jnp.broadcast_to(work[:, k : k + 1], (32, 128)) for k in range(begin, begin + PANEL)]
        rows = [work[k : k + 1] for k in range(begin, begin + PANEL)]
        factors = []
        for j in range(PANEL):
            k = begin + j
            pivot = columns[j][k : k + 1]
            roots = jnp.where(line == k, pivot, roots)
            factor = jnp.where(line > k, columns[j] * (1.0 / pivot), 0.0)
            factors.append(factor)
            for i in range(j + 1, PANEL):
                columns[i] = columns[i] - factor * columns[i][k : k + 1]
                rows[i] = rows[i] - factor[begin + i : begin + i + 1] * rows[j]
        for factor, row in zip(factors, rows):
            work = work - factor * row
    work = work / jnp.sqrt(roots)
    upper_ref[...] = jnp.where(lane >= line, work, 0.0)[:, :32]
    inverse = jnp.where(lane < 32, roll_lanes(work, -32), 0.0)
    high = inverse.astype(jnp.bfloat16).astype(jnp.float32)
    factors = high + roll_lanes(high, 32) + roll_lanes(inverse - high, 64)
    cells = jnp.concatenate([cells_ref[...], cells_ref[0:32]], axis=0)
    ortho = jnp.dot(factors[:, :96].astype(jnp.bfloat16), cells, preferred_element_type=jnp.float32)
    level = level_of(jnp.max(jnp.abs(ortho), axis=1, keepdims=True))
    code = root_code(ortho, 1.0 / spacing(level))
    half = ortho.shape[1] // 2
    both = join(code[:, :half], code[:, half:])
    ortho_ref[:, 0, :half] = both
    ortho_ref[:, 0, half:] = jnp.broadcast_to(level, (32, 128))


def block_transposes(values):
    block = lane_group((8, 128), 16)
    line = lax.broadcasted_iota(jnp.int32, (8, 128), 0)

    def shear(values, index, roll, step):
        for bit in (1, 2, 4):
            mask = (index & bit) != 0
            values = [jnp.where(mask, roll(value, step * bit), value) for value in values]
        return values

    values = shear(values, line, roll_lanes, 16)
    values = shear(values, block, roll_rows, -1)
    return shear(values, line, roll_lanes, 16)


def place_kernel(in_ref, out_hbm, out_ref, sems):
    def chunk(part, index):
        return in_ref[8 * part : 8 * part + 8, 0, 128 * index : 128 * index + 128]

    scales = [code_scale(level) for level in block_transposes([chunk(part, 9) for part in range(4)])]
    copies = []
    for first in range(3):
        places = [(tile, part) for tile in range(3) for part in range(4)]
        items = block_transposes([chunk(part, 3 * first + tile) for tile, part in places])
        for (tile, part), both in zip(places, items):
            for field, code in zip((first, first + 3), halves(both)):
                out_ref[field, 8 * tile : 8 * tile + 8, 128 * part : 128 * part + 128] = from_root_code(
                    code, scales[part]
                )
        for field in (first, first + 3):
            copy = pltpu.make_async_copy(out_ref.at[field], out_hbm.at[field], sems.at[field])
            copy.start()
            copies.append(copy)
    for copy in copies:
        copy.wait()


def call(kernel, out_shape, name, scratch=(), spaces=None, vmem=40, cost=None, out_space=None):
    specs = {}
    if spaces:
        specs = dict(in_specs=[pl.BlockSpec(memory_space=space) for space in spaces])
    if out_space is not None:
        specs["out_specs"] = pl.BlockSpec(memory_space=out_space)
    return pl.pallas_call(
        kernel,
        out_shape=out_shape,
        scratch_shapes=list(scratch),
        compiler_params=pltpu.CompilerParams(vmem_limit_bytes=vmem * 1024 * 1024),
        name=name,
        cost_estimate=cost,
        **specs,
    )


def f32(*shape):
    return jax.ShapeDtypeStruct(shape, jnp.float32)


VEC = ("z_hi", "y")
SPACE = ("x", "z_lo", "core")
LINE = ("y", "core")
PLANE = ("z_hi", "z_lo", "x")


def body(perturbation, trajectory, step_order):
    tiles = lax.axis_size(SPACE)
    first, second = lax.axis_size(LINE), lax.axis_size(PLANE)
    sent = call(
        pack_kernel,
        jax.ShapeDtypeStruct((32, 8 * QUADS, 128), jnp.int32),
        "pack",
        [
            pltpu.VMEM((32, 8 * QUADS, 128), jnp.int32),
            pltpu.VMEM((6, ROWS, 512), jnp.float32),
            pltpu.VMEM((18, ROWS, 512), jnp.bfloat16),
            pltpu.VMEM((8 * PAIRS, 512), jnp.int32),
            pltpu.VMEM((2, 8 * (PAIRS - WHOLE), 512), jnp.int32),
            pltpu.SemaphoreType.DMA((2 + QUADS // 2,)),
        ],
        spaces=(pltpu.HBM, pltpu.HBM),
        out_space=pltpu.HBM,
        vmem=60,
    )(perturbation[0], trajectory[0].reshape(18, ROWS, 512))
    held = lax.all_to_all(sent, VEC, split_axis=0, concat_axis=0, tiled=True)
    side = jax.ShapeDtypeStruct((HALO_ROWS, 128), jnp.int32)
    state, base, far, near = call(
        unpack_kernel,
        (f32(6, ROWS, 8, 128), f32(36, ROWS, 128), side, side),
        "unpack",
        [pltpu.VMEM((HALO_ROWS, 128), jnp.int32)] * 2,
        spaces=(pltpu.SMEM, pltpu.VMEM),
    )(step_order, held.reshape(32 * 8 * QUADS, 128))
    far = lax.ppermute(far, SPACE, [(i, (i + 1 if i % 2 else i - 1) % tiles) for i in range(tiles)])
    near = lax.ppermute(near, SPACE, [(i, i ^ 1) for i in range(tiles)])
    coefs = pltpu.VMEM((2, COEF, ROWS + 16, 128), jnp.float32)
    kept, middle = call(
        inner_kernel,
        (f32(6, 6, ROWS, 8, 128), f32(32, 768)),
        "inner",
        [pltpu.VMEM((2, COEF, ROWS, 128), jnp.float32)],
        cost=pl.CostEstimate(flops=20_000_000, bytes_accessed=8_000_000, transcendentals=0),
    )(state, base)
    cells, gram = call(
        outer_kernel,
        (jax.ShapeDtypeStruct((64, 2304), jnp.bfloat16), f32(first, 8, 128)),
        "outer",
        [
            pltpu.VMEM((32, 2304), jnp.float32),
            pltpu.VMEM((6, 6, ROWS, 8, 128), jnp.float32),
            coefs,
            pltpu.VMEM((2, HALO_ROWS, 128), jnp.int32),
            pltpu.VMEM((6, 2 * HALO, 8, 128), jnp.float32),
        ],
    )(state, base, far, near, kept, middle)
    gram = lax.all_to_all(gram, LINE, split_axis=0, concat_axis=0, tiled=True)
    gram = call(sum_kernel, f32(second, 8, 128), "sums")(gram)
    gram = lax.all_to_all(gram, PLANE, split_axis=0, concat_axis=0, tiled=True)
    entries = float(6 * ROWS * 512 * tiles)
    ortho, upper = call(
        lambda *refs: solve_kernel(entries, *refs), (jax.ShapeDtypeStruct((32, 1, 1280), jnp.int32), f32(32, 32)), "solve"
    )(gram, cells)
    ortho = lax.all_to_all(ortho, VEC, split_axis=0, concat_axis=0, tiled=True)
    placed = call(
        place_kernel,
        f32(6, ROWS, 512),
        "place",
        [pltpu.VMEM((6, ROWS, 512), jnp.float32), pltpu.SemaphoreType.DMA((6,))],
        spaces=(pltpu.VMEM,),
        out_space=pltpu.HBM,
    )(ortho)
    return placed[None], upper


def solution(mesh):
    fine = jax.sharding.Mesh(mesh.devices.reshape(4, 8, 4, 2, 2), VEC + SPACE)
    in_specs = (P(VEC, None, SPACE, None), P(VEC, None, None, SPACE, None), P())
    out_specs = (P(VEC, None, SPACE, None), P())
    return jax.shard_map(body, mesh=fine, in_specs=in_specs, out_specs=out_specs, check_vma=False)
```

```python
import jax
import jax.numpy as jnp
from jax import lax
from jax.experimental import pallas as pl
from jax.experimental.pallas import tpu as pltpu
from jax.sharding import PartitionSpec as P

GRAVITY_TOP = 1.0
GRAVITY_LOW = 0.5
DEPTH = 1.0
CORIOLIS = 0.3
TIME_STEP = 0.25

ROWS = 24
HALO = 6
WINDOW = 28
PAD = ROWS + 2 * HALO
PERT_PAIRS = 9
PAIRS = 36
WHOLE = 32
SPLIT_FROM = 4
QUADS = WHOLE // 4
BASE_QUAD = PERT_PAIRS // 4
TOP_CODE = 32000.0
BASE_SCALE = 16384.0
STEP_ROWS = tuple(HALO - section for section in range(6))
STATE_HALO_ROWS = 3 * HALO * 8
HALO_ROWS = STATE_HALO_ROWS + 3 * sum(STEP_ROWS) + 1
COEF = 14
PANEL = 16


def roll_lanes(value, shift):
    shift %= value.shape[-1]
    return pltpu.roll(value, shift, 1) if shift else value


def roll_rows(value, shift):
    shift %= value.shape[0]
    return pltpu.roll(value, shift, 0) if shift else value


def lane_group(shape, size):
    return lax.broadcasted_iota(jnp.int32, shape, 1) // size


def quad_transposes(quads):
    group = lane_group((8, 128), 32)
    odd, upper = (group % 2) == 1, group >= 2
    moved = [(roll_lanes(b, 32), roll_lanes(a, -32), roll_lanes(d, 32), roll_lanes(c, -32)) for a, b, c, d in quads]
    quads = [
        (jnp.where(odd, p, a), jnp.where(odd, b, q), jnp.where(odd, r, c), jnp.where(odd, d, t))
        for (a, b, c, d), (p, q, r, t) in zip(quads, moved)
    ]
    moved = [tuple(roll_lanes(item, 64) for item in quad) for quad in quads]
    return [
        (jnp.where(upper, r, a), jnp.where(upper, t, b), jnp.where(upper, c, p), jnp.where(upper, d, q))
        for (a, b, c, d), (p, q, r, t) in zip(quads, moved)
    ]


def join(first, second):
    return (first & 0xFFFF) | (second << 16)


def halves(value):
    return (value << 16) >> 16, value >> 16


def to_code(value):
    return jnp.round(value).astype(jnp.int32)


def level_of(largest):
    return jnp.ceil(8.0 * jnp.log2(jnp.maximum(largest, 1e-30))).astype(jnp.int32)


def spacing(level):
    return jnp.exp2(level.astype(jnp.float32) * 0.125)


def root_code(value, inverse):
    size = jnp.minimum(TOP_CODE * jnp.sqrt(jnp.abs(value) * inverse), 32767.0)
    return to_code(jnp.where(value < 0, -size, size))


def from_root_code(code, scale):
    code = code.astype(jnp.float32)
    return code * jnp.abs(code) * scale


def code_scale(level):
    return spacing(level) * (1.0 / (TOP_CODE * TOP_CODE))


def spread_level(level):
    for shift in (1, 2, 4, 8, 16):
        level = level + roll_lanes(level, shift)
    return level


def pack_kernel(pert_hbm, traj_hbm, out_hbm, out_ref, pert_ref, traj_ref, pair_ref, split_ref, sems):
    copies = [
        pltpu.make_async_copy(pert_hbm, pert_ref, sems.at[0]),
        pltpu.make_async_copy(traj_hbm, traj_ref, sems.at[1]),
    ]
    for copy in copies:
        copy.start()
    copies[0].wait()
    largest = jnp.abs(pert_ref[0, 0:8])
    for field in range(6):
        for tile in range(3):
            largest = jnp.maximum(largest, jnp.abs(pert_ref[field, 8 * tile : 8 * tile + 8]))
    level = level_of(jnp.max(largest, axis=(0, 1), keepdims=True))
    inverse = jnp.broadcast_to(1.0 / spacing(level), (8, 512))
    level = jnp.broadcast_to(level, (8, 128))

    for pair in range(PERT_PAIRS):
        field, tile = pair // 3, pair % 3
        first = root_code(pert_ref[field, 8 * tile : 8 * tile + 8], inverse)
        second = root_code(pert_ref[field + 3, 8 * tile : 8 * tile + 8], inverse)
        pair_ref[8 * pair : 8 * pair + 8] = join(first, second)
    copies[1].wait()
    for section in range(3):
        for field in range(3):
            value = [
                to_code(traj_ref[6 * section + i].astype(jnp.float32) * BASE_SCALE)
                for i in (field, field + 3)
            ]
            both = join(*value)
            for tile in range(3):
                pair = PERT_PAIRS + 9 * tile + 3 * section + field
                pair_ref[8 * pair : 8 * pair + 8] = both[8 * tile : 8 * tile + 8]
    spare = lax.broadcasted_iota(jnp.int32, (8, 128), 1) % 32 >= WINDOW
    for parity in range(2):
        split_ref[parity] = roll_lanes(pair_ref[8 * WHOLE :], 6 - 16 * parity)
    for begin in range(0, QUADS, 2):
        places, quads = [], []
        for quad in range(begin, begin + 2):
            raw = [pair_ref[8 * pair : 8 * pair + 8] for pair in range(4 * quad, 4 * quad + 4)]
            for parity in range(2):
                items = [roll_lanes(item, 6 - 16 * parity) for item in raw]
                for part in range(4):
                    columns = slice(128 * part, 128 * part + 128)
                    four = [item[:, columns] for item in items]
                    for i in range(4):
                        piece = 4 * quad + i - SPLIT_FROM
                        if piece >= 0:
                            moved = split_ref[parity, 8 * (piece // 7) : 8 * (piece // 7) + 8, columns]
                            moved = roll_lanes(moved, WINDOW - 4 * (piece % 7))
                            four[i] = jnp.where(spare, moved, four[i])
                        elif piece == -SPLIT_FROM:
                            four[i] = jnp.where(spare, level, four[i])
                    places.append((8 * part + parity, 8 * quad))
                    quads.append(four)
        for (target, at), four in zip(places, quad_transposes(quads)):
            for position, item in enumerate(four):
                out_ref[target + 2 * position, at : at + 8] = item
        rows = pl.ds(8 * begin, 16)
        copy = pltpu.make_async_copy(
            out_ref.at[:, rows], out_hbm.at[:, rows], sems.at[2 + begin // 2]
        )
        copy.start()
        copies.append(copy)
    for copy in copies[2:]:
        copy.wait()


def odd_tile():
    return lax.axis_index("core") == 1


def unpack_kernel(order_ref, in_ref, state_ref, base_ref, far_ref, near_ref, up_ref, down_ref):
    column = lax.broadcasted_iota(jnp.int32, (8, 128), 1) % 32
    scale = None
    for quad in range(BASE_QUAD + 1):
        rows = [
            [
                in_ref[pl.ds(8 * QUADS * 8 * i + 8 * quad + row, 8, stride=8 * QUADS), :]
                for i in range(4)
            ]
            for row in range(8)
        ]
        for row, four in enumerate(quad_transposes(rows)):
            for pair, both in enumerate(four, 4 * quad):
                if pair >= PERT_PAIRS:
                    continue
                first, second = halves(both)
                if scale is None:
                    level = roll_lanes(jnp.where(column == WINDOW, first, 0), -WINDOW)
                    level = spread_level(level)
                    scale = code_scale(level)
                field, line = pair // 3, 8 * (pair % 3) + row
                if line < HALO or line >= ROWS - HALO:
                    coded = jnp.where(column >= WINDOW, level, both)
                    side_ref, at = (up_ref, line) if line < HALO else (down_ref, line - ROWS + HALO)
                    side_ref[pl.ds(8 * (HALO * field + at), 8)] = coded
                for layer, item in enumerate((first, second)):
                    item = from_root_code(item, scale)
                    state_ref[field + 3 * layer, line] = item
    source = lax.broadcasted_iota(jnp.int32, (128, 512), 0)
    target = lax.broadcasted_iota(jnp.int32, (128, 512), 1)
    spread = ((source % 32 == target % 32) & (source // 32 == target // 128)).astype(jnp.float32)
    spread = spread.astype(jnp.bfloat16)
    lane = lax.broadcasted_iota(jnp.int32, (8, 128), 1)
    for step in range(2):
        block = in_ref[pl.ds(pl.multiple_of(order_ref[step] * (8 * QUADS), 8), 8 * QUADS), :]
        pieces = jnp.zeros((8, 128), jnp.int32)
        for piece in range(WHOLE - SPLIT_FROM):
            source = piece + SPLIT_FROM
            to = 32 * (piece // 7) + 4 * (piece % 7)
            moved = block[8 * (source // 4) : 8 * (source // 4) + 8]
            moved = roll_lanes(moved, to - 32 * (source % 4) - WINDOW)
            pieces = jnp.where((lane >= to) & (lane < to + 4), moved, pieces)
        block = jnp.concatenate([block[8 * BASE_QUAD :], pieces], axis=0)
        for layer, part in enumerate(halves(block)):
            part = part.astype(jnp.float32).astype(jnp.bfloat16)
            wide = jnp.dot(part, spread, preferred_element_type=jnp.float32) * (1.0 / BASE_SCALE)
            for unit in range(27):
                tile, field = unit // 9, 6 * (unit % 9 // 3) + unit % 3 + 3 * layer
                at = PERT_PAIRS + unit - 4 * BASE_QUAD
                item = wide[8 * (at // 4) : 8 * (at // 4) + 8, 128 * (at % 4) : 128 * (at % 4) + 128]
                base_ref[18 * step + field, 8 * tile : 8 * tile + 8] = item
    place = STATE_HALO_ROWS
    for section in range(6):
        width = STEP_ROWS[section]
        for field in range(3):
            for side_ref, rows in ((up_ref, slice(0, 8)), (down_ref, slice(ROWS - 8, ROWS))):
                codes = [
                    to_code(base_ref[6 * section + field + 3 * layer, rows] * BASE_SCALE)
                    for layer in range(2)
                ]
                both = join(*codes)
                both = both[0:width] if side_ref is up_ref else both[8 - width : 8]
                side_ref[place : place + width] = both
            place += width
    for side_ref in (up_ref, down_ref):
        side_ref[place : place + 1] = jnp.zeros((1, 128), jnp.int32)
    odd = odd_tile()

    @pl.when(odd)
    def _():
        far_ref[...] = down_ref[...]
        near_ref[...] = up_ref[...]

    @pl.when(jnp.logical_not(odd))
    def _():
        far_ref[...] = up_ref[...]
        near_ref[...] = down_ref[...]


def coefficients(fields, scale):
    results = []
    dx = lambda f: roll_rows(f, -1) - roll_rows(f, 1)
    dy = lambda f: roll_lanes(f, -1) - roll_lanes(f, 1)
    for layer in range(2):
        depth, xvel, yvel = fields[3 * layer : 3 * layer + 3]
        results += [
            scale * (depth + DEPTH),
            scale * xvel,
            scale * yvel,
            scale * dx(xvel),
            scale * dy(xvel) - TIME_STEP * CORIOLIS,
            scale * dx(yvel) + TIME_STEP * CORIOLIS,
            scale * dy(yvel),
        ]
    return results


def section_rows(cur, anchor, put, coef, kind, row, count):
    scale = 0.5 * TIME_STEP

    def dy(value):
        return roll_lanes(value, -1) - roll_lanes(value, 1)

    span = range(row - 1, row + count + 1)
    h = [[cur(3 * layer, i) for i in span] for layer in range(2)]
    top = [(scale * GRAVITY_TOP) * (h[0][i] + h[1][i]) for i in range(count + 2)]
    low = [top[i] + (scale * GRAVITY_LOW) * h[1][i] for i in range(count + 2)]
    for layer, pressure in enumerate((top, low)):
        at = COEF // 2 * layer
        u = [cur(3 * layer + 1, i) for i in span]
        v = [cur(3 * layer + 2, i) for i in span]
        depth = [coef(at, i) for i in span]
        xvel = [coef(at + 1, i) for i in span]
        flux = [depth[i] * u[i] + h[layer][i] * xvel[i] for i in range(count + 2)]
        for i in range(1, count + 1):
            line = row + i - 1
            h_i, u_i, v_i = h[layer][i], u[i], v[i]
            yvel, xvel_dx, xvel_dy, yvel_dx, yvel_dy = [coef(at + k, line) for k in range(2, 7)]
            h_new = h_i - (flux[i + 1] - flux[i - 1]) - dy(depth[i] * v_i + h_i * yvel)
            u_new = u_i - (
                xvel[i] * (u[i + 1] - u[i - 1])
                + u_i * xvel_dx
                + yvel * dy(u_i)
                + v_i * xvel_dy
                + (pressure[i + 1] - pressure[i - 1])
            )
            v_new = v_i - (
                xvel[i] * (v[i + 1] - v[i - 1])
                + u_i * yvel_dx
                + yvel * dy(v_i)
                + v_i * yvel_dy
                + dy(pressure[i])
            )
            for field, value in enumerate((h_new, u_new, v_new)):
                field += 3 * layer
                if kind == 1:
                    value = 0.75 * anchor(field, line) + 0.25 * value
                if kind == 2:
                    value = (1.0 / 3.0) * anchor(field, line) + (2.0 / 3.0) * value
                put(field, line, value)


def own_cells(tiles):
    first = lane_group((8, 128), 16) % 2 == 0
    merged = [
        [
            jnp.where(first, roll_lanes(lines[-2 * i % 8], -HALO), roll_lanes(lines[(-2 * i - 1) % 8], 16 - HALO))
            for i in range(4)
        ]
        for lines in tiles
    ]
    return quad_transposes(merged)


def inside(section, row):
    return section < row < ROWS - 1 - section


def split(value):
    high = value.astype(jnp.bfloat16)
    return high, (value - high.astype(jnp.float32)).astype(jnp.bfloat16)


def inner_kernel(state_ref, base_ref, kept_ref, middle_ref, coef_ref):
    for section in range(6):
        fields = [base_ref[6 * section + field] for field in range(6)]
        for index, value in enumerate(coefficients(fields, 0.5 * TIME_STEP)):
            coef_ref[section % 2, index] = value
        source = state_ref if section == 0 else kept_ref.at[section - 1]
        anchor = state_ref if section < 3 else kept_ref.at[2]

        def put(field, row, value):
            kept_ref[section, field, row] = value

        section_rows(
            lambda field, row: source[field, row],
            lambda field, row: anchor[field, row],
            put,
            lambda index, row: coef_ref[section % 2, index, pl.ds(row, 8, stride=0), :],
            section % 3,
            section + 1,
            ROWS - 2 - 2 * section,
        )
    tiles = [[kept_ref[5, field, 8 + row] for row in range(8)] for field in range(6)]
    for field, cells in enumerate(own_cells(tiles)):
        for quarter, item in enumerate(cells):
            middle_ref[8 * quarter : 8 * quarter + 8, 128 * field : 128 * field + 128] = item


def outer_kernel(
    state_ref, base_ref, far_ref, near_ref, kept_ref, middle_ref, cells_ref, gram_ref, whole_ref, edge_ref, coef_ref, sides_ref, halo_ref
):
    odd = odd_tile()

    @pl.when(odd)
    def _():
        sides_ref[0] = near_ref[...]
        sides_ref[1] = far_ref[...]

    @pl.when(jnp.logical_not(odd))
    def _():
        sides_ref[0] = far_ref[...]
        sides_ref[1] = near_ref[...]

    column = lax.broadcasted_iota(jnp.int32, (8, 128), 1) % 32
    for side in range(2):
        level = roll_lanes(jnp.where(column == WINDOW, sides_ref[side, 0:8], 0), -WINDOW)
        scale = code_scale(spread_level(level))
        for field in range(3):
            for line in range(HALO):
                both = sides_ref[side, pl.ds(8 * (HALO * field + line), 8)]
                for layer, code in enumerate(halves(both)):
                    halo_ref[field + 3 * layer, HALO * side + line] = from_root_code(code, scale)

    def slot(row):
        return row + HALO if row < ROWS // 2 else row - HALO

    def after(section):
        def read(field, row):
            if section < 0:
                if row < 0:
                    return halo_ref[field, row + HALO]
                if row >= ROWS:
                    return halo_ref[field, row - ROWS + HALO]
                return state_ref[field, row]
            if inside(section, row):
                return kept_ref[section, field, row]
            return edge_ref[section, field, slot(row)]

        return read

    place = STATE_HALO_ROWS
    for section in range(6):
        width = STEP_ROWS[section]
        fields = []
        for field in range(6):
            at = place + width * (field % 3)
            low, high = [
                halves(sides_ref[side, at : at + width])[field // 3].astype(jnp.float32) * (1.0 / BASE_SCALE)
                for side in range(2)
            ]
            value = base_ref[6 * section + field]
            fields.append(jnp.concatenate([low, value[: 16 - width], value[8 + width :], high], axis=0))
        place += 3 * width
        for index, value in enumerate(coefficients(fields, 0.5 * TIME_STEP)):
            coef_ref[section % 2, index] = value

        def put(field, row, value):
            edge_ref[section, field, slot(row)] = value

        for begin in (section + 1 - HALO, ROWS - 1 - section):
            section_rows(
                after(section - 1),
                after(-1 if section < 3 else 2),
                put,
                lambda index, row: coef_ref[
                    section % 2, index, pl.ds(row + (width if row < 12 else 8 - width), 8, stride=0), :
                ],
                section % 3,
                begin,
                HALO,
            )
    last = after(5)
    for field in range(6):
        outer = [[last(field, 8 * tile + row) for row in range(8)] for tile in (0, 2)]
        for tile, cells in zip((0, 2), own_cells(outer)):
            for quarter, item in enumerate(cells):
                unit = 3 * field + tile
                whole_ref[8 * quarter : 8 * quarter + 8, 128 * unit : 128 * unit + 128] = item
        unit = 3 * field + 1
        whole_ref[:, 128 * unit : 128 * unit + 128] = middle_ref[:, 128 * field : 128 * field + 128]
    cells = jnp.concatenate(split(whole_ref[...]), axis=0)
    cells_ref[...] = cells
    gram = lax.dot_general(cells, cells, (((1,), (1,)), ((), ())), preferred_element_type=jnp.float32)
    gram = gram[:32] + gram[32:]
    gram = gram[:, :32] + gram[:, 32:]
    compact = jnp.concatenate([gram[8 * i : 8 * i + 8] for i in range(4)], axis=1)
    for peer in range(gram_ref.shape[0]):
        gram_ref[peer] = compact


def sum_kernel(in_ref, out_ref):
    total = in_ref[0]
    for peer in range(1, in_ref.shape[0]):
        total = total + in_ref[peer]
    for peer in range(out_ref.shape[0]):
        out_ref[peer] = total


def solve_kernel(entries, parts_ref, cells_ref, ortho_ref, upper_ref):
    total = parts_ref[0]
    for peer in range(1, parts_ref.shape[0]):
        total = total + parts_ref[peer]
    total = total / entries
    lane = lax.broadcasted_iota(jnp.int32, (32, 128), 1)
    line = lax.broadcasted_iota(jnp.int32, (32, 128), 0)
    wide = jnp.concatenate([roll_lanes(total, -32 * i) for i in range(4)], axis=0)
    work = jnp.where(lane < 32, wide, jnp.where(lane == line + 32, 1.0, 0.0))
    roots = jnp.zeros((32, 128), jnp.float32)
    for begin in range(0, 32, PANEL):
        columns = [jnp.broadcast_to(work[:, k : k + 1], (32, 128)) for k in range(begin, begin + PANEL)]
        rows = [work[k : k + 1] for k in range(begin, begin + PANEL)]
        factors = []
        for j in range(PANEL):
            k = begin + j
            pivot = columns[j][k : k + 1]
            roots = jnp.where(line == k, pivot, roots)
            factor = jnp.where(line > k, columns[j] * (1.0 / pivot), 0.0)
            factors.append(factor)
            for i in range(j + 1, PANEL):
                columns[i] = columns[i] - factor * columns[i][k : k + 1]
                rows[i] = rows[i] - factor[begin + i : begin + i + 1] * rows[j]
        for factor, row in zip(factors, rows):
            work = work - factor * row
    work = work / jnp.sqrt(roots)
    upper_ref[...] = jnp.where(lane >= line, work, 0.0)[:, :32]
    inverse = jnp.where(lane < 32, roll_lanes(work, -32), 0.0)
    high = inverse.astype(jnp.bfloat16).astype(jnp.float32)
    factors = high + roll_lanes(high, 32) + roll_lanes(inverse - high, 64)
    cells = jnp.concatenate([cells_ref[...], cells_ref[0:32]], axis=0)
    ortho = jnp.dot(factors[:, :96].astype(jnp.bfloat16), cells, preferred_element_type=jnp.float32)
    level = level_of(jnp.max(jnp.abs(ortho), axis=1, keepdims=True))
    code = root_code(ortho, 1.0 / spacing(level))
    half = ortho.shape[1] // 2
    both = join(code[:, :half], code[:, half:])
    ortho_ref[:, 0, :half] = both
    ortho_ref[:, 0, half:] = jnp.broadcast_to(level, (32, 128))


def block_transposes(values):
    block = lane_group((8, 128), 16)
    line = lax.broadcasted_iota(jnp.int32, (8, 128), 0)

    def shear(values, index, roll, step):
        for bit in (1, 2, 4):
            mask = (index & bit) != 0
            values = [jnp.where(mask, roll(value, step * bit), value) for value in values]
        return values

    values = shear(values, line, roll_lanes, 16)
    values = shear(values, block, roll_rows, -1)
    return shear(values, line, roll_lanes, 16)


def place_kernel(in_ref, out_hbm, out_ref, sems):
    def chunk(part, index):
        return in_ref[8 * part : 8 * part + 8, 0, 128 * index : 128 * index + 128]

    scales = [code_scale(level) for level in block_transposes([chunk(part, 9) for part in range(4)])]
    copies = []
    for first in range(3):
        places = [(tile, part) for tile in range(3) for part in range(4)]
        items = block_transposes([chunk(part, 3 * first + tile) for tile, part in places])
        for (tile, part), both in zip(places, items):
            for field, code in zip((first, first + 3), halves(both)):
                out_ref[field, 8 * tile : 8 * tile + 8, 128 * part : 128 * part + 128] = from_root_code(
                    code, scales[part]
                )
        for field in (first, first + 3):
            copy = pltpu.make_async_copy(out_ref.at[field], out_hbm.at[field], sems.at[field])
            copy.start()
            copies.append(copy)
    for copy in copies:
        copy.wait()


def call(kernel, out_shape, name, scratch=(), spaces=None, vmem=40, cost=None, out_space=None):
    specs = {}
    if spaces:
        specs = dict(in_specs=[pl.BlockSpec(memory_space=space) for space in spaces])
    if out_space is not None:
        specs["out_specs"] = pl.BlockSpec(memory_space=out_space)
    return pl.pallas_call(
        kernel,
        out_shape=out_shape,
        scratch_shapes=list(scratch),
        compiler_params=pltpu.CompilerParams(vmem_limit_bytes=vmem * 1024 * 1024),
        name=name,
        cost_estimate=cost,
        **specs,
    )


def f32(*shape):
    return jax.ShapeDtypeStruct(shape, jnp.float32)


VEC = ("z_hi", "y")
SPACE = ("x", "z_lo", "core")
LINE = ("y", "core")
PLANE = ("z_hi", "z_lo", "x")


def body(perturbation, trajectory, step_order):
    tiles = lax.axis_size(SPACE)
    first, second = lax.axis_size(LINE), lax.axis_size(PLANE)
    sent = call(
        pack_kernel,
        jax.ShapeDtypeStruct((32, 8 * QUADS, 128), jnp.int32),
        "pack",
        [
            pltpu.VMEM((32, 8 * QUADS, 128), jnp.int32),
            pltpu.VMEM((6, ROWS, 512), jnp.float32),
            pltpu.VMEM((18, ROWS, 512), jnp.bfloat16),
            pltpu.VMEM((8 * PAIRS, 512), jnp.int32),
            pltpu.VMEM((2, 8 * (PAIRS - WHOLE), 512), jnp.int32),
            pltpu.SemaphoreType.DMA((2 + QUADS // 2,)),
        ],
        spaces=(pltpu.HBM, pltpu.HBM),
        out_space=pltpu.HBM,
        vmem=60,
    )(perturbation[0], trajectory[0].reshape(18, ROWS, 512))
    held = lax.all_to_all(sent, VEC, split_axis=0, concat_axis=0, tiled=True)
    side = jax.ShapeDtypeStruct((HALO_ROWS, 128), jnp.int32)
    state, base, far, near = call(
        unpack_kernel,
        (f32(6, ROWS, 8, 128), f32(36, ROWS, 128), side, side),
        "unpack",
        [pltpu.VMEM((HALO_ROWS, 128), jnp.int32)] * 2,
        spaces=(pltpu.SMEM, pltpu.VMEM),
    )(step_order, held.reshape(32 * 8 * QUADS, 128))
    far = lax.ppermute(far, SPACE, [(i, (i + 1 if i % 2 else i - 1) % tiles) for i in range(tiles)])
    near = lax.ppermute(near, SPACE, [(i, i ^ 1) for i in range(tiles)])
    coefs = pltpu.VMEM((2, COEF, 32, 128), jnp.float32)
    kept, middle = call(
        inner_kernel,
        (f32(6, 6, ROWS, 8, 128), f32(32, 768)),
        "inner",
        [pltpu.VMEM((2, COEF, ROWS, 128), jnp.float32)],
        cost=pl.CostEstimate(flops=20_000_000, bytes_accessed=8_000_000, transcendentals=0),
    )(state, base)
    cells, gram = call(
        outer_kernel,
        (jax.ShapeDtypeStruct((64, 2304), jnp.bfloat16), f32(first, 8, 128)),
        "outer",
        [
            pltpu.VMEM((32, 2304), jnp.float32),
            pltpu.VMEM((6, 6, ROWS, 8, 128), jnp.float32),
            coefs,
            pltpu.VMEM((2, HALO_ROWS, 128), jnp.int32),
            pltpu.VMEM((6, 2 * HALO, 8, 128), jnp.float32),
        ],
    )(state, base, far, near, kept, middle)
    gram = lax.all_to_all(gram, LINE, split_axis=0, concat_axis=0, tiled=True)
    gram = call(sum_kernel, f32(second, 8, 128), "sums")(gram)
    gram = lax.all_to_all(gram, PLANE, split_axis=0, concat_axis=0, tiled=True)
    entries = float(6 * ROWS * 512 * tiles)
    ortho, upper = call(
        lambda *refs: solve_kernel(entries, *refs), (jax.ShapeDtypeStruct((32, 1, 1280), jnp.int32), f32(32, 32)), "solve"
    )(gram, cells)
    ortho = lax.all_to_all(ortho, VEC, split_axis=0, concat_axis=0, tiled=True)
    placed = call(
        place_kernel,
        f32(6, ROWS, 512),
        "place",
        [pltpu.VMEM((6, ROWS, 512), jnp.float32), pltpu.SemaphoreType.DMA((6,))],
        spaces=(pltpu.VMEM,),
        out_space=pltpu.HBM,
    )(ortho)
    return placed[None], upper


def solution(mesh):
    fine = jax.sharding.Mesh(mesh.devices.reshape(4, 8, 4, 2, 2), VEC + SPACE)
    in_specs = (P(VEC, None, SPACE, None), P(VEC, None, None, SPACE, None), P())
    out_specs = (P(VEC, None, SPACE, None), P())
    return jax.shard_map(body, mesh=fine, in_specs=in_specs, out_specs=out_specs, check_vma=False)
```
